32 devices in a mesh: groups: 2 (over y), cell: 4 (over z), frame: 4 (over x, core).
Axes of the slice: x: 2, y: 2, z: 4, core: 2. Of those that a mesh axis runs over, the one named last changes fastest.
Arguments:
- frames: bfloat16 [32768, 1024], P(('groups', 'cell', 'frame')), parts along dimension 0, may hold values from -6 to 6
- labels: int32 [32768, 1], P(('groups', 'cell', 'frame')), parts along dimension 0, may hold values from 0 to 23, as said below
- centroids: bfloat16 [24, 256, 1024], P('cell'), may hold values from -0.6 to 0.6
- sharpness: float32 [24], P('cell'), may hold values from 0.5 to 2
Outputs:
- new_centroids: float32 [48, 256, 1024], P(('groups', 'cell'), 'frame'), parts along dimension 0
- child_mass: float32 [48, 256], P(('groups', 'cell'), 'frame'), parts along dimension 0
- frame_score: float32 [32768], P(('groups', 'cell', 'frame')), parts along dimension 0
The draws below stay inside these ranges and needn't reach their ends.
There are 2 independent parts, one for each index of `groups`. The reference program is written for one: setup_inputs(seed, part) draws one part's arguments, and reference() takes and returns one part's arrays. A program takes and returns all parts, laid end to end along the dimension named above; an argument that names none is the same for every part. Nothing has to cross between parts.
Inputs may be any that keep to these rules, and one draw needn't show every extreme that they name: Among the frames of one device (aligned blocks of 1024 rows) no label occurs more than 128 times, and the labels c with the same c // 6 occur at most 512 times together; in every such block some label occurs exactly 128 times and some group of labels with the same c // 6 exactly 512 times.
All inputs are finite; a program needn't handle non-finite values.
Results may differ from the reference program's by a relative error of at most 0.0026.
Values may be sent and summed in bfloat16 or wider, within the bound.
No kernel may reach another device: no remote copies, remote signals or barrier semaphores. Data moves between devices by JAX's collectives and lax.ppermute only.
A program may use at most 128 MiB of HBM per device.

```python
import math
import jax
import jax.numpy as jnp
from jax import lax

DIM = 1024
KIDS = 256
CELLS_PER_SHARD = 6
FR_DEV = 1024
CELLS = 24
CAP = 128
OWN = 512
FRAMES = 16384
N_CELL = 4
N_FRAME = 4


def draw_frames(key, part):
    key = jax.random.fold_in(key, 5)
    random_keys = jax.random.split(key, 1)
    values = jax.random.truncated_normal(random_keys[0], -6.0, 6.0, (FRAMES, DIM), jnp.float32)
    return values.astype(jnp.bfloat16)


def draw_centroids(key, part):
    key = jax.random.fold_in(key, 7)
    values = 0.1 * jax.random.truncated_normal(key, -6.0, 6.0, (CELLS, KIDS, DIM), jnp.float32)
    return values.astype(jnp.bfloat16)


def draw_labels(key, part):
    key = jax.random.fold_in(key, 11)
    holders = CELLS // CELLS_PER_SHARD
    blocks = FRAMES // FR_DEV
    busiest_holder = jax.random.randint(jax.random.fold_in(key, 1), (), 0, holders)
    heavy_cell = jax.random.randint(jax.random.fold_in(key, 2), (), 0, CELLS_PER_SHARD)
    entry_count = holders * OWN
    replicas = CELLS_PER_SHARD * CAP

    def one_block(block_key):
        random_keys = jax.random.split(block_key, 5)
        holder_ids = jnp.arange(holders, dtype=jnp.int32)
        holder_reward = jax.random.randint(random_keys[0], (holders,), 0, 4)
        holder_reward = jnp.where(holder_ids == busiest_holder, 4, holder_reward)
        entry_ids = jnp.arange(entry_count, dtype=jnp.int32)
        entry_holder = entry_ids // OWN
        entry_jitter = jax.random.randint(random_keys[1], (entry_count,), 0, 4096)
        entry_score = (holder_reward[entry_holder] * 4096 + entry_jitter) * entry_count + entry_ids
        item_order = jnp.argsort(-entry_score, stable=True).astype(jnp.int32)
        picked = item_order[:FR_DEV]
        taken_mask = jnp.zeros((entry_count,), jnp.int32).at[picked].set(1).reshape(holders, OWN)
        own_rank = (jnp.cumsum(taken_mask, axis=1) - 1).reshape(-1)
        local_ids = jnp.arange(CELLS_PER_SHARD, dtype=jnp.int32)
        cell_reward = jax.random.randint(random_keys[2], (holders, CELLS_PER_SHARD), 0, 4)
        compelled = (holder_ids[:, None] == busiest_holder) & (local_ids[None, :] == heavy_cell)
        cell_reward = jnp.where(compelled, 4, cell_reward)
        replica_ids = jnp.arange(replicas, dtype=jnp.int32)
        replica_local = replica_ids // CAP
        replica_jitter = jax.random.randint(random_keys[3], (holders, replicas), 0, 4096)
        replica_score = (cell_reward[:, replica_local] * 4096 + replica_jitter) * replicas + replica_ids[None, :]
        copy_order = jnp.argsort(-replica_score, axis=1, stable=True).astype(jnp.int32)
        local_list = copy_order // CAP
        picked_owner = entry_holder[picked]
        picked_rank = own_rank[picked]
        block_labels = picked_owner * CELLS_PER_SHARD + local_list[picked_owner, picked_rank]
        return jax.random.permutation(random_keys[4], block_labels)
    labels_all = jax.vmap(one_block)(jax.random.split(key, blocks))
    return labels_all.reshape(FRAMES, 1).astype(jnp.int32)


def shard_levels(key, extent, shards, smallest, high):
    level, own = 1.0, jax.random.fold_in(key, 6)
    for position, shards_of in shards:
        heights = jnp.exp(jax.random.uniform(jax.random.fold_in(own, position), (shards_of,), jnp.float32, smallest / len(shards), high / len(shards)))
        level = level * jnp.repeat(heights, extent[position] // shards_of).reshape([-1 if axis == position else 1 for axis in range(len(extent))])
    return level


def setup_inputs(seed: int = 0, part: int = 0) -> dict:
    key_list = jax.random.split(jax.random.key(seed), 5)
    own_keys = jax.random.split(jax.random.fold_in(key_list[4], part), 5)
    return {
        "frames": draw_frames(jax.random.fold_in(jax.random.fold_in(key_list[4], part), 71), part),
        "labels": draw_labels(jax.random.fold_in(jax.random.fold_in(key_list[4], part), 71), part),
        "centroids": draw_centroids(jax.random.fold_in(key_list[4], 71), part),
        "sharpness": jnp.clip(jnp.exp(math.log(2.0) - 1.3862944 * jax.random.uniform(key_list[3], (CELLS,), jnp.float32) ** shard_levels(key_list[3], (CELLS,), ((0, 4),), -0.2, 0.2)), 0.5, 2.0),
    }


prior_mass = 1.0


def reference(frames, labels, centroids, sharpness):
    frame_label = labels[:, 0].astype(jnp.int32)
    ordering = jnp.argsort(frame_label, stable=True).astype(jnp.int32)
    cell_ids = jnp.arange(CELLS, dtype=jnp.int32)
    cell_counts = jnp.sum((frame_label[:, None] == cell_ids[None, :]).astype(jnp.int32), axis=0).astype(jnp.int32)
    cell_starts = (jnp.cumsum(cell_counts) - cell_counts).astype(jnp.int32)
    longest = CAP * N_CELL * N_FRAME
    arranged = jnp.concatenate([frames[ordering], jnp.zeros((longest, DIM), jnp.bfloat16)], axis=0)
    order_padded = jnp.concatenate([ordering, jnp.full((longest,), FRAMES, jnp.int32)], axis=0)

    def per_cell(cell_id):
        chosen = lax.dynamic_slice_in_dim(arranged, cell_starts[cell_id], longest, 0)
        is_valid = jnp.arange(longest, dtype=jnp.int32) < cell_counts[cell_id]
        centre = centroids[cell_id]
        products = jnp.dot(chosen, centre.T, preferred_element_type=jnp.float32)
        centre_wide = centre.astype(jnp.float32)
        half_norm = 0.5 * jnp.sum(centre_wide * centre_wide, axis=1)
        scores_cell = sharpness[cell_id] * (products - half_norm[None, :])
        highest = jnp.max(scores_cell, axis=1, keepdims=True)
        exponent = jnp.exp(scores_cell - highest)
        totals = jnp.sum(exponent, axis=1, keepdims=True)
        log_total = highest[:, 0] + jnp.log(totals[:, 0])
        responsibility = jnp.where(is_valid[:, None], exponent / totals, 0.0)
        numerator = lax.dot_general(responsibility.astype(jnp.bfloat16), chosen, (((0,), (0,)), ((), ())), preferred_element_type=jnp.float32)
        mass_sum = jnp.sum(responsibility, axis=0)
        updated = (numerator + prior_mass * centre_wide) / (mass_sum[:, None] + prior_mass)
        return updated, mass_sum, log_total

    updated, mass_sum, log_total = lax.map(per_cell, cell_ids)
    positions = cell_starts[:, None] + jnp.arange(longest, dtype=jnp.int32)[None, :]
    in_cell = jnp.arange(longest, dtype=jnp.int32)[None, :] < cell_counts[:, None]
    target = jnp.where(in_cell, order_padded[positions], FRAMES).astype(jnp.int32)
    scores_out = jnp.zeros((FRAMES + 1,), jnp.float32).at[target.reshape(-1)].set(log_total.reshape(-1))[:FRAMES]
    return updated, mass_sum, scores_out
```

```python
import functools

import jax
import jax.numpy as jnp
from jax import lax
from jax.experimental import pallas as pl
from jax.experimental.pallas import tpu as pltpu
from jax.sharding import PartitionSpec as P

prior_mass = 1.0
cores = 2
wire = jnp.bfloat16
vmem_limit = 48 * 1024 * 1024


def _hot(flat_row, segment, own_slots):
    rows = flat_row.shape[1]
    slot = lax.broadcasted_iota(jnp.int32, (own_slots, rows), 0) + segment * own_slots
    return jnp.where(slot == flat_row, 1.0, 0.0).astype(jnp.bfloat16)


def _pick(flat_row, frames_ref, segment, out_ref):
    hot = _hot(flat_row, segment, out_ref.shape[0])
    out_ref[...] = jnp.dot(hot, frames_ref[...], preferred_element_type=jnp.float32).astype(
        jnp.bfloat16
    )


def _place_kernel(
    cells_local, window, own_slots, segments, rel_ref, frames_ref, flat_ref, off_ref, meta_ref, *outs
):
    rows = rel_ref.shape[1]
    cells = meta_ref.shape[0]
    rel = rel_ref[...]
    cell = lax.broadcasted_iota(jnp.int32, (cells, rows), 0)
    base = jnp.zeros_like(cell)
    segment = jnp.zeros_like(rel)
    for g in range(1, cells // cells_local):
        base += jnp.where(cell >= g * cells_local, cells_local, 0)
        segment += jnp.where(rel >= g * cells_local, 1, 0)
    hits = jnp.where(rel == cell, 1, 0)
    lane = lax.broadcasted_iota(jnp.int32, (cells, rows), 1)
    running = hits
    step = 1
    while step < rows:
        running += jnp.where(lane >= step, pltpu.roll(running, step, 1), 0)
        step *= 2
    count = jnp.sum(hits, axis=1, keepdims=True)
    start = jnp.sum(jnp.where((rel < cell) & (rel >= base), 1, 0), axis=1, keepdims=True)
    first = jnp.minimum((start >> 4) << 4, own_slots - window)
    position = jnp.sum(hits * (running + (start - 1)), axis=0, keepdims=True)
    flat = segment * own_slots + position
    flat_ref[...] = flat
    off_ref[...] = jnp.sum(hits * (running + (start - first - 1)), axis=0, keepdims=True)
    column = lax.broadcasted_iota(jnp.int32, meta_ref.shape, 1)
    meta_ref[...] = jnp.where(
        column == 0, first, jnp.where(column == 1, start - first, jnp.where(column == 2, count, 0))
    )
    for g, out_ref in zip(segments, outs, strict=True):
        _pick(flat, frames_ref, g, out_ref)


def _pick_kernel(segments, flat_ref, frames_ref, *outs):
    flat = flat_ref[...]
    for g, out_ref in zip(segments, outs, strict=True):
        _pick(flat, frames_ref, g, out_ref)


def _cell_kernel(sources, window, pieces, share, lanes, *refs):
    meta = refs[:sources]
    sharp_ref = refs[sources + 1]
    refs = refs[sources + 2 :]
    centre_refs, refs = refs[:pieces], refs[pieces:]
    row_refs, refs = refs[:sources], refs[sources:]
    keep_ref, mass_ref, score_ref = refs[:3]
    send_refs, (held, sems) = refs[3:-2], refs[-2:]
    copies = []
    for s in range(sources):
        first = pl.multiple_of(meta[s][lanes[s], 0], 16)
        copies.append(
            pltpu.make_async_copy(
                row_refs[s].at[pl.ds(first, window)],
                held.at[pl.ds(s * window, window)],
                sems.at[s],
            )
        )
    for copy in copies:
        copy.start()
    centre = jnp.concatenate([c[...].reshape(c.shape[-2:]) for c in centre_refs], axis=0)
    wide = centre.astype(jnp.float32)
    half_norm = 0.5 * jnp.sum(wide * wide, axis=1, keepdims=True)
    slot = lax.broadcasted_iota(jnp.int32, (1, sources * window), 1)
    valid = slot < 0
    for s in range(sources):
        begin = s * window + meta[s][lanes[s], 1]
        valid = valid | ((slot >= begin) & (slot < begin + meta[s][lanes[s], 2]))
    for copy in copies:
        copy.wait()
    chosen = held[...]
    products = lax.dot_general(
        centre, chosen, (((1,), (1,)), ((), ())), preferred_element_type=jnp.float32
    )
    scores = sharp_ref[0] * (products - half_norm)
    top = jnp.max(scores, axis=0, keepdims=True)
    exponent = jnp.exp(scores - top)
    total = jnp.sum(exponent, axis=0, keepdims=True)
    score_ref[...] = jnp.broadcast_to(
        jnp.where(valid, top + jnp.log(total), 0.0), score_ref.shape
    )
    resp = exponent * jnp.where(valid, 1.0 / total, 0.0)
    mass = jnp.sum(resp, axis=1, keepdims=True)
    mass_ref[...] = jnp.broadcast_to(mass, (mass.shape[0], 128)).T[: mass_ref.shape[0]]
    low = resp.astype(jnp.bfloat16)
    numer = jnp.dot(low, chosen, preferred_element_type=jnp.float32)
    keep_ref[...] = numer[:share]
    for n, ref in enumerate(send_refs):
        ref[...] = numer[(n + 1) * share : (n + 2) * share].astype(ref.dtype)


def _score_kernel(cells, window, rel_ref, off_ref, values_ref, out_ref):
    rows = rel_ref.shape[1]
    hot = jnp.where(
        lax.broadcasted_iota(jnp.int32, (window, rows), 0) == off_ref[...], 1.0, 0.0
    ).astype(jnp.bfloat16)
    rest = values_ref[...]
    mine = lax.broadcasted_iota(jnp.int32, (cells, rows), 0) == rel_ref[...]
    total = jnp.zeros((cells, rows), jnp.float32)
    for _ in range(3):
        term = rest.astype(jnp.bfloat16)
        rest = rest - term.astype(jnp.float32)
        total += jnp.dot(term, hot, preferred_element_type=jnp.float32)
    out_ref[...] = jnp.sum(jnp.where(mine, total, 0.0), axis=0, keepdims=True)


def _params():
    return pltpu.CompilerParams(vmem_limit_bytes=vmem_limit)


def _cell_call(meta, code, sharp, centre_in, row_blocks, window, lanes, kids, share, sends):
    sources = len(row_blocks)
    width = row_blocks[0].shape[1]
    pieces = len(centre_in)
    arrays, specs = zip(*centre_in, strict=True)
    whole = lambda shape: pl.BlockSpec(shape, lambda g, *_: (0,) * len(shape))
    out_shape = [
        jax.ShapeDtypeStruct((share, width), jnp.float32),
        jax.ShapeDtypeStruct((8, kids), jnp.float32),
        jax.ShapeDtypeStruct((8, sources * window), jnp.float32),
    ] + [jax.ShapeDtypeStruct((share, width), wire)] * sends
    rows = sources * window
    return pl.pallas_call(
        functools.partial(_cell_kernel, sources, window, pieces, share, lanes),
        grid_spec=pltpu.PrefetchScalarGridSpec(
            num_scalar_prefetch=sources + 2,
            grid=(1,),
            in_specs=list(specs) + [pl.BlockSpec(memory_space=pl.ANY)] * sources,
            out_specs=[whole(o.shape) for o in out_shape],
            scratch_shapes=[
                pltpu.VMEM((rows, width), jnp.bfloat16),
                pltpu.SemaphoreType.DMA((sources,)),
            ],
        ),
        out_shape=out_shape,
        compiler_params=_params(),
        cost_estimate=pl.CostEstimate(
            flops=4 * kids * rows * width,
            bytes_accessed=2 * (kids + rows) * width + 6 * kids * width,
            transcendentals=kids * rows,
        ),
    )(*meta, code, sharp, *arrays, *row_blocks)


def on_device(frames, labels, centroids, sharpness):
    cell_count = lax.axis_size("cell")
    frame_count = lax.axis_size("frame")
    group_count = lax.axis_size("groups")
    cells_local, kids, width = centroids.shape
    rows = frames.shape[0]
    cells_total = cells_local * cell_count
    half = cell_count // 2
    chips = frame_count // cores
    per_core = cells_local // cores
    cell_cap = 3 * rows // cells_total
    own_slots = 2 * rows // cell_count
    sources = half * cores
    window = -(-(cell_cap + 16) // 16) * 16
    while sources * window % 128:
        window += 16
    window = min(window, own_slots)
    share = kids // chips
    piece = share // group_count

    z = lax.axis_index("cell")
    j = lax.axis_index("frame")
    y = lax.axis_index("groups")
    x, k = j // cores, j % cores
    p, h = z % half, z // half

    def at(zz, xx, kk):
        return zz * frame_count + xx * cores + kk

    def hop_core(v):
        return lax.ppermute(v, "frame", [(i, i ^ 1) for i in range(frame_count)])

    def hop_chip(v, s):
        return lax.ppermute(
            v,
            "frame",
            [(a * cores + c, (a + s) % chips * cores + c) for a in range(chips) for c in range(cores)],
        )

    def hop_member(v, s):
        return lax.ppermute(
            v, "cell", [(b * half + i, b * half + (i + s) % half) for b in range(2) for i in range(half)]
        )

    def hop_partner(v):
        return lax.ppermute(v, "cell", [(i, (i + half) % cell_count) for i in range(cell_count)])

    def hop_group(v):
        return lax.ppermute(v, "groups", [(i, (i + 1) % group_count) for i in range(group_count)])

    def hop_any(v, s, kk):
        pairs = [
            (at(b * half + i, a, c), at(b * half + (i + s) % half, a, c ^ kk))
            for b in range(2)
            for i in range(half)
            for a in range(chips)
            for c in range(cores)
        ]
        return lax.ppermute(v, ("cell", "frame"), pairs)

    foreign_sharp = hop_partner(sharpness)
    foreign_pieces = []
    for i in range(per_core):
        mine = lax.dynamic_slice(
            centroids, (k * per_core + i, (x * group_count + y) * piece, 0), (1, piece, width)
        )
        first = hop_partner(mine[0])
        found = {(0, 0): first}
        for s in range(1, chips):
            found[s, 0] = hop_chip(first, -s)
        for g in range(1, group_count):
            for s in range(chips):
                found[s, g] = hop_group(found[s, g - 1])
        foreign_pieces.append([found[s, g] for s in range(chips) for g in range(group_count)])

    label = labels.reshape(1, rows)
    owner, local = label // cells_local, label % cells_local
    member = (owner % half - p + half) % half
    foreign = (owner // half != h).astype(jnp.int32)
    other = (local // per_core) ^ k
    rel = ((member * 2 + foreign) * 2 + other) * per_core + local % per_core

    seg = lambda s, t: s * 2 + t
    first_segs = [seg(s, 1) for s in range(1, half)]
    next_segs = [seg(s, 0) for s in range(1, half)]
    last_segs = [seg(0, 1), seg(0, 0)]
    block = jax.ShapeDtypeStruct((own_slots, width), jnp.bfloat16)
    pick_cost = lambda n: pl.CostEstimate(
        flops=2 * n * own_slots * rows * width,
        bytes_accessed=2 * width * (rows + n * own_slots),
        transcendentals=0,
    )
    flat, off, meta, *blocks = pl.pallas_call(
        functools.partial(_place_kernel, cells_local, window, own_slots, first_segs),
        out_shape=[
            jax.ShapeDtypeStruct((1, rows), jnp.int32),
            jax.ShapeDtypeStruct((1, rows), jnp.int32),
            jax.ShapeDtypeStruct((cells_total, 128), jnp.int32),
        ]
        + [block] * len(first_segs),
        compiler_params=_params(),
        cost_estimate=pick_cost(len(first_segs)),
    )(rel, frames)
    segments = dict(zip(first_segs, blocks, strict=True))
    for group in (last_segs, next_segs):
        blocks = pl.pallas_call(
            functools.partial(_pick_kernel, group),
            out_shape=[block] * len(group),
            compiler_params=_params(),
            cost_estimate=pick_cost(len(group)),
        )(flat, frames)
        segments.update(zip(group, blocks, strict=True))

    metas = []
    for s in range(half):
        part = meta[seg(s, 0) * cells_local : (seg(s, 1) + 1) * cells_local]
        for kk in range(cores):
            metas.append(part if s == kk == 0 else hop_any(part, s, kk))
    held = {}
    for t in (1, 0):
        held[t] = []
        for s in range(half):
            mine = segments[seg(s, t)]
            if s:
                mine = hop_member(mine, s)
            held[t] += [mine, hop_core(mine)]

    code = jnp.stack([x, y, k]).astype(jnp.int32)
    results = {}
    for t in (1, 0):
        for i in range(per_core):
            lanes = [t * cells_local + (n % cores) * per_core + i for n in range(sources)]
            sharp = lax.dynamic_slice(
                foreign_sharp if t else sharpness, (k * per_core + i,), (1,)
            )
            centre_in = []
            for s in range(chips):
                for g in range(group_count):
                    if t:
                        spec = pl.BlockSpec((piece, width), lambda n, *_: (0, 0))
                        centre_in.append((foreign_pieces[i][s * group_count + g], spec))
                    else:

                        def where_from(n, *scalars, s=s, g=g, i=i):
                            c = scalars[sources]
                            chip = lax.rem(c[0] + s, chips)
                            return c[2] * per_core + i, chip * group_count + lax.rem(c[1] + g, group_count), 0

                        centre_in.append((centroids, pl.BlockSpec((1, piece, width), where_from)))
            results[t, i] = _cell_call(
                metas, code, sharp, centre_in, held[t], window, lanes, kids, share, chips - 1
            )

    def over_chips(t, i):
        keep, _, _, *sends = results[t, i]
        for s in range(1, chips):
            keep = keep + hop_chip(sends[s - 1], s).astype(jnp.float32)
        return keep

    numer = []
    for i in range(per_core):
        numer.append(hop_partner(over_chips(1, i).astype(wire)))
    for i in range(per_core):
        numer[i] = over_chips(0, i) + numer[i].astype(jnp.float32)

    order = [(t, i) for t in (1, 0) for i in range(per_core)]
    mass_all = jnp.stack([results[o][1][0] for o in order])
    mass_sum = mass_all[:, :share]
    for s in range(1, chips):
        mass_sum = mass_sum + hop_chip(mass_all[:, s * share : (s + 1) * share], s)
    mass = mass_sum[per_core:] + hop_partner(mass_sum[:per_core])

    score_all = jnp.stack([results[o][2][0] for o in order])
    back = {}
    for s in range(half):
        for kk in range(cores):
            n = s * cores + kk
            part = score_all[:, n * window : (n + 1) * window]
            back[s, kk] = part if n == 0 else hop_any(part, -s, kk)
    values = []
    for s in range(half):
        for t in range(2):
            for kk in range(cores):
                at_row = 0 if t else per_core
                values.append(back[s, kk][at_row : at_row + per_core])
    frame_score = pl.pallas_call(
        functools.partial(_score_kernel, cells_total, window),
        out_shape=jax.ShapeDtypeStruct((1, rows), jnp.float32),
        compiler_params=_params(),
        cost_estimate=pl.CostEstimate(
            flops=6 * cells_total * window * rows, bytes_accessed=4 * cells_total * window, transcendentals=0
        ),
    )(rel, off, jnp.concatenate(values, axis=0)).reshape(rows)

    updated = []
    for i in range(per_core):
        previous = jnp.concatenate(
            [
                lax.dynamic_slice(
                    centroids,
                    (k * per_core + i, (x * group_count + (y + g) % group_count) * piece, 0),
                    (1, piece, width),
                )
                for g in range(group_count)
            ],
            axis=1,
        )[0].astype(jnp.float32)
        updated.append(
            (numer[i] + prior_mass * previous) / (mass[i][:, None] + prior_mass)
        )
    updated = jnp.stack(updated)
    mine_at = ((k - y) % group_count) * piece
    theirs_at = ((1 - k - y) % group_count) * piece

    def swap(v):
        mine = lax.dynamic_slice_in_dim(v, mine_at, piece, 1)
        theirs = hop_core(lax.dynamic_slice_in_dim(v, theirs_at, piece, 1))
        return jnp.where(
            k == 0, jnp.concatenate([mine, theirs], 0), jnp.concatenate([theirs, mine], 0)
        )

    return swap(updated), swap(mass), frame_score


def solution(mesh):
    return jax.shard_map(
        on_device,
        mesh=mesh,
        in_specs=(
            P(("groups", "cell", "frame"), None),
            P(("groups", "cell", "frame"), None),
            P("cell", None, None),
            P("cell"),
        ),
        out_specs=(
            P(("groups", "cell"), "frame", None),
            P(("groups", "cell"), "frame"),
            P(("groups", "cell", "frame")),
        ),
        check_vma=False,
    )
```

```python
import functools

import jax
import jax.numpy as jnp
from jax import lax
from jax.experimental import pallas as pl
from jax.experimental.pallas import tpu as pltpu
from jax.sharding import PartitionSpec as P

prior_mass = 1.0
cores = 2
wire = jnp.bfloat16
vmem_limit = 16 * 1024 * 1024
anywhere = pl.BlockSpec(memory_space=pl.ANY)
cheap = pl.CostEstimate(flops=1, bytes_accessed=1, transcendentals=0)
dear = pl.CostEstimate(flops=20_000_000_000, bytes_accessed=1, transcendentals=0)
meta_extra = 16


def _hot(flat_row, segment, own_slots):
    rows = flat_row.shape[1]
    slot = lax.broadcasted_iota(jnp.int32, (own_slots, rows), 0) + segment * own_slots
    return jnp.where(slot == flat_row, 1.0, 0.0).astype(jnp.bfloat16)


def _pick(flat_row, meta, frames_ref, segment, out_ref):
    own_slots = out_ref.shape[0] - meta_extra
    hot = _hot(flat_row, segment, own_slots)
    out_ref[pl.ds(0, own_slots)] = jnp.dot(
        hot, frames_ref[...], preferred_element_type=jnp.float32
    ).astype(jnp.bfloat16)
    out_ref[pl.ds(own_slots, meta_extra)] = jnp.zeros((meta_extra, out_ref.shape[1]), jnp.bfloat16)
    out_ref[pl.ds(own_slots, meta_extra), pl.ds(0, 128)] = meta[
        segment * meta_extra : (segment + 1) * meta_extra
    ].astype(jnp.bfloat16)


def _place_kernel(
    cells_local, window, own_slots, segments, rel_ref, frames_ref, flat_ref, off_ref, meta_ref, *outs
):
    rows = rel_ref.shape[1]
    lines = meta_ref.shape[0]
    rel = rel_ref[...]
    line = lax.broadcasted_iota(jnp.int32, (lines, rows), 0)
    base = (line // meta_extra) * meta_extra
    segment = rel // meta_extra
    hits = jnp.where(rel == line, 1, 0)
    lane = lax.broadcasted_iota(jnp.int32, (lines, rows), 1)
    running = hits
    step = 1
    while step < rows:
        running += jnp.where(lane >= step, pltpu.roll(running, step, 1), 0)
        step *= 2
    count = jnp.sum(hits, axis=1, keepdims=True)
    start = jnp.sum(jnp.where((rel < line) & (rel >= base), 1, 0), axis=1, keepdims=True)
    first = jnp.minimum((start >> 4) << 4, own_slots - window)
    position = jnp.sum(hits * (running + (start - 1)), axis=0, keepdims=True)
    flat = segment * own_slots + position
    flat_ref[...] = flat
    off_ref[...] = jnp.sum(hits * (running + (start - first - 1)), axis=0, keepdims=True)
    column = lax.broadcasted_iota(jnp.int32, meta_ref.shape, 1)
    meta = jnp.where(
        column == 0,
        first >> 4,
        jnp.where(column == 1, start - first, jnp.where(column == 2, count, 0)),
    ).astype(jnp.float32)
    meta_ref[...] = meta
    for g, out_ref in zip(segments, outs, strict=True):
        _pick(flat, meta, frames_ref, g, out_ref)


def _pick_kernel(segments, separate, flat_ref, meta_ref, frames_ref, *outs):
    flat, meta = flat_ref[...], meta_ref[...]
    size = outs[0].shape[0] // (1 if separate else len(segments))
    for n, g in enumerate(segments):
        target = outs[n] if separate else outs[0].at[pl.ds(n * size, size)]
        _pick(flat, meta, frames_ref, g, target)


def _split(lines, rows):
    high = lines.astype(jnp.bfloat16).astype(jnp.float32)
    middle = (lines - high).astype(jnp.bfloat16).astype(jnp.float32)
    rest = jnp.zeros((rows - 3 * lines.shape[0], lines.shape[1]), jnp.float32)
    return jnp.concatenate([high, middle, lines - high - middle, rest], axis=0)


def _round(value):
    return lax.reduce_precision(value, 8, 7)


def _note_kernel(score_ref, out_ref):
    out_ref[...] = score_ref[:, 0]


def _prior_kernel(group_count, code_ref, *refs):
    for g in range(group_count):
        size = refs[g].shape[1]
        refs[-1][:, g * size : (g + 1) * size] = refs[g][...].astype(jnp.float32)


def _cell_kernel(sources, window, pieces, share, steps, per_core, begin, span, bases, earlier, tail, *refs):
    code_ref, sharp_ref = refs[:2]
    refs = refs[2:]
    centre_refs, refs = refs[:pieces], refs[pieces:]
    row_refs, refs = refs[:sources], refs[sources:]
    earlier_refs, refs = refs[:earlier], refs[earlier:]
    keep_ref, mass_ref, score_ref = refs[:3]
    send_refs, (held, sems, meta_low, meta_wide, meta_ref, meta_sems) = refs[3:-6], refs[-6:]
    step = pl.program_id(0)

    def entry(n, at_step, field):
        return meta_ref[n * meta_extra + (n % cores) * per_core + begin + at_step, field]

    def copies(at_step, half):
        found = []
        for n in range(sources):
            first = entry(n, at_step, 0) * 16 + bases[n]
            found.append(
                pltpu.make_async_copy(
                    row_refs[n].at[pl.ds(pl.multiple_of(first, 16), window)],
                    held.at[half, pl.ds(n * window, window)],
                    sems.at[half, n],
                )
            )
        return found

    now = lax.rem(step, 2)

    @pl.when(step == 0)
    def _():
        lines = [
            pltpu.make_async_copy(
                row_refs[n].at[pl.ds(bases[n] + span - meta_extra, meta_extra), pl.ds(0, 128)],
                meta_low.at[pl.ds(n * meta_extra, meta_extra)],
                meta_sems.at[n],
            )
            for n in range(sources)
        ]
        for copy in lines:
            copy.start()
        for copy in lines:
            copy.wait()
        meta_wide[...] = meta_low[...].astype(jnp.float32).astype(jnp.int32)
        to_scalars = pltpu.make_async_copy(meta_wide, meta_ref, meta_sems.at[sources])
        to_scalars.start()
        to_scalars.wait()
        for copy in copies(0, 0):
            copy.start()

    if steps > 1:

        @pl.when(step + 1 < steps)
        def _():
            for copy in copies(step + 1, 1 - now):
                copy.start()

    centre = jnp.concatenate([c[0] for c in centre_refs], axis=0)
    wide = centre.astype(jnp.float32)
    half_norm = 0.5 * jnp.sum(wide * wide, axis=1, keepdims=True)
    slot = lax.broadcasted_iota(jnp.int32, (1, sources * window), 1)
    valid = slot < 0
    for n in range(sources):
        low = n * window + entry(n, step, 1)
        valid = valid | ((slot >= low) & (slot < low + entry(n, step, 2)))
    for copy in copies(step, now):
        copy.wait()
    chosen = held[now]
    products = lax.dot_general(
        centre, chosen, (((1,), (1,)), ((), ())), preferred_element_type=jnp.float32
    )
    scores = sharp_ref[code_ref[2] * per_core + begin + step] * (products - half_norm)
    top = jnp.max(scores, axis=0, keepdims=True)
    exponent = jnp.exp(scores - top)
    total = jnp.sum(exponent, axis=0, keepdims=True)
    score_ref[0] = jnp.broadcast_to(
        jnp.where(valid, top + jnp.log(total), 0.0), score_ref.shape[1:]
    )
    resp = exponent * jnp.where(valid, 1.0 / total, 0.0)
    mass = jnp.sum(resp, axis=1, keepdims=True)
    mass_ref[step] = jnp.broadcast_to(mass, (mass.shape[0], 128)).T[: mass_ref.shape[1]]
    low = resp.astype(jnp.bfloat16)
    numer = jnp.dot(low, chosen, preferred_element_type=jnp.float32)
    keep_ref[0] = numer[:share]
    for n, ref in enumerate(send_refs):
        at_row = pl.multiple_of(step * share, share)
        ref[pl.ds(at_row, share)] = numer[(n + 1) * share : (n + 2) * share].astype(ref.dtype)

    if tail:

        @pl.when(step == steps - 1)
        def _():
            lines = [r[i, :1] for r in (*earlier_refs, mass_ref) for i in range(r.shape[0])]
            for n, ref in enumerate(send_refs):
                part = [v[:, (n + 1) * share : (n + 2) * share] for v in lines]
                rows = _split(jnp.concatenate(part, axis=0), tail)
                ref[pl.ds(steps * share, tail)] = jnp.zeros((tail, ref.shape[1]), ref.dtype)
                ref[pl.ds(steps * share, tail), pl.ds(0, share)] = rows.astype(ref.dtype)


def _pack_kernel(sources, window, *refs):
    line = 0
    for score_ref in refs[:-sources]:
        size = score_ref.shape[0]
        for n, out_ref in enumerate(refs[-sources:]):
            out_ref[line : line + size] = score_ref[:, n * window : (n + 1) * window]
        line += size


def _score_kernel(cells, window, rel_ref, off_ref, values_ref, out_ref):
    rows = rel_ref.shape[1]
    hot = jnp.where(
        lax.broadcasted_iota(jnp.int32, (window, rows), 0) == off_ref[...], 1.0, 0.0
    ).astype(jnp.bfloat16)
    rest = values_ref[...]
    mine = lax.broadcasted_iota(jnp.int32, (cells, rows), 0) == rel_ref[...]
    total = jnp.zeros((cells, rows), jnp.float32)
    for _ in range(3):
        term = rest.astype(jnp.bfloat16)
        rest = rest - term.astype(jnp.float32)
        total += jnp.dot(term, hot, preferred_element_type=jnp.float32)
    out_ref[...] = jnp.sum(jnp.where(mine, total, 0.0), axis=0, keepdims=True)


def _after(value, *others):
    return lax.optimization_barrier((value, *others))[0]


def _params():
    return pltpu.CompilerParams(vmem_limit_bytes=vmem_limit)


def _cell_call(code, sharp, centre_in, row_blocks, window, per_core, begin, steps, kids, share, sends, earlier, tail):
    sources = len(row_blocks)
    row_arrays, bases = zip(*row_blocks, strict=True)
    width = row_arrays[0].shape[1]
    arrays, specs = zip(*centre_in, strict=True)
    span = row_arrays[0].shape[0] // 2
    rows = sources * window
    out_shape = [
        jax.ShapeDtypeStruct((steps, share, width), jnp.float32),
        jax.ShapeDtypeStruct((steps, 8, kids), jnp.float32),
        jax.ShapeDtypeStruct((steps, 8, rows), jnp.float32),
    ] + [jax.ShapeDtypeStruct((steps * share + tail, width), wire)] * sends
    fixed = lambda shape: pl.BlockSpec(shape, lambda n, *_: (0,) * len(shape))
    moving = lambda shape: pl.BlockSpec((1, *shape[1:]), lambda n, *_: (n, 0, 0))
    return pl.pallas_call(
        functools.partial(
            _cell_kernel, sources, window, len(arrays), share, steps, per_core, begin, span, bases, len(earlier), tail
        ),
        grid_spec=pltpu.PrefetchScalarGridSpec(
            num_scalar_prefetch=2,
            grid=(steps,),
            in_specs=list(specs) + [anywhere] * sources + [fixed(v.shape) for v in earlier],
            out_specs=[
                (moving if n in (0, 2) else fixed)(o.shape) for n, o in enumerate(out_shape)
            ],
            scratch_shapes=[
                pltpu.VMEM((min(steps, 2), rows, width), jnp.bfloat16),
                pltpu.SemaphoreType.DMA((min(steps, 2), sources)),
                pltpu.VMEM((sources * meta_extra, 128), jnp.bfloat16),
                pltpu.VMEM((sources * meta_extra, 128), jnp.int32),
                pltpu.SMEM((sources * meta_extra, 128), jnp.int32),
                pltpu.SemaphoreType.DMA((sources + 1,)),
            ],
        ),
        out_shape=out_shape,
        compiler_params=_params(),
        cost_estimate=cheap,
    )(code, sharp, *arrays, *row_arrays, *earlier)


def on_device(frames, labels, centroids, sharpness):
    cell_count = lax.axis_size("cell")
    frame_count = lax.axis_size("frame")
    group_count = 2
    cells_local, kids, width = centroids.shape
    rows = frames.shape[0]
    cells_total = cells_local * cell_count
    half = cell_count // 2
    chips = frame_count // cores
    per_core = cells_local // cores
    cell_cap = 3 * rows // cells_total
    own_slots = 2 * rows // cell_count
    sources = half * cores
    window = -(-(cell_cap + 16) // 16) * 16
    while sources * window % 128:
        window += 16
    window = min(window, own_slots)
    share = kids // chips
    piece = share // group_count

    z = lax.axis_index("cell")
    j = lax.axis_index("frame")
    y = lax.axis_index("groups")
    x, k = j // cores, j % cores
    p, h = z % half, z // half

    def at(zz, xx, kk):
        return zz * frame_count + xx * cores + kk

    def hop_core(v):
        return lax.ppermute(v, "frame", [(i, i ^ 1) for i in range(frame_count)])

    def hop_chip(v, s):
        return lax.ppermute(
            v,
            "frame",
            [(a * cores + c, (a + s) % chips * cores + c) for a in range(chips) for c in range(cores)],
        )

    def hop_member(v, s):
        return lax.ppermute(
            v, "cell", [(b * half + i, b * half + (i + s) % half) for b in range(2) for i in range(half)]
        )

    def hop_partner(v):
        return lax.ppermute(v, "cell", [(i, (i + half) % cell_count) for i in range(cell_count)])

    def hop_group(v):
        return lax.ppermute(v, "groups", [(i, 1 - i) for i in range(2)])

    def hop_any(v, s, kk):
        pairs = [
            (at(b * half + i, a, c), at(b * half + (i + s) % half, a, c ^ kk))
            for b in range(2)
            for i in range(half)
            for a in range(chips)
            for c in range(cores)
        ]
        return lax.ppermute(v, ("cell", "frame"), pairs)

    parts = [(0, 1), (1, per_core - 1)]
    foreign_sharp = hop_partner(sharpness)
    first = hop_partner(
        lax.dynamic_slice(
            centroids,
            (k * per_core, (x * group_count + y) * piece, 0),
            (per_core, piece, width),
        )
    )
    by_chip = [first] + [hop_chip(first, -s) for s in range(1, chips)]
    foreign_pieces = [v for c in by_chip for v in (c, hop_group(c))]
    around = by_chip[1:] + foreign_pieces[1:2]

    label = labels.reshape(1, rows)
    owner, local = label // cells_local, label % cells_local
    member = (owner % half - p + half) % half
    foreign = (owner // half != h).astype(jnp.int32)
    other = (local // per_core) ^ k
    rel = (member * 2 + foreign) * meta_extra + other * per_core + local % per_core

    seg = lambda s, t: s * 2 + t
    first_segs = [seg(s, 1) for s in range(1, half)]
    next_segs = [seg(s, 0) for s in range(1, half)]
    last_segs = [seg(0, 1), seg(0, 0)]
    span = own_slots + meta_extra
    block = jax.ShapeDtypeStruct((span, width), jnp.bfloat16)
    lines = cell_count * meta_extra
    flat, off, meta, *blocks = pl.pallas_call(
        functools.partial(_place_kernel, cells_local, window, own_slots, first_segs),
        out_shape=[
            jax.ShapeDtypeStruct((1, rows), jnp.int32),
            jax.ShapeDtypeStruct((1, rows), jnp.int32),
            jax.ShapeDtypeStruct((lines, 128), jnp.float32),
        ]
        + [block] * len(first_segs),
        compiler_params=_params(),
        cost_estimate=dear,
    )(rel, frames)
    segments = dict(zip(first_segs, blocks, strict=True))

    blocks = pl.pallas_call(
        functools.partial(_pick_kernel, next_segs, len(next_segs)),
        out_shape=[block] * len(next_segs),
        compiler_params=_params(),
        cost_estimate=dear,
    )(_after(flat, first), meta, frames)
    segments.update(zip(next_segs, blocks, strict=True))
    here = pl.pallas_call(
        functools.partial(_pick_kernel, last_segs, 0),
        out_shape=[jax.ShapeDtypeStruct((2 * span, width), jnp.bfloat16)],
        compiler_params=_params(),
        cost_estimate=dear,
    )(_after(flat, *blocks, foreign_sharp, *around), meta, frames)[0]

    here_other = hop_core(here)
    received = {t: [hop_member(segments[seg(s, t)], s) for s in range(1, half)] for t in (1, 0)}

    def held_of(t, *gate):
        base = 0 if t else span
        held = [(here, base), (here_other, base)]
        for v in received[t]:
            v = _after(v, *gate)
            held += [(v, 0), (hop_core(v), 0)]
        return held

    held = {1: held_of(1, *around)}

    code = jnp.stack([x, y, k]).astype(jnp.int32)
    tail = -(-3 * per_core // 16) * 16

    def masses_in(rows):
        rows = rows[:, :share].astype(jnp.float32)
        return sum(rows[n * per_core : (n + 1) * per_core] for n in range(3))

    def over_chips(result, steps, earlier, extra):
        keep, mass, _, *sends = result
        mass = jnp.concatenate([*earlier, mass])[:, 0, :share]
        for s in range(1, chips):
            got = hop_chip(sends[s - 1], s)
            keep = keep + got[: steps * share].reshape(keep.shape).astype(jnp.float32)
            if extra:
                mass = mass + masses_in(got[steps * share :])
        return keep, mass

    results, totals, masses, theirs, notes = [], [], [], [], []
    for t, begin, size in [(1, *part) for part in parts] + [(0, 0, per_core)]:
        code_here = _after(code, notes[-1] if t else totals[1]) if results else code
        if not t:
            held[0] = held_of(0, totals[0])
        centre_in = []
        for s in range(chips):
            for g in range(group_count):
                if t:
                    spec = pl.BlockSpec((1, piece, width), lambda n, *_, o=begin: (o + n, 0, 0))
                    centre_in.append((foreign_pieces[s * group_count + g], spec))
                else:

                    def where_from(n, c, sharp_ref, s=s, g=g, o=begin):
                        chip = lax.rem(c[0] + s, chips)
                        return c[2] * per_core + o + n, chip * group_count + lax.rem(c[1] + g, group_count), 0

                    centre_in.append((centroids, pl.BlockSpec((1, piece, width), where_from)))
        earlier = [r[1] for r in results] if t else []
        extra = 0 if t and begin + size < per_core else tail
        results.append(
            _cell_call(
                code_here, foreign_sharp if t else sharpness, centre_in, held[t], window, per_core,
                begin, size, kids, share, chips - 1, earlier if extra else [], extra,
            )
        )
        if t:
            scores = results[-1][2]
            if totals:
                scores = _after(scores, totals[0])
            notes.append(
                pl.pallas_call(
                    _note_kernel,
                    out_shape=jax.ShapeDtypeStruct((size, sources * window), jnp.float32),
                    compiler_params=_params(),
                    cost_estimate=dear,
                )(scores)
            )
        else:
            results[-1] = [*results[-1][:3], *(_after(v, theirs[0]) for v in results[-1][3:])]
        total, mass = over_chips(results[-1], size, earlier, extra)
        if t and extra:
            total = _after(total, notes[-1])
        masses.append(mass)
        if t:
            total = total.astype(wire).reshape(size * share, width)
            if extra:
                high = _round(mass)
                middle = _round(mass - high)
                terms = jnp.concatenate([high, middle, mass - high - middle])
                behind = jnp.pad(
                    terms.astype(wire), ((0, tail - terms.shape[0]), (0, width - share))
                )
                total = jnp.concatenate([total, behind])
            theirs.append(hop_partner(total))
        totals.append(total)
    theirs = [_after(v, totals[-1]) for v in theirs]
    got = jnp.concatenate([v[: size * share] for v, (_, size) in zip(theirs, parts, strict=True)])
    numer = totals[-1] + got.reshape(totals[-1].shape).astype(jnp.float32)
    mass = masses[-1] + masses_in(theirs[-1][-tail:])

    score_parts = pl.pallas_call(
        functools.partial(_pack_kernel, sources, window),
        out_shape=[jax.ShapeDtypeStruct((2 * per_core, window), jnp.float32)] * sources,
        compiler_params=_params(),
        cost_estimate=dear,
    )(*notes, results[-1][2][:, 0])

    back = {}
    for s in range(half):
        for kk in range(cores):
            n = s * cores + kk
            back[s, kk] = score_parts[n] if n == 0 else hop_any(score_parts[n], -s, kk)
    values = []
    for s in range(half):
        for t in range(2):
            at_row = 0 if t else per_core
            for kk in range(cores):
                values.append(back[s, kk][at_row : at_row + per_core])
            values.append(jnp.zeros((meta_extra - cells_local, window), jnp.float32))
    frame_score = pl.pallas_call(
        functools.partial(_score_kernel, lines, window),
        out_shape=jax.ShapeDtypeStruct((1, rows), jnp.float32),
        compiler_params=_params(),
        cost_estimate=dear,
    )(rel, off, jnp.concatenate(values, axis=0)).reshape(rows)

    def prior_from(n, c, g=0):
        return c[2], c[0] * group_count + lax.rem(c[1] + g, group_count), 0

    previous = pl.pallas_call(
        functools.partial(_prior_kernel, group_count),
        grid_spec=pltpu.PrefetchScalarGridSpec(
            num_scalar_prefetch=1,
            grid=(1,),
            in_specs=[
                pl.BlockSpec((per_core, piece, width), functools.partial(prior_from, g=g))
                for g in range(group_count)
            ],
            out_specs=pl.BlockSpec((per_core, share, width), lambda n, c: (0, 0, 0)),
        ),
        out_shape=jax.ShapeDtypeStruct((per_core, share, width), jnp.float32),
        compiler_params=_params(),
        cost_estimate=dear,
    )(code, *([centroids] * group_count))
    updated = (numer + prior_mass * previous) / (mass[:, :, None] + prior_mass)
    mine_at = ((k - y) % group_count) * piece
    theirs_at = ((1 - k - y) % group_count) * piece

    def both(at_kid):
        lines = jnp.pad(
            lax.dynamic_slice_in_dim(mass, at_kid, piece, 1), ((0, 0), (0, width - piece))
        )
        return lax.dynamic_slice_in_dim(updated, at_kid, piece, 1), lines

    mine, mass_mine = both(mine_at)
    theirs, mass_theirs = both(theirs_at)
    swapped = hop_core(
        jnp.concatenate([theirs, jnp.broadcast_to(mass_theirs[:, None], (per_core, 8, width))], 1)
    )

    def ordered(a, b):
        return jnp.where(k == 0, jnp.concatenate([a, b], 0), jnp.concatenate([b, a], 0))

    return (
        ordered(mine, swapped[:, :piece]),
        ordered(mass_mine[:, :piece], swapped[:, piece, :piece]),
        frame_score,
    )


def solution(mesh):
    return jax.shard_map(
        on_device,
        mesh=mesh,
        in_specs=(
            P(("groups", "cell", "frame"), None),
            P(("groups", "cell", "frame"), None),
            P("cell", None, None),
            P("cell"),
        ),
        out_specs=(
            P(("groups", "cell"), "frame", None),
            P(("groups", "cell"), "frame"),
            P(("groups", "cell", "frame")),
        ),
        check_vma=False,
    )
```

```python
import functools

import jax
import jax.numpy as jnp
from jax import lax
from jax.experimental import pallas as pl
from jax.experimental.pallas import tpu as pltpu
from jax.sharding import PartitionSpec as P

prior_mass = 1.0
cores = 2
wire = jnp.bfloat16
vmem_limit = 16 * 1024 * 1024
anywhere = pl.BlockSpec(memory_space=pl.ANY)
cheap = pl.CostEstimate(flops=1, bytes_accessed=1, transcendentals=0)
busy = pl.CostEstimate(flops=20_000_000_000, bytes_accessed=1, transcendentals=0)
dear = pl.CostEstimate(flops=20_000_000_000, bytes_accessed=1_000_000_000, transcendentals=0)
meta_extra = 16


def _hot(flat_row, segment, own_slots):
    rows = flat_row.shape[1]
    slot = lax.broadcasted_iota(jnp.int32, (own_slots, rows), 0) + segment * own_slots
    return jnp.where(slot == flat_row, 1.0, 0.0).astype(jnp.bfloat16)


def _pick(flat_row, meta, frames_ref, segment, out_ref):
    own_slots = out_ref.shape[0] - meta_extra
    hot = _hot(flat_row, segment, own_slots)
    out_ref[pl.ds(0, own_slots)] = jnp.dot(
        hot, frames_ref[...], preferred_element_type=jnp.float32
    ).astype(jnp.bfloat16)
    out_ref[pl.ds(own_slots, meta_extra)] = jnp.zeros((meta_extra, out_ref.shape[1]), jnp.bfloat16)
    out_ref[pl.ds(own_slots, meta_extra), pl.ds(0, 128)] = meta[
        segment * meta_extra : (segment + 1) * meta_extra
    ].astype(jnp.bfloat16)


def _place_kernel(
    per_core, reach, window, own_slots, segments, rel_ref, frames_ref, flat_ref, off_ref, meta_ref, *outs
):
    rows = rel_ref.shape[1]
    lines = meta_ref.shape[0]
    rel = rel_ref[...]
    line = lax.broadcasted_iota(jnp.int32, (lines, rows), 0)
    base = (line // meta_extra) * meta_extra
    segment = rel // meta_extra
    hits = jnp.where(rel == line, 1, 0)
    lane = lax.broadcasted_iota(jnp.int32, (lines, rows), 1)
    running = hits
    step = 1
    while step < rows:
        running += jnp.where(lane >= step, pltpu.roll(running, step, 1), 0)
        step *= 2
    count = jnp.sum(hits, axis=1, keepdims=True)
    ahead = jnp.sum(jnp.where((rel < line) & (rel >= base), 1, 0), axis=1, keepdims=True)
    behind = jnp.sum(
        jnp.where((rel >= line) & (rel < base + meta_extra), 1, 0), axis=1, keepdims=True
    )
    back = (line - base)[:, :1] >= per_core
    start = jnp.where(back, own_slots - behind, ahead)
    floor = jnp.where(back, own_slots - reach, 0)
    first = jnp.minimum(((start - floor) >> 4) << 4, reach - window) + floor
    position = jnp.sum(hits * (running + (start - 1)), axis=0, keepdims=True)
    flat = segment * own_slots + position
    flat_ref[...] = flat
    off_ref[...] = jnp.sum(hits * (running + (start - first - 1)), axis=0, keepdims=True)
    column = lax.broadcasted_iota(jnp.int32, meta_ref.shape, 1)
    meta = jnp.where(
        column == 0,
        (first - floor) >> 4,
        jnp.where(column == 1, start - first, jnp.where(column == 2, count, 0)),
    ).astype(jnp.float32)
    meta_ref[...] = meta
    for g, out_ref in zip(segments, outs, strict=True):
        _pick(flat, meta, frames_ref, g, out_ref)


def _pick_kernel(segments, separate, flat_ref, meta_ref, frames_ref, *outs):
    flat, meta = flat_ref[...], meta_ref[...]
    size = outs[0].shape[0] // (1 if separate else len(segments))
    for n, g in enumerate(segments):
        target = outs[n] if separate else outs[0].at[pl.ds(n * size, size)]
        _pick(flat, meta, frames_ref, g, target)


def _split(lines, rows):
    high = lines.astype(jnp.bfloat16).astype(jnp.float32)
    middle = (lines - high).astype(jnp.bfloat16).astype(jnp.float32)
    rest = jnp.zeros((rows - 3 * lines.shape[0], lines.shape[1]), jnp.float32)
    return jnp.concatenate([high, middle, lines - high - middle, rest], axis=0)


def _round(value):
    return lax.reduce_precision(value, 8, 7)


def _note_kernel(score_ref, out_ref):
    out_ref[...] = score_ref[:, 0]


def _copy_kernel(in_ref, out_ref):
    out_ref[...] = in_ref[...]


def _prior_kernel(group_count, code_ref, *refs):
    for g in range(group_count):
        size = refs[g].shape[1]
        refs[-1][:, g * size : (g + 1) * size] = refs[g][...].astype(jnp.float32)


def _cell_kernel(sources, window, reach, pieces, near, share, steps, per_core, begin, span, bases, earlier, tail, *refs):
    code_ref, sharp_ref = refs[:2]
    refs = refs[2:]
    centre_refs, refs = (refs[:1], refs[1:]) if near else (refs[:pieces], refs[pieces:])
    piece = share // 2
    row_refs, refs = refs[:sources], refs[sources:]
    earlier_refs, refs = refs[:earlier], refs[earlier:]
    keep_ref, mass_ref, score_ref = refs[:3]
    send_refs, (held, centres, sems, meta_low, meta_wide, meta_ref, meta_sems) = refs[3:-7], refs[-7:]
    step = pl.program_id(0)
    cell = (code_ref[2] * per_core if near else 0) + begin
    loads = []
    for n in range(sources):
        low = bases[n] + (0 if n % cores == 0 else span - meta_extra - reach)
        loads.append(
            pltpu.make_async_copy(
                row_refs[n].at[pl.ds(low, reach)],
                held.at[n, pl.ds(0, reach)],
                sems.at[n],
            )
        )
    for n in range(pieces):
        s, g = n // 2, n % 2
        if near:
            chip = lax.rem(code_ref[0] + s, pieces // 2)
            kid = (chip * 2 + lax.rem(code_ref[1] + g, 2)) * piece
            source = centre_refs[0].at[pl.ds(cell, steps), pl.ds(pl.multiple_of(kid, piece), piece)]
        else:
            source = centre_refs[n].at[pl.ds(begin, steps)]
        loads.append(
            pltpu.make_async_copy(source, centres.at[:, pl.ds(n * piece, piece)], sems.at[sources + n])
        )

    @pl.when(step == 0)
    def _():
        lines = [
            pltpu.make_async_copy(
                row_refs[n].at[pl.ds(bases[n] + span - meta_extra, meta_extra), pl.ds(0, 128)],
                meta_low.at[pl.ds(n * meta_extra, meta_extra)],
                meta_sems.at[n],
            )
            for n in range(sources)
        ]
        for copy in lines + loads:
            copy.start()
        for copy in lines:
            copy.wait()
        meta_wide[...] = meta_low[...].astype(jnp.float32).astype(jnp.int32)
        to_scalars = pltpu.make_async_copy(meta_wide, meta_ref, meta_sems.at[sources])
        to_scalars.start()
        to_scalars.wait()
        for copy in loads:
            copy.wait()

    def entry(n, field):
        return meta_ref[n * meta_extra + (n % cores) * per_core + begin + step, field]

    centre = centres[step]
    wide = centre.astype(jnp.float32)
    half_norm = 0.5 * jnp.sum(wide * wide, axis=1, keepdims=True)
    slot = lax.broadcasted_iota(jnp.int32, (1, sources * window), 1)
    valid = slot < 0
    for n in range(sources):
        low = n * window + entry(n, 1)
        valid = valid | ((slot >= low) & (slot < low + entry(n, 2)))
    chosen = jnp.concatenate(
        [held[n, pl.ds(pl.multiple_of(entry(n, 0) * 16, 16), window)] for n in range(sources)]
    )
    products = lax.dot_general(
        centre, chosen, (((1,), (1,)), ((), ())), preferred_element_type=jnp.float32
    )
    scores = sharp_ref[code_ref[2] * per_core + begin + step] * (products - half_norm)
    top = jnp.max(scores, axis=0, keepdims=True)
    exponent = jnp.exp(scores - top)
    total = jnp.sum(exponent, axis=0, keepdims=True)
    score_ref[0] = jnp.broadcast_to(
        jnp.where(valid, top + jnp.log(total), 0.0), score_ref.shape[1:]
    )
    resp = exponent * jnp.where(valid, 1.0 / total, 0.0)
    mass = jnp.sum(resp, axis=1, keepdims=True)
    mass_ref[step] = jnp.broadcast_to(mass, (mass.shape[0], 128)).T[: mass_ref.shape[1]]
    low = resp.astype(jnp.bfloat16)
    numer = jnp.dot(low, chosen, preferred_element_type=jnp.float32)
    keep_ref[0] = numer[:share]
    for n, ref in enumerate(send_refs):
        at_row = pl.multiple_of(step * share, share)
        ref[pl.ds(at_row, share)] = numer[(n + 1) * share : (n + 2) * share].astype(ref.dtype)

    if tail:

        @pl.when(step == steps - 1)
        def _():
            lines = [r[i, :1] for r in (*earlier_refs, mass_ref) for i in range(r.shape[0])]
            for n, ref in enumerate(send_refs):
                part = [v[:, (n + 1) * share : (n + 2) * share] for v in lines]
                rows = _split(jnp.concatenate(part, axis=0), tail)
                ref[pl.ds(steps * share, tail)] = jnp.zeros((tail, ref.shape[1]), ref.dtype)
                ref[pl.ds(steps * share, tail), pl.ds(0, share)] = rows.astype(ref.dtype)


def _pack_kernel(sources, window, *refs):
    line = 0
    for score_ref in refs[:-sources]:
        size = score_ref.shape[0]
        for n, out_ref in enumerate(refs[-sources:]):
            out_ref[line : line + size] = score_ref[:, n * window : (n + 1) * window]
        line += size


def _score_kernel(cells, window, rel_ref, off_ref, values_ref, out_ref):
    rows = rel_ref.shape[1]
    hot = jnp.where(
        lax.broadcasted_iota(jnp.int32, (window, rows), 0) == off_ref[...], 1.0, 0.0
    ).astype(jnp.bfloat16)
    rest = values_ref[...]
    mine = lax.broadcasted_iota(jnp.int32, (cells, rows), 0) == rel_ref[...]
    total = jnp.zeros((cells, rows), jnp.float32)
    for _ in range(3):
        term = rest.astype(jnp.bfloat16)
        rest = rest - term.astype(jnp.float32)
        total += jnp.dot(term, hot, preferred_element_type=jnp.float32)
    out_ref[...] = jnp.sum(jnp.where(mine, total, 0.0), axis=0, keepdims=True)


def _after(value, *others):
    return lax.optimization_barrier((value, *others))[0]


def _update_kernel(per_core, chips, piece, tail, code_ref, keep_ref, mass_ref, *refs):
    got_refs, refs = refs[: 2 * (chips - 1)], refs[2 * (chips - 1) :]
    first_ref, others_ref, tail_ref, prior_ref, out_ref, swap_ref, lines_ref, weight = refs
    step = pl.program_id(0)
    lines = mass_ref[:, 0, :128]
    for ref in [*got_refs[1::2], tail_ref]:
        rows = ref[...].astype(jnp.float32)
        for n in range(3):
            lines = lines + rows[n * per_core : (n + 1) * per_core]
    line = lax.broadcasted_iota(jnp.int32, lines.shape, 0)
    mine = jnp.sum(jnp.where(line == step, lines, 0.0), axis=0, keepdims=True)
    weight[...] = jnp.broadcast_to(1.0 / (mine + prior_mass), (128, 128)).T

    @pl.when(step == 0)
    def _():
        lines_ref[...] = jnp.concatenate(
            [lines, jnp.zeros((lines_ref.shape[0] - per_core, 128), jnp.float32)], axis=0
        )

    def updated(at_kid):
        rows = pl.ds(pl.multiple_of(at_kid, piece), piece)
        numer = keep_ref[0, rows] + prior_mass * prior_ref[0, rows]
        for ref in got_refs[0::2]:
            numer = numer + ref[rows].astype(jnp.float32)
        far = jnp.where(step == 0, first_ref[rows], others_ref[rows])
        return (numer + far.astype(jnp.float32)) * weight[rows, :1]

    here = lax.rem(code_ref[2] + code_ref[1], 2) * piece
    out_ref[0] = updated(here)
    swap_ref[0, :piece] = updated(piece - here)
    swap_ref[0, piece:] = jnp.zeros((8, swap_ref.shape[2]), jnp.float32)
    swap_ref[0, piece:, :128] = jnp.broadcast_to(mine, (8, 128))


def _finish_kernel(per_core, piece, code_ref, _, swap_ref, lines_ref, out_ref, mass_ref, sem):
    other = 1 - code_ref[2]
    copy = pltpu.make_async_copy(
        swap_ref.at[:, pl.ds(0, piece)], out_ref.at[pl.ds(other * per_core, per_core)], sem
    )
    copy.start()
    mine = lines_ref[:per_core]
    theirs = swap_ref[:, piece, :128]
    lines = jnp.where(
        other == 1, jnp.concatenate([mine, theirs], axis=0), jnp.concatenate([theirs, mine], axis=0)
    )
    here = lax.rem(code_ref[2] + code_ref[1], 2)
    mass_ref[...] = jnp.where(here == 0, lines[:, :piece], lines[:, piece : 2 * piece])
    copy.wait()


def _params():
    return pltpu.CompilerParams(vmem_limit_bytes=vmem_limit)


def _cell_call(code, sharp, arrays, near, row_blocks, window, reach, per_core, begin, steps, kids, share, sends, earlier, tail):
    sources = len(row_blocks)
    row_arrays, bases = zip(*row_blocks, strict=True)
    width = row_arrays[0].shape[1]
    pieces = kids // (share // 2)
    span = row_arrays[0].shape[0] // 2
    rows = sources * window
    out_shape = [
        jax.ShapeDtypeStruct((steps, share, width), jnp.float32),
        jax.ShapeDtypeStruct((steps, 8, kids), jnp.float32),
        jax.ShapeDtypeStruct((steps, 8, rows), jnp.float32),
    ] + [jax.ShapeDtypeStruct((steps * share + tail, width), wire)] * sends
    fixed = lambda shape: pl.BlockSpec(shape, lambda n, *_: (0,) * len(shape))
    moving = lambda shape: pl.BlockSpec((1, *shape[1:]), lambda n, *_: (n, 0, 0))
    return pl.pallas_call(
        functools.partial(
            _cell_kernel, sources, window, reach, pieces, near, share, steps, per_core, begin, span, bases, len(earlier), tail
        ),
        grid_spec=pltpu.PrefetchScalarGridSpec(
            num_scalar_prefetch=2,
            grid=(steps,),
            in_specs=[anywhere] * (len(arrays) + sources) + [fixed(v.shape) for v in earlier],
            out_specs=[
                (moving if n in (0, 2) else fixed)(o.shape) for n, o in enumerate(out_shape)
            ],
            scratch_shapes=[
                pltpu.VMEM((sources, reach, width), jnp.bfloat16),
                pltpu.VMEM((steps, kids, width), jnp.bfloat16),
                pltpu.SemaphoreType.DMA((sources + pieces,)),
                pltpu.VMEM((sources * meta_extra, 128), jnp.bfloat16),
                pltpu.VMEM((sources * meta_extra, 128), jnp.int32),
                pltpu.SMEM((sources * meta_extra, 128), jnp.int32),
                pltpu.SemaphoreType.DMA((sources + 1,)),
            ],
        ),
        out_shape=out_shape,
        compiler_params=pltpu.CompilerParams(vmem_limit_bytes=44 * 1024 * 1024),
        cost_estimate=busy,
    )(code, sharp, *arrays, *row_arrays, *earlier)


def on_device(frames, labels, centroids, sharpness):
    cell_count = lax.axis_size("cell")
    frame_count = lax.axis_size("frame")
    group_count = 2
    cells_local, kids, width = centroids.shape
    rows = frames.shape[0]
    cells_total = cells_local * cell_count
    half = cell_count // 2
    chips = frame_count // cores
    per_core = cells_local // cores
    cell_cap = 3 * rows // cells_total
    own_slots = 2 * rows // cell_count
    sources = half * cores
    window = -(-(cell_cap + 16) // 16) * 16
    while sources * window % 128:
        window += 16
    reach = min(own_slots, -(-per_core * cell_cap // 16) * 16)
    window = min(window, reach)
    share = kids // chips
    piece = share // group_count

    z = lax.axis_index("cell")
    j = lax.axis_index("frame")
    y = lax.axis_index("groups")
    x, k = j // cores, j % cores
    p, h = z % half, z // half

    def at(zz, xx, kk):
        return zz * frame_count + xx * cores + kk

    def hop_core(v):
        return lax.ppermute(v, "frame", [(i, i ^ 1) for i in range(frame_count)])

    def hop_chip(v, s):
        return lax.ppermute(
            v,
            "frame",
            [(a * cores + c, (a + s) % chips * cores + c) for a in range(chips) for c in range(cores)],
        )

    def hop_member(v, s):
        return lax.ppermute(
            v, "cell", [(b * half + i, b * half + (i + s) % half) for b in range(2) for i in range(half)]
        )

    def hop_partner(v):
        return lax.ppermute(v, "cell", [(i, (i + half) % cell_count) for i in range(cell_count)])

    def hop_group(v):
        return lax.ppermute(v, "groups", [(i, 1 - i) for i in range(2)])

    def hop_any(v, s, kk):
        pairs = [
            (at(b * half + i, a, c), at(b * half + (i + s) % half, a, c ^ kk))
            for b in range(2)
            for i in range(half)
            for a in range(chips)
            for c in range(cores)
        ]
        return lax.ppermute(v, ("cell", "frame"), pairs)

    parts = [(0, 1), (1, per_core - 1)]
    foreign_sharp = hop_partner(sharpness)
    first = hop_partner(
        lax.dynamic_slice(
            centroids,
            (k * per_core, (x * group_count + y) * piece, 0),
            (per_core, piece, width),
        )
    )
    by_chip = [first] + [hop_chip(first, -s) for s in range(1, chips)]
    foreign_pieces = [v for c in by_chip for v in (c, hop_group(c))]
    around = by_chip[1:] + foreign_pieces[1:2]

    label = labels.reshape(1, rows)
    owner, local = label // cells_local, label % cells_local
    member = (owner % half - p + half) % half
    foreign = (owner // half != h).astype(jnp.int32)
    other = (local // per_core) ^ k
    rel = (member * 2 + foreign) * meta_extra + other * per_core + local % per_core

    seg = lambda s, t: s * 2 + t
    first_segs = [seg(s, 1) for s in range(1, half)]
    next_segs = [seg(s, 0) for s in range(1, half)]
    last_segs = [seg(0, 1), seg(0, 0)]
    span = own_slots + meta_extra
    block = jax.ShapeDtypeStruct((span, width), jnp.bfloat16)
    lines = cell_count * meta_extra
    flat, off, meta, *blocks = pl.pallas_call(
        functools.partial(_place_kernel, per_core, reach, window, own_slots, first_segs),
        out_shape=[
            jax.ShapeDtypeStruct((1, rows), jnp.int32),
            jax.ShapeDtypeStruct((1, rows), jnp.int32),
            jax.ShapeDtypeStruct((lines, 128), jnp.float32),
        ]
        + [block] * len(first_segs),
        compiler_params=_params(),
        cost_estimate=dear,
    )(rel, frames)
    segments = dict(zip(first_segs, blocks, strict=True))

    blocks = pl.pallas_call(
        functools.partial(_pick_kernel, next_segs, len(next_segs)),
        out_shape=[block] * len(next_segs),
        compiler_params=_params(),
        cost_estimate=dear,
    )(_after(flat, first), meta, frames)
    segments.update(zip(next_segs, blocks, strict=True))
    here = pl.pallas_call(
        functools.partial(_pick_kernel, last_segs, 0),
        out_shape=[jax.ShapeDtypeStruct((2 * span, width), jnp.bfloat16)],
        compiler_params=_params(),
        cost_estimate=dear,
    )(_after(flat, *blocks, foreign_sharp, *around), meta, frames)[0]

    here_other = hop_core(here)
    received = {t: [hop_member(segments[seg(s, t)], s) for s in range(1, half)] for t in (1, 0)}

    def held_of(t, *gate):
        base = 0 if t else span
        held = [(here, base), (here_other, base)]
        for v in received[t]:
            v = _after(v, *gate)
            held += [(v, 0), (hop_core(v), 0)]
        return held

    held = {1: held_of(1, *around)}

    code = jnp.stack([x, y, k]).astype(jnp.int32)
    tail = -(-3 * per_core // 16) * 16

    def masses_in(rows):
        rows = rows[:, :share].astype(jnp.float32)
        return sum(rows[n * per_core : (n + 1) * per_core] for n in range(3))

    def over_chips(result, steps, earlier, extra):
        keep, mass, _, *sends = result
        mass = jnp.concatenate([*earlier, mass])[:, 0, :share]
        for s in range(1, chips):
            got = hop_chip(sends[s - 1], s)
            keep = keep + got[: steps * share].reshape(keep.shape).astype(jnp.float32)
            if extra:
                mass = mass + masses_in(got[steps * share :])
        return keep, mass

    results, totals, theirs, notes = [], [], [], []
    for t, begin, size in [(1, *part) for part in parts] + [(0, 0, per_core)]:
        if not t:
            held[0] = held_of(0, totals[1])
            notes.append(
                pl.pallas_call(
                    _copy_kernel,
                    out_shape=jax.ShapeDtypeStruct(notes[-1].shape, jnp.float32),
                    compiler_params=_params(),
                    cost_estimate=dear,
                )(_after(notes.pop(), totals[1]))
            )
        code_here = _after(code, notes[-1]) if results else code
        earlier = [r[1] for r in results] if t else []
        extra = 0 if t and begin + size < per_core else tail
        results.append(
            _cell_call(
                code_here, foreign_sharp if t else sharpness, foreign_pieces if t else [centroids],
                not t, held[t], window, reach, per_core,
                begin, size, kids, share, chips - 1, earlier if extra else [], extra,
            )
        )
        if t:
            scores = results[-1][2]
            if totals:
                scores = _after(scores, totals[0])
            notes.append(
                pl.pallas_call(
                    _note_kernel,
                    out_shape=jax.ShapeDtypeStruct((size, sources * window), jnp.float32),
                    compiler_params=_params(),
                    cost_estimate=dear,
                )(scores)
            )
        if not t:
            arrived = [hop_chip(results[-1][3 + n], n + 1) for n in range(chips - 1)]
            break
        total, mass = over_chips(results[-1], size, earlier, extra)
        if t and extra:
            total = _after(total, notes[-1])
        total = total.astype(wire).reshape(size * share, width)
        if extra:
            high = _round(mass)
            middle = _round(mass - high)
            terms = jnp.concatenate([high, middle, mass - high - middle])
            behind = jnp.pad(terms.astype(wire), ((0, tail - terms.shape[0]), (0, width - share)))
            total = jnp.concatenate([total, behind])
        theirs.append(hop_partner(total))
        totals.append(total)
    score_parts = pl.pallas_call(
        functools.partial(_pack_kernel, sources, window),
        out_shape=[jax.ShapeDtypeStruct((2 * per_core, window), jnp.float32)] * sources,
        compiler_params=_params(),
        cost_estimate=dear,
    )(*notes, results[-1][2][:, 0])

    back = {}
    for s in range(half):
        for kk in range(cores):
            n = s * cores + kk
            back[s, kk] = score_parts[n] if n == 0 else hop_any(score_parts[n], -s, kk)
    values = []
    for s in range(half):
        for t in range(2):
            at_row = 0 if t else per_core
            for kk in range(cores):
                values.append(back[s, kk][at_row : at_row + per_core])
            values.append(jnp.zeros((meta_extra - cells_local, window), jnp.float32))
    frame_score = pl.pallas_call(
        functools.partial(_score_kernel, lines, window),
        out_shape=jax.ShapeDtypeStruct((1, rows), jnp.float32),
        compiler_params=_params(),
        cost_estimate=cheap,
    )(rel, off, jnp.concatenate(values, axis=0)).reshape(rows)

    def prior_from(n, c, g=0):
        return c[2], c[0] * group_count + lax.rem(c[1] + g, group_count), 0

    previous = pl.pallas_call(
        functools.partial(_prior_kernel, group_count),
        grid_spec=pltpu.PrefetchScalarGridSpec(
            num_scalar_prefetch=1,
            grid=(1,),
            in_specs=[
                pl.BlockSpec((per_core, piece, width), functools.partial(prior_from, g=g))
                for g in range(group_count)
            ],
            out_specs=pl.BlockSpec((per_core, share, width), lambda n, c: (0, 0, 0)),
        ),
        out_shape=jax.ShapeDtypeStruct((per_core, share, width), jnp.float32),
        compiler_params=_params(),
        cost_estimate=dear,
    )(code, *([centroids] * group_count))
    theirs = [_after(v, *arrived) for v in theirs]
    one_cell = lambda block, where: pl.BlockSpec(block, where)
    whole = lambda v: pl.BlockSpec(v.shape, lambda n, c: (0,) * v.ndim)
    behind = lambda steps: pl.BlockSpec((tail, 128), lambda n, c: (steps * share // tail, 0))
    keep, mass = results[-1][:2]
    got, got_specs = [], []
    for v in arrived:
        got += [v, v]
        got_specs += [one_cell((share, width), lambda n, c: (n, 0)), behind(per_core)]
    out, swap, lines_mine = pl.pallas_call(
        functools.partial(_update_kernel, per_core, chips, piece, tail),
        grid_spec=pltpu.PrefetchScalarGridSpec(
            num_scalar_prefetch=1,
            grid=(per_core,),
            in_specs=[
                one_cell((1, share, width), lambda n, c: (n, 0, 0)),
                whole(mass),
                *got_specs,
                one_cell((share, width), lambda n, c: (0, 0)),
                one_cell((share, width), lambda n, c: (jnp.maximum(n - 1, 0), 0)),
                behind(per_core - 1),
                one_cell((1, share, width), lambda n, c: (n, 0, 0)),
            ],
            out_specs=[
                one_cell((1, piece, width), lambda n, c: (c[2] * per_core + n, 0, 0)),
                one_cell((1, piece + 8, width), lambda n, c: (n, 0, 0)),
                pl.BlockSpec((8, 128), lambda n, c: (0, 0)),
            ],
            scratch_shapes=[pltpu.VMEM((128, 128), jnp.float32)],
        ),
        out_shape=[
            jax.ShapeDtypeStruct((cells_local, piece, width), jnp.float32),
            jax.ShapeDtypeStruct((per_core, piece + 8, width), jnp.float32),
            jax.ShapeDtypeStruct((8, 128), jnp.float32),
        ],
        compiler_params=_params(),
        cost_estimate=dear,
    )(code, keep, mass, *got, theirs[0], theirs[1], theirs[1], previous)
    new_centroids, child_mass = pl.pallas_call(
        functools.partial(_finish_kernel, per_core, piece),
        in_specs=[pl.BlockSpec(memory_space=pltpu.SMEM), anywhere]
        + [pl.BlockSpec(memory_space=pltpu.VMEM)] * 2,
        out_specs=[anywhere, pl.BlockSpec(memory_space=pltpu.VMEM)],
        out_shape=[
            jax.ShapeDtypeStruct(out.shape, jnp.float32),
            jax.ShapeDtypeStruct((cells_local, piece), jnp.float32),
        ],
        scratch_shapes=[pltpu.SemaphoreType.DMA(())],
        input_output_aliases={1: 0},
        compiler_params=_params(),
        cost_estimate=dear,
    )(code, out, hop_core(swap), lines_mine)
    return new_centroids, child_mass, frame_score


def solution(mesh):
    return jax.shard_map(
        on_device,
        mesh=mesh,
        in_specs=(
            P(("groups", "cell", "frame"), None),
            P(("groups", "cell", "frame"), None),
            P("cell", None, None),
            P("cell"),
        ),
        out_specs=(
            P(("groups", "cell"), "frame", None),
            P(("groups", "cell"), "frame"),
            P(("groups", "cell", "frame")),
        ),
        check_vma=False,
    )
```

```python
import functools

import jax
import jax.numpy as jnp
from jax import lax
from jax.experimental import pallas as pl
from jax.experimental.pallas import tpu as pltpu
from jax.sharding import PartitionSpec as P

prior_mass = 1.0
cores = 2
wire = jnp.bfloat16
vmem_limit = 16 * 1024 * 1024
anywhere = pl.BlockSpec(memory_space=pl.ANY)
cheap = pl.CostEstimate(flops=1, bytes_accessed=1, transcendentals=0)
busy = pl.CostEstimate(flops=20_000_000_000, bytes_accessed=1, transcendentals=0)
dear = pl.CostEstimate(flops=20_000_000_000, bytes_accessed=1_000_000_000, transcendentals=0)
meta_extra = 16


def _hot(flat_row, segment, own_slots):
    rows = flat_row.shape[1]
    slot = lax.broadcasted_iota(jnp.int32, (own_slots, rows), 0) + segment * own_slots
    return jnp.where(slot == flat_row, 1.0, 0.0).astype(jnp.bfloat16)


def _pick(flat_row, meta, frames_ref, segment, out_ref):
    own_slots = out_ref.shape[0] - meta_extra
    hot = _hot(flat_row, segment, own_slots)
    out_ref[pl.ds(0, own_slots)] = jnp.dot(
        hot, frames_ref[...], preferred_element_type=jnp.float32
    ).astype(jnp.bfloat16)
    out_ref[pl.ds(own_slots, meta_extra)] = jnp.zeros((meta_extra, out_ref.shape[1]), jnp.bfloat16)
    out_ref[pl.ds(own_slots, meta_extra), pl.ds(0, 128)] = meta[
        segment * meta_extra : (segment + 1) * meta_extra
    ].astype(jnp.bfloat16)


def _place_kernel(
    per_core, reach, window, own_slots, segments, rel_ref, frames_ref, flat_ref, off_ref, meta_ref, *outs
):
    rows = rel_ref.shape[1]
    lines = meta_ref.shape[0]
    rel = rel_ref[...]
    line = lax.broadcasted_iota(jnp.int32, (lines, rows), 0)
    base = (line // meta_extra) * meta_extra
    segment = rel // meta_extra
    hits = jnp.where(rel == line, 1, 0)
    lane = lax.broadcasted_iota(jnp.int32, (lines, rows), 1)
    running = hits
    step = 1
    while step < rows:
        running += jnp.where(lane >= step, pltpu.roll(running, step, 1), 0)
        step *= 2
    count = jnp.sum(hits, axis=1, keepdims=True)
    ahead = jnp.sum(jnp.where((rel < line) & (rel >= base), 1, 0), axis=1, keepdims=True)
    behind = jnp.sum(
        jnp.where((rel >= line) & (rel < base + meta_extra), 1, 0), axis=1, keepdims=True
    )
    back = (line - base)[:, :1] >= per_core
    start = jnp.where(back, own_slots - behind, ahead)
    floor = jnp.where(back, own_slots - reach, 0)
    first = jnp.minimum(((start - floor) >> 4) << 4, reach - window) + floor
    position = jnp.sum(hits * (running + (start - 1)), axis=0, keepdims=True)
    flat = segment * own_slots + position
    flat_ref[...] = flat
    off_ref[...] = jnp.sum(hits * (running + (start - first - 1)), axis=0, keepdims=True)
    column = lax.broadcasted_iota(jnp.int32, meta_ref.shape, 1)
    meta = jnp.where(
        column == 0,
        (first - floor) >> 4,
        jnp.where(column == 1, start - first, jnp.where(column == 2, count, 0)),
    ).astype(jnp.float32)
    meta_ref[...] = meta
    for g, out_ref in zip(segments, outs, strict=True):
        _pick(flat, meta, frames_ref, g, out_ref)


def _pick_kernel(segments, flat_ref, meta_ref, frames_ref, *outs):
    flat, meta = flat_ref[...], meta_ref[...]
    for g, out_ref in zip(segments, outs, strict=True):
        _pick(flat, meta, frames_ref, g, out_ref)


def _split(lines, rows):
    high = lines.astype(jnp.bfloat16).astype(jnp.float32)
    middle = (lines - high).astype(jnp.bfloat16).astype(jnp.float32)
    rest = jnp.zeros((rows - 3 * lines.shape[0], lines.shape[1]), jnp.float32)
    return jnp.concatenate([high, middle, lines - high - middle, rest], axis=0)


def _round(value):
    return lax.reduce_precision(value, 8, 7)


def _note_kernel(score_ref, out_ref):
    out_ref[...] = score_ref[:, 0]


def _copy_kernel(in_ref, out_ref):
    out_ref[...] = in_ref[...]


def _split(lines, rows):
    high = lines.astype(jnp.bfloat16).astype(jnp.float32)
    middle = (lines - high).astype(jnp.bfloat16).astype(jnp.float32)
    rest = jnp.zeros((rows - 3 * lines.shape[0], lines.shape[1]), jnp.float32)
    return jnp.concatenate([high, middle, lines - high - middle, rest], axis=0)


def _round(value):
    return lax.reduce_precision(value, 8, 7)


def _note_kernel(score_ref, out_ref):
    out_ref[...] = score_ref[:, 0]


def _copy_kernel(in_ref, out_ref):
    out_ref[...] = in_ref[...]


def _prior_kernel(group_count, code_ref, *refs):
    for g in range(group_count):
        size = refs[g].shape[1]
        refs[-1][:, g * size : (g + 1) * size] = refs[g][...].astype(jnp.float32)


def _cell_kernel(sources, window, reach, pieces, near, share, steps, per_core, begin, span, earlier, tail, *refs):
    code_ref, sharp_ref = refs[:2]
    refs = refs[2:]
    centre_refs, refs = (refs[:1], refs[1:]) if near else (refs[:pieces], refs[pieces:])
    piece = share // 2
    row_refs, refs = refs[:sources], refs[sources:]
    earlier_refs, refs = refs[:earlier], refs[earlier:]
    keep_ref, mass_ref, score_ref = refs[:3]
    send_refs, (held, centres, sems, meta_low, meta_wide, meta_ref, meta_sems) = refs[3:-7], refs[-7:]
    step = pl.program_id(0)
    cell = (code_ref[2] * per_core if near else 0) + begin
    loads = []
    for n in range(sources):
        low = 0 if n % cores == 0 else span - meta_extra - reach
        loads.append(
            pltpu.make_async_copy(
                row_refs[n].at[pl.ds(low, reach)],
                held.at[n, pl.ds(0, reach)],
                sems.at[n],
            )
        )
    for n in range(pieces):
        s, g = n // 2, n % 2
        if near:
            chip = lax.rem(code_ref[0] + s, pieces // 2)
            kid = (chip * 2 + lax.rem(code_ref[1] + g, 2)) * piece
            source = centre_refs[0].at[pl.ds(cell, steps), pl.ds(pl.multiple_of(kid, piece), piece)]
        else:
            source = centre_refs[n].at[pl.ds(begin, steps)]
        loads.append(
            pltpu.make_async_copy(source, centres.at[:, pl.ds(n * piece, piece)], sems.at[sources + n])
        )

    @pl.when(step == 0)
    def _():
        lines = [
            pltpu.make_async_copy(
                row_refs[n].at[pl.ds(span - meta_extra, meta_extra), pl.ds(0, 128)],
                meta_low.at[pl.ds(n * meta_extra, meta_extra)],
                meta_sems.at[n],
            )
            for n in range(sources)
        ]
        for copy in lines + loads:
            copy.start()
        for copy in lines:
            copy.wait()
        meta_wide[...] = meta_low[...].astype(jnp.float32).astype(jnp.int32)
        to_scalars = pltpu.make_async_copy(meta_wide, meta_ref, meta_sems.at[sources])
        to_scalars.start()
        to_scalars.wait()
        for copy in loads:
            copy.wait()

    def entry(n, field):
        return meta_ref[n * meta_extra + (n % cores) * per_core + begin + step, field]

    centre = centres[step]
    wide = centre.astype(jnp.float32)
    half_norm = 0.5 * jnp.sum(wide * wide, axis=1, keepdims=True)
    slot = lax.broadcasted_iota(jnp.int32, (1, sources * window), 1)
    valid = slot < 0
    for n in range(sources):
        low = n * window + entry(n, 1)
        valid = valid | ((slot >= low) & (slot < low + entry(n, 2)))
    chosen = jnp.concatenate(
        [held[n, pl.ds(pl.multiple_of(entry(n, 0) * 16, 16), window)] for n in range(sources)]
    )
    products = lax.dot_general(
        centre, chosen, (((1,), (1,)), ((), ())), preferred_element_type=jnp.float32
    )
    scores = sharp_ref[code_ref[2] * per_core + begin + step] * (products - half_norm)
    top = jnp.max(scores, axis=0, keepdims=True)
    exponent = jnp.exp(scores - top)
    total = jnp.sum(exponent, axis=0, keepdims=True)
    score_ref[0] = jnp.broadcast_to(
        jnp.where(valid, top + jnp.log(total), 0.0), score_ref.shape[1:]
    )
    resp = exponent * jnp.where(valid, 1.0 / total, 0.0)
    mass = jnp.sum(resp, axis=1, keepdims=True)
    mass_ref[step] = jnp.broadcast_to(mass, (mass.shape[0], 128)).T[: mass_ref.shape[1]]
    low = resp.astype(jnp.bfloat16)
    numer = jnp.dot(low, chosen, preferred_element_type=jnp.float32)
    keep_ref[0] = numer[:share] + prior_mass * centre[:share].astype(jnp.float32) if near else numer[:share]
    for n, ref in enumerate(send_refs):
        at_row = pl.multiple_of(step * share, share)
        ref[pl.ds(at_row, share)] = numer[(n + 1) * share : (n + 2) * share].astype(ref.dtype)

    if tail:

        @pl.when(step == steps - 1)
        def _():
            lines = [r[i, :1] for r in (*earlier_refs, mass_ref) for i in range(r.shape[0])]
            for n, ref in enumerate(send_refs):
                part = [v[:, (n + 1) * share : (n + 2) * share] for v in lines]
                rows = _split(jnp.concatenate(part, axis=0), tail)
                ref[pl.ds(steps * share, tail)] = jnp.zeros((tail, ref.shape[1]), ref.dtype)
                ref[pl.ds(steps * share, tail), pl.ds(0, share)] = rows.astype(ref.dtype)


def _pack_kernel(sources, window, *refs):
    line = 0
    for score_ref in refs[:-sources]:
        size = score_ref.shape[0]
        for n, out_ref in enumerate(refs[-sources:]):
            out_ref[line : line + size] = score_ref[:, n * window : (n + 1) * window]
        line += size


def _score_kernel(cells, window, rel_ref, off_ref, values_ref, out_ref):
    rows = rel_ref.shape[1]
    hot = jnp.where(
        lax.broadcasted_iota(jnp.int32, (window, rows), 0) == off_ref[...], 1.0, 0.0
    ).astype(jnp.bfloat16)
    rest = values_ref[...]
    mine = lax.broadcasted_iota(jnp.int32, (cells, rows), 0) == rel_ref[...]
    total = jnp.zeros((cells, rows), jnp.float32)
    for _ in range(3):
        term = rest.astype(jnp.bfloat16)
        rest = rest - term.astype(jnp.float32)
        total += jnp.dot(term, hot, preferred_element_type=jnp.float32)
    out_ref[...] = jnp.sum(jnp.where(mine, total, 0.0), axis=0, keepdims=True)


def _after(value, *others):
    return lax.optimization_barrier((value, *others))[0]


def _update_kernel(per_core, chips, piece, tail, code_ref, keep_ref, mass_ref, *refs):
    got_refs, refs = refs[: 2 * (chips - 1)], refs[2 * (chips - 1) :]
    first_ref, others_ref, tail_ref, out_ref, swap_ref, lines_ref, weight = refs
    step = pl.program_id(0)
    lines = mass_ref[:, 0, :128]
    for ref in [*got_refs[1::2], tail_ref]:
        rows = ref[...].astype(jnp.float32)
        for n in range(3):
            lines = lines + rows[n * per_core : (n + 1) * per_core]
    line = lax.broadcasted_iota(jnp.int32, lines.shape, 0)
    mine = jnp.sum(jnp.where(line == step, lines, 0.0), axis=0, keepdims=True)
    weight[...] = jnp.broadcast_to(1.0 / (mine + prior_mass), (128, 128)).T

    @pl.when(step == 0)
    def _():
        lines_ref[...] = jnp.concatenate(
            [lines, jnp.zeros((lines_ref.shape[0] - per_core, 128), jnp.float32)], axis=0
        )

    def updated(at_kid):
        rows = pl.ds(pl.multiple_of(at_kid, piece), piece)
        numer = keep_ref[0, rows]
        for ref in got_refs[0::2]:
            numer = numer + ref[rows].astype(jnp.float32)
        far = jnp.where(step == 0, first_ref[rows], others_ref[rows])
        return (numer + far.astype(jnp.float32)) * weight[rows, :1]

    here = lax.rem(code_ref[2] + code_ref[1], 2) * piece
    out_ref[0] = updated(here)
    swap_ref[0, :piece] = updated(piece - here)
    swap_ref[0, piece:] = jnp.zeros((8, swap_ref.shape[2]), jnp.float32)
    swap_ref[0, piece:, :128] = jnp.broadcast_to(mine, (8, 128))


def _finish_kernel(per_core, piece, code_ref, _, swap_ref, line_ref, lines_ref, out_ref, mass_ref, sem):
    other = 1 - code_ref[2]
    copy = pltpu.make_async_copy(
        swap_ref.at[:, pl.ds(0, piece)], out_ref.at[pl.ds(other * per_core, per_core)], sem
    )
    copy.start()
    mine = lines_ref[:per_core]
    theirs = line_ref[:, 0]
    lines = jnp.where(
        other == 1, jnp.concatenate([mine, theirs], axis=0), jnp.concatenate([theirs, mine], axis=0)
    )
    here = lax.rem(code_ref[2] + code_ref[1], 2)
    mass_ref[...] = jnp.where(here == 0, lines[:, :piece], lines[:, piece : 2 * piece])
    copy.wait()


def _params():
    return pltpu.CompilerParams(vmem_limit_bytes=vmem_limit)


def _cell_call(code, sharp, arrays, near, row_blocks, window, reach, per_core, begin, steps, kids, share, sends, earlier, tail):
    sources = len(row_blocks)
    span, width = row_blocks[0].shape
    pieces = kids // (share // 2)
    rows = sources * window
    out_shape = [
        jax.ShapeDtypeStruct((steps, share, width), jnp.float32),
        jax.ShapeDtypeStruct((steps, 8, kids), jnp.float32),
        jax.ShapeDtypeStruct((steps, 8, rows), jnp.float32),
    ] + [jax.ShapeDtypeStruct((steps * share + tail, width), wire)] * sends
    fixed = lambda shape: pl.BlockSpec(shape, lambda n, *_: (0,) * len(shape))
    moving = lambda shape: pl.BlockSpec((1, *shape[1:]), lambda n, *_: (n, 0, 0))
    return pl.pallas_call(
        functools.partial(
            _cell_kernel, sources, window, reach, pieces, near, share, steps, per_core, begin, span, len(earlier), tail
        ),
        grid_spec=pltpu.PrefetchScalarGridSpec(
            num_scalar_prefetch=2,
            grid=(steps,),
            in_specs=[anywhere] * (len(arrays) + sources) + [fixed(v.shape) for v in earlier],
            out_specs=[
                (moving if n in (0, 2) else fixed)(o.shape) for n, o in enumerate(out_shape)
            ],
            scratch_shapes=[
                pltpu.VMEM((sources, reach, width), jnp.bfloat16),
                pltpu.VMEM((steps, kids, width), jnp.bfloat16),
                pltpu.SemaphoreType.DMA((sources + pieces,)),
                pltpu.VMEM((sources * meta_extra, 128), jnp.bfloat16),
                pltpu.VMEM((sources * meta_extra, 128), jnp.int32),
                pltpu.SMEM((sources * meta_extra, 128), jnp.int32),
                pltpu.SemaphoreType.DMA((sources + 1,)),
            ],
        ),
        out_shape=out_shape,
        compiler_params=pltpu.CompilerParams(vmem_limit_bytes=44 * 1024 * 1024),
        cost_estimate=busy,
    )(code, sharp, *arrays, *row_blocks, *earlier)


def on_device(frames, labels, centroids, sharpness):
    cell_count = lax.axis_size("cell")
    frame_count = lax.axis_size("frame")
    group_count = 2
    cells_local, kids, width = centroids.shape
    rows = frames.shape[0]
    cells_total = cells_local * cell_count
    half = cell_count // 2
    chips = frame_count // cores
    per_core = cells_local // cores
    cell_cap = 3 * rows // cells_total
    own_slots = 2 * rows // cell_count
    sources = half * cores
    window = -(-(cell_cap + 16) // 16) * 16
    while sources * window % 128:
        window += 16
    reach = min(own_slots, -(-per_core * cell_cap // 16) * 16)
    window = min(window, reach)
    share = kids // chips
    piece = share // group_count

    z = lax.axis_index("cell")
    j = lax.axis_index("frame")
    y = lax.axis_index("groups")
    x, k = j // cores, j % cores
    p, h = z % half, z // half

    def at(zz, xx, kk):
        return zz * frame_count + xx * cores + kk

    def hop_core(v):
        return lax.ppermute(v, "frame", [(i, i ^ 1) for i in range(frame_count)])

    def hop_chip(v, s):
        return lax.ppermute(
            v,
            "frame",
            [(a * cores + c, (a + s) % chips * cores + c) for a in range(chips) for c in range(cores)],
        )

    def hop_member(v, s):
        return lax.ppermute(
            v, "cell", [(b * half + i, b * half + (i + s) % half) for b in range(2) for i in range(half)]
        )

    def hop_partner(v):
        return lax.ppermute(v, "cell", [(i, (i + half) % cell_count) for i in range(cell_count)])

    def hop_group(v):
        return lax.ppermute(v, "groups", [(i, 1 - i) for i in range(2)])

    def hop_any(v, s, kk):
        pairs = [
            (at(b * half + i, a, c), at(b * half + (i + s) % half, a, c ^ kk))
            for b in range(2)
            for i in range(half)
            for a in range(chips)
            for c in range(cores)
        ]
        return lax.ppermute(v, ("cell", "frame"), pairs)

    parts = [(0, 1), (1, per_core - 1)]
    foreign_sharp = hop_partner(sharpness)
    first = hop_partner(
        lax.dynamic_slice(
            centroids,
            (k * per_core, (x * group_count + y) * piece, 0),
            (per_core, piece, width),
        )
    )
    by_chip = [first] + [hop_chip(first, -s) for s in range(1, chips)]
    foreign_pieces = [v for c in by_chip for v in (c, hop_group(c))]
    around = by_chip[1:] + foreign_pieces[1:2]

    label = labels.reshape(1, rows)
    owner, local = label // cells_local, label % cells_local
    member = (owner % half - p + half) % half
    foreign = (owner // half != h).astype(jnp.int32)
    other = (local // per_core) ^ k
    rel = (member * 2 + foreign) * meta_extra + other * per_core + local % per_core

    seg = lambda s, t: s * 2 + t
    first_segs = [seg(s, 1) for s in range(1, half)]
    next_segs = [seg(s, 0) for s in range(1, half)]
    span = own_slots + meta_extra
    block = jax.ShapeDtypeStruct((span, width), jnp.bfloat16)
    lines = cell_count * meta_extra
    flat, off, meta, *blocks = pl.pallas_call(
        functools.partial(_place_kernel, per_core, reach, window, own_slots, first_segs),
        out_shape=[
            jax.ShapeDtypeStruct((1, rows), jnp.int32),
            jax.ShapeDtypeStruct((1, rows), jnp.int32),
            jax.ShapeDtypeStruct((lines, 128), jnp.float32),
        ]
        + [block] * len(first_segs),
        compiler_params=_params(),
        cost_estimate=dear,
    )(rel, frames)
    segments = dict(zip(first_segs, blocks, strict=True))

    blocks = pl.pallas_call(
        functools.partial(_pick_kernel, next_segs),
        out_shape=[block] * len(next_segs),
        compiler_params=_params(),
        cost_estimate=dear,
    )(_after(flat, first), meta, frames)
    segments.update(zip(next_segs, blocks, strict=True))
    received = {1: [hop_member(segments[seg(s, 1)], s) for s in range(1, half)]}
    here = {}
    for t, gate in ((1, (*blocks, foreign_sharp, *around)), (0, received[1])):
        here[t] = pl.pallas_call(
            functools.partial(_pick_kernel, [seg(0, t)]),
            out_shape=[block],
            compiler_params=_params(),
            cost_estimate=dear,
        )(_after(flat, *gate), meta, frames)[0]

    received[0] = [hop_member(segments[seg(s, 0)], s) for s in range(1, half)]

    def held_of(t, *gate):
        held = [here[t], hop_core(here[t])]
        for v in received[t]:
            v = _after(v, *gate)
            held += [v, hop_core(v)]
        return held

    held = {1: held_of(1, *around)}

    code = jnp.stack([x, y, k]).astype(jnp.int32)
    tail = -(-3 * per_core // 16) * 16

    def masses_in(rows):
        rows = rows[:, :share].astype(jnp.float32)
        return sum(rows[n * per_core : (n + 1) * per_core] for n in range(3))

    def over_chips(result, steps, earlier, extra):
        keep, mass, _, *sends = result
        mass = jnp.concatenate([*earlier, mass])[:, 0, :share]
        for s in range(1, chips):
            got = hop_chip(sends[s - 1], s)
            keep = keep + got[: steps * share].reshape(keep.shape).astype(jnp.float32)
            if extra:
                mass = mass + masses_in(got[steps * share :])
        return keep, mass

    results, totals, theirs, notes = [], [], [], []
    for t, begin, size in [(1, *part) for part in parts] + [(0, 0, per_core)]:
        if not t:
            held[0] = held_of(0, totals[0])
            notes.append(
                pl.pallas_call(
                    _copy_kernel,
                    out_shape=jax.ShapeDtypeStruct(notes[-1].shape, jnp.float32),
                    compiler_params=_params(),
                    cost_estimate=dear,
                )(_after(notes.pop(), totals[1]))
            )
        code_here = _after(code, notes[-1]) if results else code
        earlier = [r[1] for r in results] if t else []
        extra = 0 if t and begin + size < per_core else tail
        results.append(
            _cell_call(
                code_here, foreign_sharp if t else sharpness, foreign_pieces if t else [centroids],
                not t, held[t], window, reach, per_core,
                begin, size, kids, share, chips - 1, earlier if extra else [], extra,
            )
        )
        if t:
            scores = results[-1][2]
            if totals:
                scores = _after(scores, totals[0])
            notes.append(
                pl.pallas_call(
                    _note_kernel,
                    out_shape=jax.ShapeDtypeStruct((size, sources * window), jnp.float32),
                    compiler_params=_params(),
                    cost_estimate=dear,
                )(scores)
            )
        if not t:
            arrived = [hop_chip(results[-1][3 + n], n + 1) for n in range(chips - 1)]
            break
        total, mass = over_chips(results[-1], size, earlier, extra)
        if t and extra:
            total = _after(total, notes[-1])
        total = total.astype(wire).reshape(size * share, width)
        if extra:
            high = _round(mass)
            middle = _round(mass - high)
            terms = jnp.concatenate([high, middle, mass - high - middle])
            behind = jnp.pad(terms.astype(wire), ((0, tail - terms.shape[0]), (0, width - share)))
            total = jnp.concatenate([total, behind])
        theirs.append(hop_partner(total))
        totals.append(total)
    score_parts = pl.pallas_call(
        functools.partial(_pack_kernel, sources, window),
        out_shape=[jax.ShapeDtypeStruct((2 * per_core, window), jnp.float32)] * sources,
        compiler_params=_params(),
        cost_estimate=dear,
    )(*notes, results[-1][2][:, 0])

    back = {}
    for s in range(half):
        for kk in range(cores):
            n = s * cores + kk
            back[s, kk] = score_parts[n] if n == 0 else hop_any(score_parts[n], -s, kk)
    values = []
    for s in range(half):
        for t in range(2):
            at_row = 0 if t else per_core
            for kk in range(cores):
                values.append(back[s, kk][at_row : at_row + per_core])
            values.append(jnp.zeros((meta_extra - cells_local, window), jnp.float32))
    frame_score = pl.pallas_call(
        functools.partial(_score_kernel, lines, window),
        out_shape=jax.ShapeDtypeStruct((1, rows), jnp.float32),
        compiler_params=_params(),
        cost_estimate=dear,
    )(rel, off, jnp.concatenate(values, axis=0)).reshape(rows)

    theirs = [_after(v, *arrived) for v in theirs]
    one_cell = lambda block, where: pl.BlockSpec(block, where)
    whole = lambda v: pl.BlockSpec(v.shape, lambda n, c: (0,) * v.ndim)
    behind = lambda steps: pl.BlockSpec((tail, 128), lambda n, c: (steps * share // tail, 0))
    keep, mass = results[-1][:2]
    got, got_specs = [], []
    for v in arrived:
        got += [v, v]
        got_specs += [one_cell((share, width), lambda n, c: (n, 0)), behind(per_core)]
    out, swap, lines_mine = pl.pallas_call(
        functools.partial(_update_kernel, per_core, chips, piece, tail),
        grid_spec=pltpu.PrefetchScalarGridSpec(
            num_scalar_prefetch=1,
            grid=(per_core,),
            in_specs=[
                one_cell((1, share, width), lambda n, c: (n, 0, 0)),
                whole(mass),
                *got_specs,
                one_cell((share, width), lambda n, c: (0, 0)),
                one_cell((share, width), lambda n, c: (jnp.maximum(n - 1, 0), 0)),
                behind(per_core - 1),
            ],
            out_specs=[
                one_cell((1, piece, width), lambda n, c: (c[2] * per_core + n, 0, 0)),
                one_cell((1, piece + 8, width), lambda n, c: (n, 0, 0)),
                pl.BlockSpec((8, 128), lambda n, c: (0, 0)),
            ],
            scratch_shapes=[pltpu.VMEM((128, 128), jnp.float32)],
        ),
        out_shape=[
            jax.ShapeDtypeStruct((cells_local, piece, width), jnp.float32),
            jax.ShapeDtypeStruct((per_core, piece + 8, width), jnp.float32),
            jax.ShapeDtypeStruct((8, 128), jnp.float32),
        ],
        compiler_params=_params(),
        cost_estimate=busy,
    )(code, keep, mass, *got, theirs[0], theirs[1], theirs[1])
    swapped = hop_core(swap)
    new_centroids, child_mass = pl.pallas_call(
        functools.partial(_finish_kernel, per_core, piece),
        grid_spec=pltpu.PrefetchScalarGridSpec(
            num_scalar_prefetch=1,
            grid=(1,),
            in_specs=[
                anywhere,
                anywhere,
                pl.BlockSpec((per_core, 8, 128), lambda n, c: (0, piece // 8, 0)),
                pl.BlockSpec((8, 128), lambda n, c: (0, 0)),
            ],
            out_specs=[anywhere, pl.BlockSpec((cells_local, piece), lambda n, c: (0, 0))],
            scratch_shapes=[pltpu.SemaphoreType.DMA(())],
        ),
        out_shape=[
            jax.ShapeDtypeStruct(out.shape, jnp.float32),
            jax.ShapeDtypeStruct((cells_local, piece), jnp.float32),
        ],
        input_output_aliases={1: 0},
        compiler_params=_params(),
        cost_estimate=busy,
    )(code, out, swapped, swapped, lines_mine)
    return new_centroids, child_mass, frame_score


def solution(mesh):
    return jax.shard_map(
        on_device,
        mesh=mesh,
        in_specs=(
            P(("groups", "cell", "frame"), None),
            P(("groups", "cell", "frame"), None),
            P("cell", None, None),
            P("cell"),
        ),
        out_specs=(
            P(("groups", "cell"), "frame", None),
            P(("groups", "cell"), "frame"),
            P(("groups", "cell", "frame")),
        ),
        check_vma=False,
    )
```

```python
import functools

import jax
import jax.numpy as jnp
from jax import lax
from jax.experimental import pallas as pl
from jax.experimental.pallas import tpu as pltpu
from jax.sharding import PartitionSpec as P

prior_mass = 1.0
cores = 2
wire = jnp.bfloat16
vmem_limit = 16 * 1024 * 1024
anywhere = pl.BlockSpec(memory_space=pl.ANY)
cheap = pl.CostEstimate(flops=1, bytes_accessed=1, transcendentals=0)
busy = pl.CostEstimate(flops=20_000_000_000, bytes_accessed=1, transcendentals=0)
dear = pl.CostEstimate(flops=20_000_000_000, bytes_accessed=1_000_000_000, transcendentals=0)
meta_extra = 16


def _hot(flat_row, segment, own_slots):
    rows = flat_row.shape[1]
    slot = lax.broadcasted_iota(jnp.int32, (own_slots, rows), 0) + segment * own_slots
    return jnp.where(slot == flat_row, 1.0, 0.0).astype(jnp.bfloat16)


def _pick(flat_row, meta, frames_ref, segment, out_ref):
    own_slots = out_ref.shape[0] - meta_extra
    hot = _hot(flat_row, segment, own_slots)
    out_ref[pl.ds(0, own_slots)] = jnp.dot(
        hot, frames_ref[...], preferred_element_type=jnp.float32
    ).astype(jnp.bfloat16)
    out_ref[pl.ds(own_slots, meta_extra)] = jnp.zeros((meta_extra, out_ref.shape[1]), jnp.bfloat16)
    out_ref[pl.ds(own_slots, meta_extra), pl.ds(0, 128)] = meta[
        segment * meta_extra : (segment + 1) * meta_extra
    ].astype(jnp.bfloat16)


def _place_kernel(
    per_core, reach, window, own_slots, segments, rel_ref, frames_ref, flat_ref, off_ref, meta_ref, *outs
):
    rows = rel_ref.shape[1]
    lines = meta_ref.shape[0]
    rel = rel_ref[...]
    line = lax.broadcasted_iota(jnp.int32, (lines, rows), 0)
    base = (line // meta_extra) * meta_extra
    segment = rel // meta_extra
    hits = jnp.where(rel == line, 1, 0)
    lane = lax.broadcasted_iota(jnp.int32, (lines, rows), 1)
    running = hits
    step = 1
    while step < rows:
        running += jnp.where(lane >= step, pltpu.roll(running, step, 1), 0)
        step *= 2
    count = jnp.sum(hits, axis=1, keepdims=True)
    ahead = jnp.sum(jnp.where((rel < line) & (rel >= base), 1, 0), axis=1, keepdims=True)
    behind = jnp.sum(
        jnp.where((rel >= line) & (rel < base + meta_extra), 1, 0), axis=1, keepdims=True
    )
    back = (line - base)[:, :1] >= per_core
    start = jnp.where(back, own_slots - behind, ahead)
    floor = jnp.where(back, own_slots - reach, 0)
    first = jnp.minimum(((start - floor) >> 4) << 4, reach - window) + floor
    position = jnp.sum(hits * (running + (start - 1)), axis=0, keepdims=True)
    flat = segment * own_slots + position
    flat_ref[...] = flat
    off_ref[...] = jnp.sum(hits * (running + (start - first - 1)), axis=0, keepdims=True)
    column = lax.broadcasted_iota(jnp.int32, meta_ref.shape, 1)
    meta = jnp.where(
        column == 0,
        (first - floor) >> 4,
        jnp.where(column == 1, start - first, jnp.where(column == 2, count, 0)),
    ).astype(jnp.float32)
    meta_ref[...] = meta
    for g, out_ref in zip(segments, outs, strict=True):
        _pick(flat, meta, frames_ref, g, out_ref)


def _pick_kernel(segments, flat_ref, meta_ref, frames_ref, *outs):
    flat, meta = flat_ref[...], meta_ref[...]
    for g, out_ref in zip(segments, outs, strict=True):
        _pick(flat, meta, frames_ref, g, out_ref)


def _split(lines, rows):
    high = lines.astype(jnp.bfloat16).astype(jnp.float32)
    middle = (lines - high).astype(jnp.bfloat16).astype(jnp.float32)
    rest = jnp.zeros((rows - 3 * lines.shape[0], lines.shape[1]), jnp.float32)
    return jnp.concatenate([high, middle, lines - high - middle, rest], axis=0)


def _round(value):
    return lax.reduce_precision(value, 8, 7)


def _note_kernel(score_ref, out_ref):
    out_ref[...] = score_ref[:, 0]


def _copy_kernel(in_ref, out_ref):
    out_ref[...] = in_ref[...]


def _split(lines, rows):
    high = lines.astype(jnp.bfloat16).astype(jnp.float32)
    middle = (lines - high).astype(jnp.bfloat16).astype(jnp.float32)
    rest = jnp.zeros((rows - 3 * lines.shape[0], lines.shape[1]), jnp.float32)
    return jnp.concatenate([high, middle, lines - high - middle, rest], axis=0)


def _round(value):
    return lax.reduce_precision(value, 8, 7)


def _note_kernel(score_ref, out_ref):
    out_ref[...] = score_ref[:, 0]


def _copy_kernel(in_ref, out_ref):
    out_ref[...] = in_ref[...]


def _prior_kernel(group_count, code_ref, *refs):
    for g in range(group_count):
        size = refs[g].shape[1]
        refs[-1][:, g * size : (g + 1) * size] = refs[g][...].astype(jnp.float32)


def _cell_kernel(sources, window, reach, pieces, places, near, share, steps, per_core, begin, span, earlier, tail, *refs):
    code_ref, sharp_ref = refs[:2]
    refs = refs[2:]
    centre_refs, refs = refs[: len(places)], refs[len(places) :]
    piece = share // 2
    row_refs, refs = refs[:sources], refs[sources:]
    earlier_refs, refs = refs[:earlier], refs[earlier:]
    keep_ref, mass_ref, score_ref = refs[:3]
    send_refs, (held, centres, sems, meta_low, meta_wide, meta_ref, meta_sems) = refs[3:-7], refs[-7:]
    step = pl.program_id(0)
    loads = []
    for n in range(sources):
        low = 0 if n % cores == 0 else span - meta_extra - reach
        loads.append(
            pltpu.make_async_copy(
                row_refs[n].at[pl.ds(low, reach)],
                held.at[n, pl.ds(0, reach)],
                sems.at[n],
            )
        )
    if not near:
        for n, low in enumerate(places):
            loads.append(
                pltpu.make_async_copy(
                    centre_refs[n].at[pl.ds(begin, steps)],
                    centres.at[:, pl.ds(low, centre_refs[n].shape[1])],
                    sems.at[sources + n],
                )
            )

    @pl.when(step == 0)
    def _():
        lines = [
            pltpu.make_async_copy(
                row_refs[n].at[pl.ds(span - meta_extra, meta_extra), pl.ds(0, 128)],
                meta_low.at[pl.ds(n * meta_extra, meta_extra)],
                meta_sems.at[n],
            )
            for n in range(sources)
        ]
        for copy in lines + loads:
            copy.start()
        for copy in lines:
            copy.wait()
        meta_wide[...] = meta_low[...].astype(jnp.float32).astype(jnp.int32)
        to_scalars = pltpu.make_async_copy(meta_wide, meta_ref, meta_sems.at[sources])
        to_scalars.start()
        to_scalars.wait()
        for copy in loads:
            copy.wait()

    def entry(n, field):
        return meta_ref[n * meta_extra + (n % cores) * per_core + begin + step, field]

    if near:
        found = []
        for n in range(pieces):
            chip = lax.rem(code_ref[0] + n // 2, pieces // 2)
            kid = (chip * 2 + lax.rem(code_ref[1] + n % 2, 2)) * piece
            found.append(centre_refs[0][0, pl.ds(pl.multiple_of(kid, piece), piece)])
        centre = jnp.concatenate(found, axis=0)
    else:
        centre = centres[step]
    wide = centre.astype(jnp.float32)
    half_norm = 0.5 * jnp.sum(wide * wide, axis=1, keepdims=True)
    slot = lax.broadcasted_iota(jnp.int32, (1, sources * window), 1)
    valid = slot < 0
    for n in range(sources):
        low = n * window + entry(n, 1)
        valid = valid | ((slot >= low) & (slot < low + entry(n, 2)))
    chosen = jnp.concatenate(
        [held[n, pl.ds(pl.multiple_of(entry(n, 0) * 16, 16), window)] for n in range(sources)]
    )
    products = lax.dot_general(
        centre, chosen, (((1,), (1,)), ((), ())), preferred_element_type=jnp.float32
    )
    scores = sharp_ref[code_ref[2] * per_core + begin + step] * (products - half_norm)
    top = jnp.max(scores, axis=0, keepdims=True)
    exponent = jnp.exp(scores - top)
    total = jnp.sum(exponent, axis=0, keepdims=True)
    score_ref[0] = jnp.broadcast_to(
        jnp.where(valid, top + jnp.log(total), 0.0), score_ref.shape[1:]
    )
    resp = exponent * jnp.where(valid, 1.0 / total, 0.0)
    mass = jnp.sum(resp, axis=1, keepdims=True)
    mass_ref[step] = jnp.broadcast_to(mass, (mass.shape[0], 128)).T[: mass_ref.shape[1]]
    low = resp.astype(jnp.bfloat16)
    numer = jnp.dot(low, chosen, preferred_element_type=jnp.float32)
    keep_ref[0] = numer[:share] + prior_mass * centre[:share].astype(jnp.float32) if near else numer[:share]
    for n, ref in enumerate(send_refs):
        at_row = pl.multiple_of(step * share, share)
        ref[pl.ds(at_row, share)] = numer[(n + 1) * share : (n + 2) * share].astype(ref.dtype)

    if tail:

        @pl.when(step == steps - 1)
        def _():
            lines = [r[i, :1] for r in (*earlier_refs, mass_ref) for i in range(r.shape[0])]
            for n, ref in enumerate(send_refs):
                part = [v[:, (n + 1) * share : (n + 2) * share] for v in lines]
                rows = _split(jnp.concatenate(part, axis=0), tail)
                ref[pl.ds(steps * share, tail)] = jnp.zeros((tail, ref.shape[1]), ref.dtype)
                ref[pl.ds(steps * share, tail), pl.ds(0, share)] = rows.astype(ref.dtype)


def _pack_kernel(sources, window, *refs):
    line = 0
    for score_ref in refs[:-sources]:
        size = score_ref.shape[0]
        for n, out_ref in enumerate(refs[-sources:]):
            out_ref[line : line + size] = score_ref[:, n * window : (n + 1) * window]
        line += size


def _score_kernel(cells, window, rel_ref, off_ref, values_ref, out_ref):
    rows = rel_ref.shape[1]
    hot = jnp.where(
        lax.broadcasted_iota(jnp.int32, (window, rows), 0) == off_ref[...], 1.0, 0.0
    ).astype(jnp.bfloat16)
    rest = values_ref[...]
    mine = lax.broadcasted_iota(jnp.int32, (cells, rows), 0) == rel_ref[...]
    total = jnp.zeros((cells, rows), jnp.float32)
    for _ in range(3):
        term = rest.astype(jnp.bfloat16)
        rest = rest - term.astype(jnp.float32)
        total += jnp.dot(term, hot, preferred_element_type=jnp.float32)
    out_ref[...] = jnp.sum(jnp.where(mine, total, 0.0), axis=0, keepdims=True)


def _after(value, *others):
    return lax.optimization_barrier((value, *others))[0]


def _update_kernel(per_core, chips, piece, mine, code_ref, keep_ref, mass_ref, *refs):
    got_refs, refs = refs[: 2 * (chips - 1)], refs[2 * (chips - 1) :]
    (first_ref, others_ref, tail_ref), out_ref, weight = refs[:3], refs[3], refs[-1]
    step = pl.program_id(0)
    lines = mass_ref[:, 0, :128]
    for ref in [*got_refs[1::2], tail_ref]:
        rows = ref[...].astype(jnp.float32)
        for n in range(3):
            lines = lines + rows[n * per_core : (n + 1) * per_core]
    line = lax.broadcasted_iota(jnp.int32, lines.shape, 0)
    mass = jnp.sum(jnp.where(line == step, lines, 0.0), axis=0, keepdims=True)
    weight[...] = jnp.broadcast_to(1.0 / (mass + prior_mass), (128, 128)).T
    numer = keep_ref[0]
    for ref in got_refs[0::2]:
        numer = numer + ref[...].astype(jnp.float32)
    far = jnp.where(step == 0, first_ref[...], others_ref[...])
    low = lax.rem((code_ref[2] if mine else 1 - code_ref[2]) + code_ref[1], 2) * piece
    numer = numer + far.astype(jnp.float32)
    out_ref[0, :piece] = numer * weight[pl.ds(pl.multiple_of(low, piece), piece), :1]
    if not mine:
        out_ref[0, piece:] = jnp.zeros((8, out_ref.shape[2]), jnp.float32)
        out_ref[0, piece:, :128] = jnp.broadcast_to(mass, (8, 128))
        lines_ref = refs[4]

        @pl.when(step == 0)
        def _():
            lines_ref[...] = jnp.concatenate(
                [lines, jnp.zeros((lines_ref.shape[0] - per_core, 128), jnp.float32)], axis=0
            )


def _finish_kernel(per_core, piece, code_ref, _, swap_ref, line_ref, lines_ref, out_ref, mass_ref, sem):
    other = 1 - code_ref[2]
    copy = pltpu.make_async_copy(
        swap_ref.at[:, pl.ds(0, piece)], out_ref.at[pl.ds(other * per_core, per_core)], sem
    )
    copy.start()
    mine = lines_ref[:per_core]
    theirs = line_ref[:, 0]
    lines = jnp.where(
        other == 1, jnp.concatenate([mine, theirs], axis=0), jnp.concatenate([theirs, mine], axis=0)
    )
    here = lax.rem(code_ref[2] + code_ref[1], 2)
    mass_ref[...] = jnp.where(here == 0, lines[:, :piece], lines[:, piece : 2 * piece])
    copy.wait()


def _params():
    return pltpu.CompilerParams(vmem_limit_bytes=vmem_limit)


def _cell_call(code, sharp, arrays, near, row_blocks, window, reach, per_core, begin, steps, kids, share, sends, earlier, tail):
    sources = len(row_blocks)
    span, width = row_blocks[0].shape
    pieces = kids // (share // 2)
    arrays, places = zip(*arrays, strict=True)
    rows = sources * window
    out_shape = [
        jax.ShapeDtypeStruct((steps, share, width), jnp.float32),
        jax.ShapeDtypeStruct((steps, 8, kids), jnp.float32),
        jax.ShapeDtypeStruct((steps, 8, rows), jnp.float32),
    ] + [jax.ShapeDtypeStruct((steps * share + tail, width), wire)] * sends
    fixed = lambda shape: pl.BlockSpec(shape, lambda n, *_: (0,) * len(shape))
    moving = lambda shape: pl.BlockSpec((1, *shape[1:]), lambda n, *_: (n, 0, 0))
    return pl.pallas_call(
        functools.partial(
            _cell_kernel, sources, window, reach, pieces, places, near, share, steps, per_core, begin, span, len(earlier), tail
        ),
        grid_spec=pltpu.PrefetchScalarGridSpec(
            num_scalar_prefetch=2,
            grid=(steps,),
            in_specs=(
                [pl.BlockSpec((1, kids, width), lambda n, c, _: (c[2] * per_core + begin + n, 0, 0))]
                if near
                else [anywhere] * len(arrays)
            )
            + [anywhere] * sources
            + [fixed(v.shape) for v in earlier],
            out_specs=[
                (moving if n in (0, 2) else fixed)(o.shape) for n, o in enumerate(out_shape)
            ],
            scratch_shapes=[
                pltpu.VMEM((sources, reach, width), jnp.bfloat16),
                pltpu.VMEM((1 if near else steps, kids, width), jnp.bfloat16),
                pltpu.SemaphoreType.DMA((sources + len(places),)),
                pltpu.VMEM((sources * meta_extra, 128), jnp.bfloat16),
                pltpu.VMEM((sources * meta_extra, 128), jnp.int32),
                pltpu.SMEM((sources * meta_extra, 128), jnp.int32),
                pltpu.SemaphoreType.DMA((sources + 1,)),
            ],
        ),
        out_shape=out_shape,
        compiler_params=pltpu.CompilerParams(vmem_limit_bytes=44 * 1024 * 1024),
        cost_estimate=busy,
    )(code, sharp, *arrays, *row_blocks, *earlier)


def on_device(frames, labels, centroids, sharpness):
    cell_count = lax.axis_size("cell")
    frame_count = lax.axis_size("frame")
    group_count = 2
    cells_local, kids, width = centroids.shape
    rows = frames.shape[0]
    cells_total = cells_local * cell_count
    half = cell_count // 2
    chips = frame_count // cores
    per_core = cells_local // cores
    cell_cap = 3 * rows // cells_total
    own_slots = 2 * rows // cell_count
    sources = half * cores
    window = -(-(cell_cap + 16) // 16) * 16
    while sources * window % 128:
        window += 16
    reach = min(own_slots, -(-per_core * cell_cap // 16) * 16)
    window = min(window, reach)
    share = kids // chips
    piece = share // group_count

    z = lax.axis_index("cell")
    j = lax.axis_index("frame")
    y = lax.axis_index("groups")
    x, k = j // cores, j % cores
    p, h = z % half, z // half

    def at(zz, xx, kk):
        return zz * frame_count + xx * cores + kk

    def hop_core(v):
        return lax.ppermute(v, "frame", [(i, i ^ 1) for i in range(frame_count)])

    def hop_chip(v, s):
        return lax.ppermute(
            v,
            "frame",
            [(a * cores + c, (a + s) % chips * cores + c) for a in range(chips) for c in range(cores)],
        )

    def hop_member(v, s):
        return lax.ppermute(
            v, "cell", [(b * half + i, b * half + (i + s) % half) for b in range(2) for i in range(half)]
        )

    def hop_partner(v):
        return lax.ppermute(v, "cell", [(i, (i + half) % cell_count) for i in range(cell_count)])

    def hop_group(v):
        return lax.ppermute(v, "groups", [(i, 1 - i) for i in range(2)])

    def hop_any(v, s, kk):
        pairs = [
            (at(b * half + i, a, c), at(b * half + (i + s) % half, a, c ^ kk))
            for b in range(2)
            for i in range(half)
            for a in range(chips)
            for c in range(cores)
        ]
        return lax.ppermute(v, ("cell", "frame"), pairs)

    parts = [(0, 1), (1, per_core - 1)]
    foreign_sharp = hop_partner(sharpness)
    first = hop_partner(
        lax.dynamic_slice(
            centroids,
            (k * per_core, (x * group_count + y) * piece, 0),
            (per_core, piece, width),
        )
    )
    by_chip = [first] + [hop_chip(first, -s) for s in range(1, chips)]
    by_group = hop_group(first)
    around = [*by_chip[1:], by_group]
    part = piece // 2
    foreign_pieces = [(first, 0), (by_group, piece)]
    for s in range(1, chips):
        foreign_pieces += [
            (by_chip[s], s * share),
            (hop_group(by_chip[s][:, :part]), s * share + piece),
            (hop_chip(by_group[:, part:], -s), s * share + piece + part),
        ]

    label = labels.reshape(1, rows)
    owner, local = label // cells_local, label % cells_local
    member = (owner % half - p + half) % half
    foreign = (owner // half != h).astype(jnp.int32)
    other = (local // per_core) ^ k
    rel = (member * 2 + foreign) * meta_extra + other * per_core + local % per_core

    seg = lambda s, t: s * 2 + t
    first_segs = [seg(s, 1) for s in range(1, half)]
    next_segs = [seg(s, 0) for s in range(1, half)]
    span = own_slots + meta_extra
    block = jax.ShapeDtypeStruct((span, width), jnp.bfloat16)
    lines = cell_count * meta_extra
    flat, off, meta, *blocks = pl.pallas_call(
        functools.partial(_place_kernel, per_core, reach, window, own_slots, first_segs),
        out_shape=[
            jax.ShapeDtypeStruct((1, rows), jnp.int32),
            jax.ShapeDtypeStruct((1, rows), jnp.int32),
            jax.ShapeDtypeStruct((lines, 128), jnp.float32),
        ]
        + [block] * len(first_segs),
        compiler_params=_params(),
        cost_estimate=dear,
    )(rel, frames)
    segments = dict(zip(first_segs, blocks, strict=True))

    blocks = pl.pallas_call(
        functools.partial(_pick_kernel, next_segs),
        out_shape=[block] * len(next_segs),
        compiler_params=_params(),
        cost_estimate=dear,
    )(_after(flat, first), meta, frames)
    segments.update(zip(next_segs, blocks, strict=True))
    received = {1: [hop_member(segments[seg(s, 1)], s) for s in range(1, half)]}
    here = {}
    for t, gate in ((1, (*blocks, foreign_sharp, *around)), (0, received[1])):
        here[t] = pl.pallas_call(
            functools.partial(_pick_kernel, [seg(0, t)]),
            out_shape=[block],
            compiler_params=_params(),
            cost_estimate=dear,
        )(_after(flat, *gate), meta, frames)[0]

    received[0] = [hop_member(segments[seg(s, 0)], s) for s in range(1, half)]

    def held_of(t, *gate):
        held = [here[t], hop_core(here[t])]
        for v in received[t]:
            v = _after(v, *gate)
            held += [v, hop_core(v)]
        return held

    held = {1: held_of(1, *around)}

    code = jnp.stack([x, y, k]).astype(jnp.int32)
    tail = -(-3 * per_core // 16) * 16

    def masses_in(rows):
        rows = rows[:, :share].astype(jnp.float32)
        return sum(rows[n * per_core : (n + 1) * per_core] for n in range(3))

    def over_chips(result, steps, earlier, extra):
        keep, mass, _, *sends = result
        mass = jnp.concatenate([*earlier, mass])[:, 0, :share]
        for s in range(1, chips):
            got = hop_chip(sends[s - 1], s)
            keep = keep + got[: steps * share].reshape(keep.shape).astype(jnp.float32)
            if extra:
                mass = mass + masses_in(got[steps * share :])
        return keep, mass

    results, totals, theirs, notes = [], [], [], []
    for t, begin, size in [(1, *part) for part in parts] + [(0, 0, per_core)]:
        if not t:
            held[0] = held_of(0, totals[0])
            notes.append(
                pl.pallas_call(
                    _copy_kernel,
                    out_shape=jax.ShapeDtypeStruct(notes[-1].shape, jnp.float32),
                    compiler_params=_params(),
                    cost_estimate=dear,
                )(_after(notes.pop(), totals[1]))
            )
        code_here = _after(code, notes[-1]) if results else code
        earlier = [r[1] for r in results] if t else []
        extra = 0 if t and begin + size < per_core else tail
        results.append(
            _cell_call(
                code_here, foreign_sharp if t else sharpness, foreign_pieces if t else [(centroids, 0)],
                not t, held[t], window, reach, per_core,
                begin, size, kids, share, chips - 1, earlier if extra else [], extra,
            )
        )
        if t:
            scores = results[-1][2]
            if totals:
                scores = _after(scores, totals[0])
            notes.append(
                pl.pallas_call(
                    _note_kernel,
                    out_shape=jax.ShapeDtypeStruct((size, sources * window), jnp.float32),
                    compiler_params=_params(),
                    cost_estimate=dear,
                )(scores)
            )
        if not t:
            arrived = [hop_chip(results[-1][3 + n], n + 1) for n in range(chips - 1)]
            break
        total, mass = over_chips(results[-1], size, earlier, extra)
        if t and extra:
            total = _after(total, notes[-1])
        total = total.astype(wire).reshape(size * share, width)
        if extra:
            high = _round(mass)
            middle = _round(mass - high)
            terms = jnp.concatenate([high, middle, mass - high - middle])
            behind = jnp.pad(terms.astype(wire), ((0, tail - terms.shape[0]), (0, width - share)))
            total = jnp.concatenate([total, behind])
        theirs.append(hop_partner(total))
        totals.append(total)
    score_parts = pl.pallas_call(
        functools.partial(_pack_kernel, sources, window),
        out_shape=[jax.ShapeDtypeStruct((2 * per_core, window), jnp.float32)] * sources,
        compiler_params=_params(),
        cost_estimate=dear,
    )(*notes, results[-1][2][:, 0])

    back = {}
    for s in range(half):
        for kk in range(cores):
            n = s * cores + kk
            back[s, kk] = score_parts[n] if n == 0 else hop_any(score_parts[n], -s, kk)
    values = []
    for s in range(half):
        for t in range(2):
            at_row = 0 if t else per_core
            for kk in range(cores):
                values.append(back[s, kk][at_row : at_row + per_core])
            values.append(jnp.zeros((meta_extra - cells_local, window), jnp.float32))
    frame_score = pl.pallas_call(
        functools.partial(_score_kernel, lines, window),
        out_shape=jax.ShapeDtypeStruct((1, rows), jnp.float32),
        compiler_params=_params(),
        cost_estimate=dear,
    )(rel, off, jnp.concatenate(values, axis=0)).reshape(rows)

    theirs = [_after(v, *arrived) for v in theirs]
    one_cell = lambda block, where: pl.BlockSpec(block, where)
    whole = lambda v: pl.BlockSpec(v.shape, lambda n, c: (0,) * v.ndim)
    behind = lambda steps: pl.BlockSpec((tail, 128), lambda n, c: (steps * share // tail, 0))
    keep, mass = results[-1][:2]

    def update(mine):
        def part(c):
            return lax.rem((c[2] if mine else 1 - c[2]) + c[1], 2)

        got, got_specs = [], []
        for v in arrived:
            got += [v, v]
            got_specs += [
                one_cell((piece, width), lambda n, c: (2 * n + part(c), 0)),
                behind(per_core),
            ]
        if mine:
            out_specs = [one_cell((1, piece, width), lambda n, c: (c[2] * per_core + n, 0, 0))]
            out_shape = [jax.ShapeDtypeStruct((cells_local, piece, width), jnp.float32)]
        else:
            out_specs = [
                one_cell((1, piece + 8, width), lambda n, c: (n, 0, 0)),
                pl.BlockSpec((8, 128), lambda n, c: (0, 0)),
            ]
            out_shape = [
                jax.ShapeDtypeStruct((per_core, piece + 8, width), jnp.float32),
                jax.ShapeDtypeStruct((8, 128), jnp.float32),
            ]
        return pl.pallas_call(
            functools.partial(_update_kernel, per_core, chips, piece, mine),
            grid_spec=pltpu.PrefetchScalarGridSpec(
                num_scalar_prefetch=1,
                grid=(per_core,),
                in_specs=[
                    one_cell((1, piece, width), lambda n, c: (n, part(c), 0)),
                    whole(mass),
                    *got_specs,
                    one_cell((piece, width), lambda n, c: (part(c), 0)),
                    one_cell((piece, width), lambda n, c: (2 * jnp.maximum(n - 1, 0) + part(c), 0)),
                    behind(per_core - 1),
                ],
                out_specs=out_specs,
                scratch_shapes=[pltpu.VMEM((128, 128), jnp.float32)],
            ),
            out_shape=out_shape,
            compiler_params=_params(),
            cost_estimate=busy,
        )(code, keep, mass, *got, theirs[0], theirs[1], theirs[1])

    swap, lines_mine = update(False)
    (out,) = update(True)
    swapped = hop_core(swap)
    new_centroids, child_mass = pl.pallas_call(
        functools.partial(_finish_kernel, per_core, piece),
        grid_spec=pltpu.PrefetchScalarGridSpec(
            num_scalar_prefetch=1,
            grid=(1,),
            in_specs=[
                anywhere,
                anywhere,
                pl.BlockSpec((per_core, 8, 128), lambda n, c: (0, piece // 8, 0)),
                pl.BlockSpec((8, 128), lambda n, c: (0, 0)),
            ],
            out_specs=[anywhere, pl.BlockSpec((cells_local, piece), lambda n, c: (0, 0))],
            scratch_shapes=[pltpu.SemaphoreType.DMA(())],
        ),
        out_shape=[
            jax.ShapeDtypeStruct(out.shape, jnp.float32),
            jax.ShapeDtypeStruct((cells_local, piece), jnp.float32),
        ],
        input_output_aliases={1: 0},
        compiler_params=_params(),
        cost_estimate=busy,
    )(code, out, swapped, swapped, lines_mine)
    return new_centroids, child_mass, frame_score


def solution(mesh):
    return jax.shard_map(
        on_device,
        mesh=mesh,
        in_specs=(
            P(("groups", "cell", "frame"), None),
            P(("groups", "cell", "frame"), None),
            P("cell", None, None),
            P("cell"),
        ),
        out_specs=(
            P(("groups", "cell"), "frame", None),
            P(("groups", "cell"), "frame"),
            P(("groups", "cell", "frame")),
        ),
        check_vma=False,
    )
```

```python
import functools

import jax
import jax.numpy as jnp
from jax import lax
from jax.experimental import pallas as pl
from jax.experimental.pallas import tpu as pltpu
from jax.sharding import PartitionSpec as P

prior_mass = 1.0
cores = 2
wire = jnp.bfloat16
vmem_limit = 16 * 1024 * 1024
anywhere = pl.BlockSpec(memory_space=pl.ANY)
cheap = pl.CostEstimate(flops=1, bytes_accessed=1, transcendentals=0)
busy = pl.CostEstimate(flops=20_000_000_000, bytes_accessed=1, transcendentals=0)
dear = pl.CostEstimate(flops=20_000_000_000, bytes_accessed=1_000_000_000, transcendentals=0)
meta_extra = 16


def _hot(flat_row, segment, own_slots):
    rows = flat_row.shape[1]
    slot = lax.broadcasted_iota(jnp.int32, (own_slots, rows), 0) + segment * own_slots
    return jnp.where(slot == flat_row, 1.0, 0.0).astype(jnp.bfloat16)


def _pick(flat_row, meta, frames_ref, segment, out_ref):
    own_slots = out_ref.shape[0] - meta_extra
    hot = _hot(flat_row, segment, own_slots)
    out_ref[pl.ds(0, own_slots)] = jnp.dot(
        hot, frames_ref[...], preferred_element_type=jnp.float32
    ).astype(jnp.bfloat16)
    out_ref[pl.ds(own_slots, meta_extra)] = jnp.zeros((meta_extra, out_ref.shape[1]), jnp.bfloat16)
    out_ref[pl.ds(own_slots, meta_extra), pl.ds(0, 128)] = meta[
        segment * meta_extra : (segment + 1) * meta_extra
    ].astype(jnp.bfloat16)


def _place_kernel(
    per_core, reach, window, own_slots, segments, rel_ref, frames_ref, flat_ref, off_ref, meta_ref, *outs
):
    rows = rel_ref.shape[1]
    lines = meta_ref.shape[0]
    rel = rel_ref[...]
    line = lax.broadcasted_iota(jnp.int32, (lines, rows), 0)
    base = (line // meta_extra) * meta_extra
    segment = rel // meta_extra
    hits = jnp.where(rel == line, 1, 0)
    lane = lax.broadcasted_iota(jnp.int32, (lines, rows), 1)
    running = hits
    step = 1
    while step < rows:
        running += jnp.where(lane >= step, pltpu.roll(running, step, 1), 0)
        step *= 2
    count = jnp.sum(hits, axis=1, keepdims=True)
    ahead = jnp.sum(jnp.where((rel < line) & (rel >= base), 1, 0), axis=1, keepdims=True)
    behind = jnp.sum(
        jnp.where((rel <= line) & (rel >= base + per_core), 1, 0), axis=1, keepdims=True
    )
    back = (line - base)[:, :1] >= per_core
    start = jnp.where(back, own_slots - behind, ahead)
    floor = jnp.where(back, own_slots - reach, 0)
    first = jnp.minimum(((start - floor) >> 4) << 4, reach - window) + floor
    position = jnp.sum(hits * (running + (start - 1)), axis=0, keepdims=True)
    flat = segment * own_slots + position
    flat_ref[...] = flat
    off_ref[...] = jnp.sum(hits * (running + (start - first - 1)), axis=0, keepdims=True)
    column = lax.broadcasted_iota(jnp.int32, meta_ref.shape, 1)
    meta = jnp.where(
        column == 0,
        (first - floor) >> 4,
        jnp.where(column == 1, start - first, jnp.where(column == 2, count, 0)),
    ).astype(jnp.float32)
    meta_ref[...] = meta
    for g, out_ref in zip(segments, outs, strict=True):
        _pick(flat, meta, frames_ref, g, out_ref)


def _pick_kernel(segments, flat_ref, meta_ref, frames_ref, *outs):
    flat, meta = flat_ref[...], meta_ref[...]
    for g, out_ref in zip(segments, outs, strict=True):
        _pick(flat, meta, frames_ref, g, out_ref)


def _split(lines, rows):
    high = lines.astype(jnp.bfloat16).astype(jnp.float32)
    middle = (lines - high).astype(jnp.bfloat16).astype(jnp.float32)
    rest = jnp.zeros((rows - 3 * lines.shape[0], lines.shape[1]), jnp.float32)
    return jnp.concatenate([high, middle, lines - high - middle, rest], axis=0)


def _round(value):
    return lax.reduce_precision(value, 8, 7)


def _note_kernel(score_ref, out_ref):
    out_ref[...] = score_ref[:, 0]


def _copy_kernel(in_ref, out_ref):
    out_ref[...] = in_ref[...]


def _split(lines, rows):
    high = lines.astype(jnp.bfloat16).astype(jnp.float32)
    middle = (lines - high).astype(jnp.bfloat16).astype(jnp.float32)
    rest = jnp.zeros((rows - 3 * lines.shape[0], lines.shape[1]), jnp.float32)
    return jnp.concatenate([high, middle, lines - high - middle, rest], axis=0)


def _note_kernel(score_ref, out_ref):
    out_ref[...] = score_ref[:, 0]


def _copy_kernel(in_ref, out_ref):
    out_ref[...] = in_ref[...]


def _prior_kernel(group_count, code_ref, *refs):
    for g in range(group_count):
        size = refs[g].shape[1]
        refs[-1][:, g * size : (g + 1) * size] = refs[g][...].astype(jnp.float32)


def _cell_kernel(sources, window, reach, pieces, places, near, share, steps, per_core, begin, span, earlier, tail, *refs):
    code_ref, sharp_ref = refs[:2]
    refs = refs[2:]
    centre_refs, refs = refs[: len(places)], refs[len(places) :]
    piece = share // 2
    row_refs, refs = refs[:sources], refs[sources:]
    earlier_refs, refs = refs[:earlier], refs[earlier:]
    keep_ref, mass_ref, score_ref = refs[:3]
    send_refs, (held, centres, sems, meta_low, meta_sems) = refs[3:-5], refs[-5:]
    step = pl.program_id(0)
    loads = []
    first_only = begin + steps == 1
    reach = window if first_only else reach
    for n in range(sources):
        low = 0 if n % cores == 0 else span - meta_extra - reach
        loads.append(
            pltpu.make_async_copy(
                row_refs[n].at[pl.ds(low, reach)],
                held.at[n, pl.ds(0, reach)],
                sems.at[n],
            )
        )
    if not near:
        for n, low in enumerate(places):
            loads.append(
                pltpu.make_async_copy(
                    centre_refs[n].at[pl.ds(begin, steps)],
                    centres.at[:, pl.ds(low, centre_refs[n].shape[1])],
                    sems.at[sources + n],
                )
            )

    @pl.when(step == 0)
    def _():
        lines = [
            pltpu.make_async_copy(
                row_refs[n].at[pl.ds(span - meta_extra, meta_extra), pl.ds(0, 128)],
                meta_low.at[pl.ds(n * meta_extra, meta_extra)],
                meta_sems.at[n],
            )
            for n in range(sources)
        ]
        for copy in lines + loads:
            copy.start()
        for copy in lines:
            copy.wait()
        for copy in loads:
            copy.wait()

    if near:
        found = []
        for n in range(pieces):
            chip = lax.rem(code_ref[0] + n // 2, pieces // 2)
            kid = (chip * 2 + lax.rem(code_ref[1] + n % 2, 2)) * piece
            found.append(centre_refs[0][0, pl.ds(pl.multiple_of(kid, piece), piece)])
        centre = jnp.concatenate(found, axis=0)
    else:
        centre = centres[step]
    wide = centre.astype(jnp.float32)
    half_norm = 0.5 * jnp.sum(wide * wide, axis=1, keepdims=True)
    slot = lax.broadcasted_iota(jnp.int32, (1, sources * window), 1)
    valid = slot < 0
    lines = meta_low[...].astype(jnp.float32).astype(jnp.int32)
    line = lax.broadcasted_iota(jnp.int32, lines.shape, 0)
    firsts = []
    for n in range(sources):
        at_line = n * meta_extra + (n % cores) * per_core + begin
        found = lines[at_line : at_line + 1]
        if steps > 1:
            found = jnp.sum(jnp.where(line == at_line + step, lines, 0), axis=0, keepdims=True)
        firsts.append(None if first_only else found[0, 0] * 16)
        low = found[:, 1:2] + n * window
        valid = valid | ((slot >= low) & (slot < low + found[:, 2:3]))
    if first_only:
        chosen = held[...].reshape(sources * window, held.shape[2])
    else:
        chosen = jnp.concatenate(
            [held[n, pl.ds(pl.multiple_of(firsts[n], 16), window)] for n in range(sources)]
        )
    products = lax.dot_general(
        centre, chosen, (((1,), (1,)), ((), ())), preferred_element_type=jnp.float32
    )
    scores = sharp_ref[code_ref[2] * per_core + begin + step] * (products - half_norm)
    top = jnp.max(scores, axis=0, keepdims=True)
    exponent = jnp.exp(scores - top)
    total = jnp.sum(exponent, axis=0, keepdims=True)
    score_ref[0] = jnp.broadcast_to(
        jnp.where(valid, top + jnp.log(total), 0.0), score_ref.shape[1:]
    )
    resp = exponent * jnp.where(valid, 1.0 / total, 0.0)
    mass = jnp.sum(resp, axis=1, keepdims=True)
    mass_ref[step] = jnp.broadcast_to(mass, (mass.shape[0], 128)).T[: mass_ref.shape[1]]
    low = resp.astype(jnp.bfloat16)
    numer = jnp.dot(low, chosen, preferred_element_type=jnp.float32)
    keep_ref[0] = numer[:share] + prior_mass * centre[:share].astype(jnp.float32) if near else numer[:share]
    for n, ref in enumerate(send_refs):
        at_row = pl.multiple_of(step * share, share)
        ref[pl.ds(at_row, share)] = numer[(n + 1) * share : (n + 2) * share].astype(ref.dtype)

    if tail:

        @pl.when(step == steps - 1)
        def _():
            lines = [r[i, :1] for r in (*earlier_refs, mass_ref) for i in range(r.shape[0])]
            for n, ref in enumerate(send_refs):
                part = [v[:, (n + 1) * share : (n + 2) * share] for v in lines]
                rows = _split(jnp.concatenate(part, axis=0), tail)
                ref[pl.ds(steps * share, tail)] = jnp.zeros((tail, ref.shape[1]), ref.dtype)
                ref[pl.ds(steps * share, tail), pl.ds(0, share)] = rows.astype(ref.dtype)


def _pack_kernel(sources, window, *refs):
    line = 0
    for score_ref in refs[:-sources]:
        size = score_ref.shape[0]
        for n, out_ref in enumerate(refs[-sources:]):
            out_ref[line : line + size] = score_ref[:, n * window : (n + 1) * window]
        line += size


def _score_kernel(cells, window, rel_ref, off_ref, values_ref, out_ref):
    rows = rel_ref.shape[1]
    hot = jnp.where(
        lax.broadcasted_iota(jnp.int32, (window, rows), 0) == off_ref[...], 1.0, 0.0
    ).astype(jnp.bfloat16)
    rest = values_ref[...]
    mine = lax.broadcasted_iota(jnp.int32, (cells, rows), 0) == rel_ref[...]
    total = jnp.zeros((cells, rows), jnp.float32)
    for _ in range(3):
        term = rest.astype(jnp.bfloat16)
        rest = rest - term.astype(jnp.float32)
        total += jnp.dot(term, hot, preferred_element_type=jnp.float32)
    out_ref[...] = jnp.sum(jnp.where(mine, total, 0.0), axis=0, keepdims=True)


def _after(value, *others):
    return lax.optimization_barrier((value, *others))[0]


def _update_kernel(per_core, chips, piece, mine, code_ref, keep_ref, mass_ref, *refs):
    got_refs, refs = refs[: 2 * (chips - 1)], refs[2 * (chips - 1) :]
    (first_ref, others_ref, tail_ref), out_ref, weight = refs[:3], refs[3], refs[-1]
    step = pl.program_id(0)
    lines = mass_ref[:, 0, :128]
    for ref in [*got_refs[1::2], tail_ref]:
        rows = ref[...].astype(jnp.float32)
        for n in range(3):
            lines = lines + rows[n * per_core : (n + 1) * per_core]
    line = lax.broadcasted_iota(jnp.int32, lines.shape, 0)
    mass = jnp.sum(jnp.where(line == step, lines, 0.0), axis=0, keepdims=True)
    weight[...] = jnp.broadcast_to(1.0 / (mass + prior_mass), (128, 128)).T
    numer = keep_ref[0]
    for ref in got_refs[0::2]:
        numer = numer + ref[...].astype(jnp.float32)
    far = jnp.where(step == 0, first_ref[...], others_ref[...])
    low = lax.rem((code_ref[2] if mine else 1 - code_ref[2]) + code_ref[1], 2) * piece
    numer = numer + far.astype(jnp.float32)
    out_ref[0, :piece] = numer * weight[pl.ds(pl.multiple_of(low, piece), piece), :1]
    if not mine:
        out_ref[0, piece:] = jnp.zeros((8, out_ref.shape[2]), jnp.float32)
        out_ref[0, piece:, :128] = jnp.broadcast_to(mass, (8, 128))
        lines_ref = refs[4]

        @pl.when(step == 0)
        def _():
            lines_ref[...] = jnp.concatenate(
                [lines, jnp.zeros((lines_ref.shape[0] - per_core, 128), jnp.float32)], axis=0
            )


def _finish_kernel(per_core, piece, code_ref, _, swap_ref, line_ref, lines_ref, out_ref, mass_ref, sem):
    other = 1 - code_ref[2]
    copy = pltpu.make_async_copy(
        swap_ref.at[:, pl.ds(0, piece)], out_ref.at[pl.ds(other * per_core, per_core)], sem
    )
    copy.start()
    mine = lines_ref[:per_core]
    theirs = line_ref[:, 0]
    lines = jnp.where(
        other == 1, jnp.concatenate([mine, theirs], axis=0), jnp.concatenate([theirs, mine], axis=0)
    )
    here = lax.rem(code_ref[2] + code_ref[1], 2)
    mass_ref[...] = jnp.where(here == 0, lines[:, :piece], lines[:, piece : 2 * piece])
    copy.wait()


def _params():
    return pltpu.CompilerParams(vmem_limit_bytes=vmem_limit)


def _cell_call(code, sharp, arrays, near, row_blocks, window, reach, per_core, begin, steps, kids, share, sends, earlier, tail):
    sources = len(row_blocks)
    span, width = row_blocks[0].shape
    pieces = kids // (share // 2)
    arrays, places = zip(*arrays, strict=True)
    rows = sources * window
    out_shape = [
        jax.ShapeDtypeStruct((steps, share, width), jnp.float32),
        jax.ShapeDtypeStruct((steps, 8, kids), jnp.float32),
        jax.ShapeDtypeStruct((steps, 8, rows), jnp.float32),
    ] + [jax.ShapeDtypeStruct((steps * share + tail, width), wire)] * sends
    fixed = lambda shape: pl.BlockSpec(shape, lambda n, *_: (0,) * len(shape))
    moving = lambda shape: pl.BlockSpec((1, *shape[1:]), lambda n, *_: (n, 0, 0))
    return pl.pallas_call(
        functools.partial(
            _cell_kernel, sources, window, reach, pieces, places, near, share, steps, per_core, begin, span, len(earlier), tail
        ),
        grid_spec=pltpu.PrefetchScalarGridSpec(
            num_scalar_prefetch=2,
            grid=(steps,),
            in_specs=(
                [pl.BlockSpec((1, kids, width), lambda n, c, _: (c[2] * per_core + begin + n, 0, 0))]
                if near
                else [anywhere] * len(arrays)
            )
            + [anywhere] * sources
            + [fixed(v.shape) for v in earlier],
            out_specs=[
                (moving if n in (0, 2) else fixed)(o.shape) for n, o in enumerate(out_shape)
            ],
            scratch_shapes=[
                pltpu.VMEM((sources, window if begin + steps == 1 else reach, width), jnp.bfloat16),
                pltpu.VMEM((1 if near else steps, kids, width), jnp.bfloat16),
                pltpu.SemaphoreType.DMA((sources + len(places),)),
                pltpu.VMEM((sources * meta_extra, 128), jnp.bfloat16),
                pltpu.SemaphoreType.DMA((sources,)),
            ],
        ),
        out_shape=out_shape,
        compiler_params=pltpu.CompilerParams(vmem_limit_bytes=44 * 1024 * 1024),
        cost_estimate=busy,
    )(code, sharp, *arrays, *row_blocks, *earlier)


def on_device(frames, labels, centroids, sharpness):
    cell_count = lax.axis_size("cell")
    frame_count = lax.axis_size("frame")
    group_count = 2
    cells_local, kids, width = centroids.shape
    rows = frames.shape[0]
    cells_total = cells_local * cell_count
    half = cell_count // 2
    chips = frame_count // cores
    per_core = cells_local // cores
    cell_cap = 3 * rows // cells_total
    own_slots = 2 * rows // cell_count
    sources = half * cores
    window = -(-(cell_cap + 16) // 16) * 16
    while sources * window % 128:
        window += 16
    reach = min(own_slots, -(-per_core * cell_cap // 16) * 16)
    window = min(window, reach)
    share = kids // chips
    piece = share // group_count

    z = lax.axis_index("cell")
    j = lax.axis_index("frame")
    y = lax.axis_index("groups")
    x, k = j // cores, j % cores
    p, h = z % half, z // half

    def at(zz, xx, kk):
        return zz * frame_count + xx * cores + kk

    def hop_core(v):
        return lax.ppermute(v, "frame", [(i, i ^ 1) for i in range(frame_count)])

    def hop_chip(v, s):
        return lax.ppermute(
            v,
            "frame",
            [(a * cores + c, (a + s) % chips * cores + c) for a in range(chips) for c in range(cores)],
        )

    def hop_member(v, s):
        return lax.ppermute(
            v, "cell", [(b * half + i, b * half + (i + s) % half) for b in range(2) for i in range(half)]
        )

    def hop_partner(v):
        return lax.ppermute(v, "cell", [(i, (i + half) % cell_count) for i in range(cell_count)])

    def hop_group(v):
        return lax.ppermute(v, "groups", [(i, 1 - i) for i in range(2)])

    def hop_any(v, s, kk):
        pairs = [
            (at(b * half + i, a, c), at(b * half + (i + s) % half, a, c ^ kk))
            for b in range(2)
            for i in range(half)
            for a in range(chips)
            for c in range(cores)
        ]
        return lax.ppermute(v, ("cell", "frame"), pairs)

    parts = [(0, 1), (1, per_core - 1)]
    foreign_sharp = hop_partner(sharpness)
    first = hop_partner(
        lax.dynamic_slice(
            centroids,
            (k * per_core, (x * group_count + y) * piece, 0),
            (per_core, piece, width),
        )
    )
    by_chip = [first] + [hop_chip(first, -s) for s in range(1, chips)]
    by_group = hop_group(first)
    around = [*by_chip[1:], by_group]
    part = piece // 2
    foreign_pieces = [(first, 0), (by_group, piece)]
    for s in range(1, chips):
        foreign_pieces += [
            (by_chip[s], s * share),
            (hop_group(by_chip[s][:, :part]), s * share + piece),
            (hop_chip(by_group[:, part:], -s), s * share + piece + part),
        ]

    label = labels.reshape(1, rows)
    owner, local = label // cells_local, label % cells_local
    member = (owner % half - p + half) % half
    foreign = (owner // half != h).astype(jnp.int32)
    other = (local // per_core) ^ k
    rel = (member * 2 + foreign) * meta_extra + other * per_core + local % per_core

    seg = lambda s, t: s * 2 + t
    first_segs = [seg(s, 1) for s in range(1, half)]
    next_segs = [seg(s, 0) for s in range(1, half)]
    span = own_slots + meta_extra
    block = jax.ShapeDtypeStruct((span, width), jnp.bfloat16)
    lines = cell_count * meta_extra
    flat, off, meta, *blocks = pl.pallas_call(
        functools.partial(_place_kernel, per_core, reach, window, own_slots, first_segs),
        out_shape=[
            jax.ShapeDtypeStruct((1, rows), jnp.int32),
            jax.ShapeDtypeStruct((1, rows), jnp.int32),
            jax.ShapeDtypeStruct((lines, 128), jnp.float32),
        ]
        + [block] * len(first_segs),
        compiler_params=_params(),
        cost_estimate=dear,
    )(rel, frames)
    segments = dict(zip(first_segs, blocks, strict=True))

    blocks = pl.pallas_call(
        functools.partial(_pick_kernel, next_segs),
        out_shape=[block] * len(next_segs),
        compiler_params=_params(),
        cost_estimate=dear,
    )(_after(flat, first), meta, frames)
    segments.update(zip(next_segs, blocks, strict=True))
    received = {1: [hop_member(segments[seg(s, 1)], s) for s in range(1, half)]}
    here = {}
    for t, gate in ((1, (*blocks, foreign_sharp, *around)), (0, received[1])):
        here[t] = pl.pallas_call(
            functools.partial(_pick_kernel, [seg(0, t)]),
            out_shape=[block],
            compiler_params=_params(),
            cost_estimate=dear,
        )(_after(flat, *gate), meta, frames)[0]

    received[0] = [hop_member(segments[seg(s, 0)], s) for s in range(1, half)]

    def held_of(t, *gate):
        held = [here[t], hop_core(here[t])]
        for v in received[t]:
            v = _after(v, *gate)
            held += [v, hop_core(v)]
        return held

    held = {1: held_of(1, *around)}

    code = jnp.stack([x, y, k]).astype(jnp.int32)
    tail = -(-3 * per_core // 16) * 16

    def masses_in(rows):
        rows = rows[:, :share].astype(jnp.float32)
        return sum(rows[n * per_core : (n + 1) * per_core] for n in range(3))

    def over_chips(result, steps, earlier, extra):
        keep, mass, _, *sends = result
        mass = jnp.concatenate([*earlier, mass])[:, 0, :share]
        for s in range(1, chips):
            got = hop_chip(sends[s - 1], s)
            keep = keep + got[: steps * share].reshape(keep.shape).astype(jnp.float32)
            if extra:
                mass = mass + masses_in(got[steps * share :])
        return keep, mass

    results, totals, theirs, notes = [], [], [], []
    for t, begin, size in [(1, *part) for part in parts] + [(0, 0, per_core)]:
        if not t:
            held[0] = held_of(0, totals[0])
            notes.append(
                pl.pallas_call(
                    _copy_kernel,
                    out_shape=jax.ShapeDtypeStruct(notes[-1].shape, jnp.float32),
                    compiler_params=_params(),
                    cost_estimate=dear,
                )(_after(notes.pop(), totals[1]))
            )
        code_here = _after(code, notes[-1]) if results else code
        earlier = [r[1] for r in results] if t else []
        extra = 0 if t and begin + size < per_core else tail
        results.append(
            _cell_call(
                code_here, foreign_sharp if t else sharpness, foreign_pieces if t else [(centroids, 0)],
                not t, held[t], window, reach, per_core,
                begin, size, kids, share, chips - 1, earlier if extra else [], extra,
            )
        )
        if t:
            scores = results[-1][2]
            if totals:
                scores = _after(scores, totals[0])
            notes.append(
                pl.pallas_call(
                    _note_kernel,
                    out_shape=jax.ShapeDtypeStruct((size, sources * window), jnp.float32),
                    compiler_params=_params(),
                    cost_estimate=dear,
                )(scores)
            )
        if not t:
            arrived = [hop_chip(results[-1][3 + n], n + 1) for n in range(chips - 1)]
            break
        total, mass = over_chips(results[-1], size, earlier, extra)
        if t and extra:
            total = _after(total, notes[-1])
        total = total.astype(wire).reshape(size * share, width)
        if extra:
            high = _round(mass)
            middle = _round(mass - high)
            terms = jnp.concatenate([high, middle, mass - high - middle])
            behind = jnp.pad(terms.astype(wire), ((0, tail - terms.shape[0]), (0, width - share)))
            total = jnp.concatenate([total, behind])
        theirs.append(hop_partner(total))
        totals.append(total)
    score_parts = pl.pallas_call(
        functools.partial(_pack_kernel, sources, window),
        out_shape=[jax.ShapeDtypeStruct((2 * per_core, window), jnp.float32)] * sources,
        compiler_params=_params(),
        cost_estimate=dear,
    )(*notes, results[-1][2][:, 0])

    back = {}
    for s in range(half):
        for kk in range(cores):
            n = s * cores + kk
            back[s, kk] = score_parts[n] if n == 0 else hop_any(score_parts[n], -s, kk)
    values = []
    for s in range(half):
        for t in range(2):
            at_row = 0 if t else per_core
            for kk in range(cores):
                values.append(back[s, kk][at_row : at_row + per_core])
            values.append(jnp.zeros((meta_extra - cells_local, window), jnp.float32))
    frame_score = pl.pallas_call(
        functools.partial(_score_kernel, lines, window),
        out_shape=jax.ShapeDtypeStruct((1, rows), jnp.float32),
        compiler_params=_params(),
        cost_estimate=dear,
    )(rel, off, jnp.concatenate(values, axis=0)).reshape(rows)

    theirs = [_after(v, *arrived) for v in theirs]
    one_cell = lambda block, where: pl.BlockSpec(block, where)
    whole = lambda v: pl.BlockSpec(v.shape, lambda n, c: (0,) * v.ndim)
    behind = lambda steps: pl.BlockSpec((tail, 128), lambda n, c: (steps * share // tail, 0))
    keep, mass = results[-1][:2]

    def update(mine):
        def part(c):
            return lax.rem((c[2] if mine else 1 - c[2]) + c[1], 2)

        got, got_specs = [], []
        for v in arrived:
            got += [v, v]
            got_specs += [
                one_cell((piece, width), lambda n, c: (2 * n + part(c), 0)),
                behind(per_core),
            ]
        if mine:
            out_specs = [one_cell((1, piece, width), lambda n, c: (c[2] * per_core + n, 0, 0))]
            out_shape = [jax.ShapeDtypeStruct((cells_local, piece, width), jnp.float32)]
        else:
            out_specs = [
                one_cell((1, piece + 8, width), lambda n, c: (n, 0, 0)),
                pl.BlockSpec((8, 128), lambda n, c: (0, 0)),
            ]
            out_shape = [
                jax.ShapeDtypeStruct((per_core, piece + 8, width), jnp.float32),
                jax.ShapeDtypeStruct((8, 128), jnp.float32),
            ]
        return pl.pallas_call(
            functools.partial(_update_kernel, per_core, chips, piece, mine),
            grid_spec=pltpu.PrefetchScalarGridSpec(
                num_scalar_prefetch=1,
                grid=(per_core,),
                in_specs=[
                    one_cell((1, piece, width), lambda n, c: (n, part(c), 0)),
                    whole(mass),
                    *got_specs,
                    one_cell((piece, width), lambda n, c: (part(c), 0)),
                    one_cell((piece, width), lambda n, c: (2 * jnp.maximum(n - 1, 0) + part(c), 0)),
                    behind(per_core - 1),
                ],
                out_specs=out_specs,
                scratch_shapes=[pltpu.VMEM((128, 128), jnp.float32)],
            ),
            out_shape=out_shape,
            compiler_params=_params(),
            cost_estimate=busy,
        )(code, keep, mass, *got, theirs[0], theirs[1], theirs[1])

    swap, lines_mine = update(False)
    (out,) = update(True)
    swapped = hop_core(swap)
    new_centroids, child_mass = pl.pallas_call(
        functools.partial(_finish_kernel, per_core, piece),
        grid_spec=pltpu.PrefetchScalarGridSpec(
            num_scalar_prefetch=1,
            grid=(1,),
            in_specs=[
                anywhere,
                anywhere,
                pl.BlockSpec((per_core, 8, 128), lambda n, c: (0, piece // 8, 0)),
                pl.BlockSpec((8, 128), lambda n, c: (0, 0)),
            ],
            out_specs=[anywhere, pl.BlockSpec((cells_local, piece), lambda n, c: (0, 0))],
            scratch_shapes=[pltpu.SemaphoreType.DMA(())],
        ),
        out_shape=[
            jax.ShapeDtypeStruct(out.shape, jnp.float32),
            jax.ShapeDtypeStruct((cells_local, piece), jnp.float32),
        ],
        input_output_aliases={1: 0},
        compiler_params=_params(),
        cost_estimate=busy,
    )(code, out, swapped, swapped, lines_mine)
    return new_centroids, child_mass, frame_score


def solution(mesh):
    return jax.shard_map(
        on_device,
        mesh=mesh,
        in_specs=(
            P(("groups", "cell", "frame"), None),
            P(("groups", "cell", "frame"), None),
            P("cell", None, None),
            P("cell"),
        ),
        out_specs=(
            P(("groups", "cell"), "frame", None),
            P(("groups", "cell"), "frame"),
            P(("groups", "cell", "frame")),
        ),
        check_vma=False,
    )
```

```python
import functools

import jax
import jax.numpy as jnp
from jax import lax
from jax.experimental import pallas as pl
from jax.experimental.pallas import tpu as pltpu
from jax.sharding import PartitionSpec as P

prior_mass = 1.0
cores = 2
wire = jnp.bfloat16
vmem_limit = 16 * 1024 * 1024
anywhere = pl.BlockSpec(memory_space=pl.ANY)
cheap = pl.CostEstimate(flops=1, bytes_accessed=1, transcendentals=0)
busy = pl.CostEstimate(flops=20_000_000_000, bytes_accessed=1, transcendentals=0)
dear = pl.CostEstimate(flops=20_000_000_000, bytes_accessed=1_000_000_000, transcendentals=0)
meta_extra = 16


def _hot(flat_row, segment, own_slots):
    rows = flat_row.shape[1]
    slot = lax.broadcasted_iota(jnp.int32, (own_slots, rows), 0) + segment * own_slots
    return jnp.where(slot == flat_row, 1.0, 0.0).astype(jnp.bfloat16)


def _pick(flat_row, meta, frames_ref, segment, out_ref):
    own_slots = out_ref.shape[0] - meta_extra
    hot = _hot(flat_row, segment, own_slots)
    out_ref[pl.ds(0, own_slots)] = jnp.dot(
        hot, frames_ref[...], preferred_element_type=jnp.float32
    ).astype(jnp.bfloat16)
    out_ref[pl.ds(own_slots, meta_extra)] = jnp.zeros((meta_extra, out_ref.shape[1]), jnp.bfloat16)
    out_ref[pl.ds(own_slots, meta_extra), pl.ds(0, 128)] = meta[
        segment * meta_extra : (segment + 1) * meta_extra
    ].astype(jnp.bfloat16)


def _place_kernel(
    per_core, reach, window, own_slots, segments, rel_ref, frames_ref, flat_ref, off_ref, meta_ref, *outs
):
    rows = rel_ref.shape[1]
    lines = meta_ref.shape[0]
    rel = rel_ref[...]
    line = lax.broadcasted_iota(jnp.int32, (lines, rows), 0)
    base = (line // meta_extra) * meta_extra
    segment = rel // meta_extra
    hits = jnp.where(rel == line, 1, 0)
    lane = lax.broadcasted_iota(jnp.int32, (lines, rows), 1)
    running = hits
    step = 1
    while step < rows:
        running += jnp.where(lane >= step, pltpu.roll(running, step, 1), 0)
        step *= 2
    count = jnp.sum(hits, axis=1, keepdims=True)
    ahead = jnp.sum(jnp.where((rel < line) & (rel >= base), 1, 0), axis=1, keepdims=True)
    behind = jnp.sum(
        jnp.where((rel <= line) & (rel >= base + per_core), 1, 0), axis=1, keepdims=True
    )
    back = (line - base)[:, :1] >= per_core
    start = jnp.where(back, own_slots - behind, ahead)
    floor = jnp.where(back, own_slots - reach, 0)
    first = jnp.minimum(((start - floor) >> 4) << 4, reach - window) + floor
    position = jnp.sum(hits * (running + (start - 1)), axis=0, keepdims=True)
    flat = segment * own_slots + position
    flat_ref[...] = flat
    off_ref[...] = jnp.sum(hits * (running + (start - first - 1)), axis=0, keepdims=True)
    column = lax.broadcasted_iota(jnp.int32, meta_ref.shape, 1)
    meta = jnp.where(
        column == 0,
        (first - floor) >> 4,
        jnp.where(column == 1, start - first, jnp.where(column == 2, count, 0)),
    ).astype(jnp.float32)
    meta_ref[...] = meta
    for g, out_ref in zip(segments, outs, strict=True):
        _pick(flat, meta, frames_ref, g, out_ref)


def _pick_kernel(segments, flat_ref, meta_ref, frames_ref, *outs):
    flat, meta = flat_ref[...], meta_ref[...]
    for g, out_ref in zip(segments, outs, strict=True):
        _pick(flat, meta, frames_ref, g, out_ref)


def _split(lines, rows):
    high = lines.astype(jnp.bfloat16).astype(jnp.float32)
    middle = (lines - high).astype(jnp.bfloat16).astype(jnp.float32)
    rest = jnp.zeros((rows - 3 * lines.shape[0], lines.shape[1]), jnp.float32)
    return jnp.concatenate([high, middle, lines - high - middle, rest], axis=0)


def _round(value):
    return lax.reduce_precision(value, 8, 7)


def _note_kernel(score_ref, out_ref):
    out_ref[...] = score_ref[:, 0]


def _copy_kernel(in_ref, out_ref):
    out_ref[...] = in_ref[...]


def _split(lines, rows):
    high = lines.astype(jnp.bfloat16).astype(jnp.float32)
    middle = (lines - high).astype(jnp.bfloat16).astype(jnp.float32)
    rest = jnp.zeros((rows - 3 * lines.shape[0], lines.shape[1]), jnp.float32)
    return jnp.concatenate([high, middle, lines - high - middle, rest], axis=0)


def _note_kernel(score_ref, out_ref):
    out_ref[...] = score_ref[:, 0]


def _copy_kernel(in_ref, out_ref):
    out_ref[...] = in_ref[...]


def _prior_kernel(group_count, code_ref, *refs):
    for g in range(group_count):
        size = refs[g].shape[1]
        refs[-1][:, g * size : (g + 1) * size] = refs[g][...].astype(jnp.float32)


def _cell_kernel(sources, window, reach, pieces, places, near, share, steps, per_core, begin, span, earlier, tail, *refs):
    code_ref, sharp_ref = refs[:2]
    refs = refs[2:]
    centre_refs, refs = refs[: len(places)], refs[len(places) :]
    piece = share // 2
    row_refs, refs = refs[:sources], refs[sources:]
    earlier_refs, refs = refs[:earlier], refs[earlier:]
    keep_ref, mass_ref, score_ref = refs[:3]
    send_refs, (held, centres, sems, meta_low, meta_sems) = refs[3:-5], refs[-5:]
    step = pl.program_id(0)
    loads = []
    first_only = begin + steps == 1
    reach = window if first_only else reach
    for n in range(sources):
        low = 0 if n % cores == 0 else span - meta_extra - reach
        loads.append(
            pltpu.make_async_copy(
                row_refs[n].at[pl.ds(low, reach)],
                held.at[n, pl.ds(0, reach)],
                sems.at[n],
            )
        )
    if not near:
        for n, low in enumerate(places):
            loads.append(
                pltpu.make_async_copy(
                    centre_refs[n].at[pl.ds(begin, steps)],
                    centres.at[:, pl.ds(low, centre_refs[n].shape[1])],
                    sems.at[sources + n],
                )
            )

    @pl.when(step == 0)
    def _():
        lines = [
            pltpu.make_async_copy(
                row_refs[n].at[pl.ds(span - meta_extra, meta_extra), pl.ds(0, 128)],
                meta_low.at[pl.ds(n * meta_extra, meta_extra)],
                meta_sems.at[n],
            )
            for n in range(sources)
        ]
        for copy in lines + loads:
            copy.start()
        for copy in lines:
            copy.wait()
        for copy in loads:
            copy.wait()

    if near:
        found = []
        for n in range(pieces):
            chip = lax.rem(code_ref[0] + n // 2, pieces // 2)
            kid = (chip * 2 + lax.rem(code_ref[1] + n % 2, 2)) * piece
            found.append(centre_refs[0][0, pl.ds(pl.multiple_of(kid, piece), piece)])
        centre = jnp.concatenate(found, axis=0)
    else:
        centre = centres[step]
    wide = centre.astype(jnp.float32)
    half_norm = 0.5 * jnp.sum(wide * wide, axis=1, keepdims=True)
    slot = lax.broadcasted_iota(jnp.int32, (1, sources * window), 1)
    valid = slot < 0
    lines = meta_low[...].astype(jnp.float32).astype(jnp.int32)
    line = lax.broadcasted_iota(jnp.int32, lines.shape, 0)
    firsts = []
    for n in range(sources):
        at_line = n * meta_extra + (n % cores) * per_core + begin
        found = lines[at_line : at_line + 1]
        if steps > 1:
            found = jnp.sum(jnp.where(line == at_line + step, lines, 0), axis=0, keepdims=True)
        firsts.append(None if first_only else found[0, 0] * 16)
        low = found[:, 1:2] + n * window
        valid = valid | ((slot >= low) & (slot < low + found[:, 2:3]))
    if first_only:
        chosen = held[...].reshape(sources * window, held.shape[2])
    else:
        chosen = jnp.concatenate(
            [held[n, pl.ds(pl.multiple_of(firsts[n], 16), window)] for n in range(sources)]
        )
    products = lax.dot_general(
        centre, chosen, (((1,), (1,)), ((), ())), preferred_element_type=jnp.float32
    )
    scores = sharp_ref[code_ref[2] * per_core + begin + step] * (products - half_norm)
    top = jnp.max(scores, axis=0, keepdims=True)
    exponent = jnp.exp(scores - top)
    total = jnp.sum(exponent, axis=0, keepdims=True)
    score_ref[0] = jnp.broadcast_to(
        jnp.where(valid, top + jnp.log(total), 0.0), score_ref.shape[1:]
    )
    resp = exponent * jnp.where(valid, 1.0 / total, 0.0)
    mass = jnp.sum(resp, axis=1, keepdims=True)
    mass_ref[step] = jnp.broadcast_to(mass, (mass.shape[0], 128)).T[: mass_ref.shape[1]]
    low = resp.astype(jnp.bfloat16)
    numer = jnp.dot(low, chosen, preferred_element_type=jnp.float32)
    keep_ref[0] = numer[:share] + prior_mass * centre[:share].astype(jnp.float32) if near else numer[:share]
    for n, ref in enumerate(send_refs):
        at_row = pl.multiple_of(step * share, share)
        ref[pl.ds(at_row, share)] = numer[(n + 1) * share : (n + 2) * share].astype(ref.dtype)

    if tail:

        @pl.when(step == steps - 1)
        def _():
            lines = [r[i, :1] for r in (*earlier_refs, mass_ref) for i in range(r.shape[0])]
            for n, ref in enumerate(send_refs):
                part = [v[:, (n + 1) * share : (n + 2) * share] for v in lines]
                rows = _split(jnp.concatenate(part, axis=0), tail)
                ref[pl.ds(steps * share, tail)] = jnp.zeros((tail, ref.shape[1]), ref.dtype)
                ref[pl.ds(steps * share, tail), pl.ds(0, share)] = rows.astype(ref.dtype)


def _pack_kernel(sources, window, *refs):
    line = 0
    for score_ref in refs[:-sources]:
        size = score_ref.shape[0]
        for n, out_ref in enumerate(refs[-sources:]):
            out_ref[line : line + size] = score_ref[:, n * window : (n + 1) * window]
        line += size


def _score_kernel(cells, window, rel_ref, off_ref, values_ref, out_ref):
    rows = rel_ref.shape[1]
    hot = jnp.where(
        lax.broadcasted_iota(jnp.int32, (window, rows), 0) == off_ref[...], 1.0, 0.0
    ).astype(jnp.bfloat16)
    rest = values_ref[...]
    mine = lax.broadcasted_iota(jnp.int32, (cells, rows), 0) == rel_ref[...]
    total = jnp.zeros((cells, rows), jnp.float32)
    for _ in range(3):
        term = rest.astype(jnp.bfloat16)
        rest = rest - term.astype(jnp.float32)
        total += jnp.dot(term, hot, preferred_element_type=jnp.float32)
    out_ref[...] = jnp.sum(jnp.where(mine, total, 0.0), axis=0, keepdims=True)


def _after(value, *others):
    return lax.optimization_barrier((value, *others))[0]


def _update_kernel(per_core, chips, piece, mine, code_ref, keep_ref, mass_ref, *refs):
    got_refs, refs = refs[: 2 * (chips - 1)], refs[2 * (chips - 1) :]
    (first_ref, others_ref, tail_ref), out_ref, weight = refs[:3], refs[3], refs[-1]
    step = pl.program_id(0)
    lines = mass_ref[:, 0, :128]
    for ref in [*got_refs[1::2], tail_ref]:
        rows = ref[...].astype(jnp.float32)
        for n in range(3):
            lines = lines + rows[n * per_core : (n + 1) * per_core]
    line = lax.broadcasted_iota(jnp.int32, lines.shape, 0)
    mass = jnp.sum(jnp.where(line == step, lines, 0.0), axis=0, keepdims=True)
    weight[...] = jnp.broadcast_to(1.0 / (mass + prior_mass), (128, 128)).T
    numer = keep_ref[0]
    for ref in got_refs[0::2]:
        numer = numer + ref[...].astype(jnp.float32)
    far = jnp.where(step == 0, first_ref[...], others_ref[...])
    low = lax.rem((code_ref[2] if mine else 1 - code_ref[2]) + code_ref[1], 2) * piece
    numer = numer + far.astype(jnp.float32)
    out_ref[0, :piece] = numer * weight[pl.ds(pl.multiple_of(low, piece), piece), :1]
    if not mine:
        out_ref[0, piece:] = jnp.zeros((8, out_ref.shape[2]), jnp.float32)
        out_ref[0, piece:, :128] = jnp.broadcast_to(mass, (8, 128))
        lines_ref = refs[4]

        @pl.when(step == 0)
        def _():
            lines_ref[...] = jnp.concatenate(
                [lines, jnp.zeros((lines_ref.shape[0] - per_core, 128), jnp.float32)], axis=0
            )


def _finish_kernel(per_core, piece, code_ref, mine_ref, swap_ref, line_ref, lines_ref, out_ref, mass_ref, sems):
    other = 1 - code_ref[2]
    copies = [
        pltpu.make_async_copy(mine_ref, out_ref.at[pl.ds(code_ref[2] * per_core, per_core)], sems.at[0]),
        pltpu.make_async_copy(
            swap_ref.at[:, pl.ds(0, piece)], out_ref.at[pl.ds(other * per_core, per_core)], sems.at[1]
        ),
    ]
    for copy in copies:
        copy.start()
    mine = lines_ref[:per_core]
    theirs = line_ref[:, 0]
    lines = jnp.where(
        other == 1, jnp.concatenate([mine, theirs], axis=0), jnp.concatenate([theirs, mine], axis=0)
    )
    here = lax.rem(code_ref[2] + code_ref[1], 2)
    mass_ref[...] = jnp.where(here == 0, lines[:, :piece], lines[:, piece : 2 * piece])
    for copy in copies:
        copy.wait()


def _params():
    return pltpu.CompilerParams(vmem_limit_bytes=vmem_limit)


def _cell_call(code, sharp, arrays, near, row_blocks, window, reach, per_core, begin, steps, kids, share, sends, earlier, tail):
    sources = len(row_blocks)
    span, width = row_blocks[0].shape
    pieces = kids // (share // 2)
    arrays, places = zip(*arrays, strict=True)
    rows = sources * window
    out_shape = [
        jax.ShapeDtypeStruct((steps, share, width), jnp.float32),
        jax.ShapeDtypeStruct((steps, 8, kids), jnp.float32),
        jax.ShapeDtypeStruct((steps, 8, rows), jnp.float32),
    ] + [jax.ShapeDtypeStruct((steps * share + tail, width), wire)] * sends
    fixed = lambda shape: pl.BlockSpec(shape, lambda n, *_: (0,) * len(shape))
    moving = lambda shape: pl.BlockSpec((1, *shape[1:]), lambda n, *_: (n, 0, 0))
    return pl.pallas_call(
        functools.partial(
            _cell_kernel, sources, window, reach, pieces, places, near, share, steps, per_core, begin, span, len(earlier), tail
        ),
        grid_spec=pltpu.PrefetchScalarGridSpec(
            num_scalar_prefetch=2,
            grid=(steps,),
            in_specs=(
                [pl.BlockSpec((1, kids, width), lambda n, c, _: (c[2] * per_core + begin + n, 0, 0))]
                if near
                else [anywhere] * len(arrays)
            )
            + [anywhere] * sources
            + [fixed(v.shape) for v in earlier],
            out_specs=[
                (moving if n in (0, 2) else fixed)(o.shape) for n, o in enumerate(out_shape)
            ],
            scratch_shapes=[
                pltpu.VMEM((sources, window if begin + steps == 1 else reach, width), jnp.bfloat16),
                pltpu.VMEM((1 if near else steps, kids, width), jnp.bfloat16),
                pltpu.SemaphoreType.DMA((sources + len(places),)),
                pltpu.VMEM((sources * meta_extra, 128), jnp.bfloat16),
                pltpu.SemaphoreType.DMA((sources,)),
            ],
        ),
        out_shape=out_shape,
        compiler_params=pltpu.CompilerParams(vmem_limit_bytes=44 * 1024 * 1024),
        cost_estimate=busy,
    )(code, sharp, *arrays, *row_blocks, *earlier)


def on_device(frames, labels, centroids, sharpness):
    cell_count = lax.axis_size("cell")
    frame_count = lax.axis_size("frame")
    group_count = 2
    cells_local, kids, width = centroids.shape
    rows = frames.shape[0]
    cells_total = cells_local * cell_count
    half = cell_count // 2
    chips = frame_count // cores
    per_core = cells_local // cores
    cell_cap = 3 * rows // cells_total
    own_slots = 2 * rows // cell_count
    sources = half * cores
    window = -(-(cell_cap + 16) // 16) * 16
    while sources * window % 128:
        window += 16
    reach = min(own_slots, -(-per_core * cell_cap // 16) * 16)
    window = min(window, reach)
    share = kids // chips
    piece = share // group_count

    z = lax.axis_index("cell")
    j = lax.axis_index("frame")
    y = lax.axis_index("groups")
    x, k = j // cores, j % cores
    p, h = z % half, z // half

    def at(zz, xx, kk):
        return zz * frame_count + xx * cores + kk

    def hop_core(v):
        return lax.ppermute(v, "frame", [(i, i ^ 1) for i in range(frame_count)])

    def hop_chip(v, s):
        return lax.ppermute(
            v,
            "frame",
            [(a * cores + c, (a + s) % chips * cores + c) for a in range(chips) for c in range(cores)],
        )

    def hop_member(v, s):
        return lax.ppermute(
            v, "cell", [(b * half + i, b * half + (i + s) % half) for b in range(2) for i in range(half)]
        )

    def hop_partner(v):
        return lax.ppermute(v, "cell", [(i, (i + half) % cell_count) for i in range(cell_count)])

    def hop_group(v):
        return lax.ppermute(v, "groups", [(i, 1 - i) for i in range(2)])

    def hop_any(v, s, kk):
        pairs = [
            (at(b * half + i, a, c), at(b * half + (i + s) % half, a, c ^ kk))
            for b in range(2)
            for i in range(half)
            for a in range(chips)
            for c in range(cores)
        ]
        return lax.ppermute(v, ("cell", "frame"), pairs)

    parts = [(0, 1), (1, per_core - 1)]
    foreign_sharp = hop_partner(sharpness)
    first = hop_partner(
        lax.dynamic_slice(
            centroids,
            (k * per_core, (x * group_count + y) * piece, 0),
            (per_core, piece, width),
        )
    )
    by_chip = [first] + [hop_chip(first, -s) for s in range(1, chips)]
    by_group = hop_group(first)
    around = [*by_chip[1:], by_group]
    part = piece // 2
    foreign_pieces = [(first, 0), (by_group, piece)]
    for s in range(1, chips):
        foreign_pieces += [
            (by_chip[s], s * share),
            (hop_group(by_chip[s][:, :part]), s * share + piece),
            (hop_chip(by_group[:, part:], -s), s * share + piece + part),
        ]

    label = labels.reshape(1, rows)
    owner, local = label // cells_local, label % cells_local
    member = (owner % half - p + half) % half
    foreign = (owner // half != h).astype(jnp.int32)
    other = (local // per_core) ^ k
    rel = (member * 2 + foreign) * meta_extra + other * per_core + local % per_core

    seg = lambda s, t: s * 2 + t
    first_segs = [seg(s, 1) for s in range(1, half)]
    next_segs = [seg(s, 0) for s in range(1, half)]
    span = own_slots + meta_extra
    block = jax.ShapeDtypeStruct((span, width), jnp.bfloat16)
    lines = cell_count * meta_extra
    flat, off, meta, *blocks = pl.pallas_call(
        functools.partial(_place_kernel, per_core, reach, window, own_slots, first_segs),
        out_shape=[
            jax.ShapeDtypeStruct((1, rows), jnp.int32),
            jax.ShapeDtypeStruct((1, rows), jnp.int32),
            jax.ShapeDtypeStruct((lines, 128), jnp.float32),
        ]
        + [block] * len(first_segs),
        compiler_params=_params(),
        cost_estimate=dear,
    )(rel, frames)
    segments = dict(zip(first_segs, blocks, strict=True))

    blocks = pl.pallas_call(
        functools.partial(_pick_kernel, next_segs),
        out_shape=[block] * len(next_segs),
        compiler_params=_params(),
        cost_estimate=dear,
    )(_after(flat, first), meta, frames)
    segments.update(zip(next_segs, blocks, strict=True))
    received = {1: [hop_member(segments[seg(s, 1)], s) for s in range(1, half)]}
    here = {}
    for t, gate in ((1, (*blocks, foreign_sharp, *around)), (0, received[1])):
        here[t] = pl.pallas_call(
            functools.partial(_pick_kernel, [seg(0, t)]),
            out_shape=[block],
            compiler_params=_params(),
            cost_estimate=dear,
        )(_after(flat, *gate), meta, frames)[0]

    received[0] = [hop_member(segments[seg(s, 0)], s) for s in range(1, half)]

    def held_of(t, *gate):
        held = [here[t], hop_core(here[t])]
        for v in received[t]:
            v = _after(v, *gate)
            held += [v, hop_core(v)]
        return held

    held = {1: held_of(1, *around)}

    code = jnp.stack([x, y, k]).astype(jnp.int32)
    tail = -(-3 * per_core // 16) * 16

    def masses_in(rows):
        rows = rows[:, :share].astype(jnp.float32)
        return sum(rows[n * per_core : (n + 1) * per_core] for n in range(3))

    def over_chips(result, steps, earlier, extra):
        keep, mass, _, *sends = result
        mass = jnp.concatenate([*earlier, mass])[:, 0, :share]
        for s in range(1, chips):
            got = hop_chip(sends[s - 1], s)
            keep = keep + got[: steps * share].reshape(keep.shape).astype(jnp.float32)
            if extra:
                mass = mass + masses_in(got[steps * share :])
        return keep, mass

    results, totals, theirs, notes = [], [], [], []
    for t, begin, size in [(1, *part) for part in parts] + [(0, 0, per_core)]:
        if not t:
            held[0] = held_of(0, totals[0])
            notes.append(
                pl.pallas_call(
                    _copy_kernel,
                    out_shape=jax.ShapeDtypeStruct(notes[-1].shape, jnp.float32),
                    compiler_params=_params(),
                    cost_estimate=dear,
                )(_after(notes.pop(), totals[1]))
            )
        code_here = _after(code, notes[-1]) if results else code
        earlier = [r[1] for r in results] if t else []
        extra = 0 if t and begin + size < per_core else tail
        results.append(
            _cell_call(
                code_here, foreign_sharp if t else sharpness, foreign_pieces if t else [(centroids, 0)],
                not t, held[t], window, reach, per_core,
                begin, size, kids, share, chips - 1, earlier if extra else [], extra,
            )
        )
        if t:
            scores = results[-1][2]
            if totals:
                scores = _after(scores, totals[0])
            notes.append(
                pl.pallas_call(
                    _note_kernel,
                    out_shape=jax.ShapeDtypeStruct((size, sources * window), jnp.float32),
                    compiler_params=_params(),
                    cost_estimate=dear,
                )(scores)
            )
        if not t:
            arrived = [hop_chip(results[-1][3 + n], n + 1) for n in range(chips - 1)]
            break
        total, mass = over_chips(results[-1], size, earlier, extra)
        if t and extra:
            total = _after(total, notes[-1])
        total = total.astype(wire).reshape(size * share, width)
        if extra:
            high = _round(mass)
            middle = _round(mass - high)
            terms = jnp.concatenate([high, middle, mass - high - middle])
            behind = jnp.pad(terms.astype(wire), ((0, tail - terms.shape[0]), (0, width - share)))
            total = jnp.concatenate([total, behind])
        theirs.append(hop_partner(total))
        totals.append(total)
    score_parts = pl.pallas_call(
        functools.partial(_pack_kernel, sources, window),
        out_shape=[jax.ShapeDtypeStruct((2 * per_core, window), jnp.float32)] * sources,
        compiler_params=_params(),
        cost_estimate=dear,
    )(*notes, results[-1][2][:, 0])

    back = {}
    for s in range(half):
        for kk in range(cores):
            n = s * cores + kk
            back[s, kk] = score_parts[n] if n == 0 else hop_any(score_parts[n], -s, kk)
    values = []
    for s in range(half):
        for t in range(2):
            at_row = 0 if t else per_core
            for kk in range(cores):
                values.append(back[s, kk][at_row : at_row + per_core])
            values.append(jnp.zeros((meta_extra - cells_local, window), jnp.float32))
    frame_score = pl.pallas_call(
        functools.partial(_score_kernel, lines, window),
        out_shape=jax.ShapeDtypeStruct((1, rows), jnp.float32),
        compiler_params=_params(),
        cost_estimate=dear,
    )(rel, off, jnp.concatenate(values, axis=0)).reshape(rows)

    theirs = [_after(v, *arrived) for v in theirs]
    one_cell = lambda block, where: pl.BlockSpec(block, where)
    whole = lambda v: pl.BlockSpec(v.shape, lambda n, c: (0,) * v.ndim)
    behind = lambda steps: pl.BlockSpec((tail, 128), lambda n, c: (steps * share // tail, 0))
    keep, mass = results[-1][:2]

    def update(mine):
        def part(c):
            return lax.rem((c[2] if mine else 1 - c[2]) + c[1], 2)

        got, got_specs = [], []
        for v in arrived:
            got += [v, v]
            got_specs += [
                one_cell((piece, width), lambda n, c: (2 * n + part(c), 0)),
                behind(per_core),
            ]
        if mine:
            out_specs = [one_cell((1, piece, width), lambda n, c: (n, 0, 0))]
            out_shape = [jax.ShapeDtypeStruct((per_core, piece, width), jnp.float32)]
        else:
            out_specs = [
                one_cell((1, piece + 8, width), lambda n, c: (n, 0, 0)),
                pl.BlockSpec((8, 128), lambda n, c: (0, 0)),
            ]
            out_shape = [
                jax.ShapeDtypeStruct((per_core, piece + 8, width), jnp.float32),
                jax.ShapeDtypeStruct((8, 128), jnp.float32),
            ]
        return pl.pallas_call(
            functools.partial(_update_kernel, per_core, chips, piece, mine),
            grid_spec=pltpu.PrefetchScalarGridSpec(
                num_scalar_prefetch=1,
                grid=(per_core,),
                in_specs=[
                    one_cell((1, piece, width), lambda n, c: (n, part(c), 0)),
                    whole(mass),
                    *got_specs,
                    one_cell((piece, width), lambda n, c: (part(c), 0)),
                    one_cell((piece, width), lambda n, c: (2 * jnp.maximum(n - 1, 0) + part(c), 0)),
                    behind(per_core - 1),
                ],
                out_specs=out_specs,
                scratch_shapes=[pltpu.VMEM((128, 128), jnp.float32)],
            ),
            out_shape=out_shape,
            compiler_params=_params(),
            cost_estimate=busy,
        )(code, keep, mass, *got, theirs[0], theirs[1], theirs[1])

    swap, lines_mine = update(False)
    (out,) = update(True)
    swapped = hop_core(swap)
    new_centroids, child_mass = pl.pallas_call(
        functools.partial(_finish_kernel, per_core, piece),
        grid_spec=pltpu.PrefetchScalarGridSpec(
            num_scalar_prefetch=1,
            grid=(1,),
            in_specs=[
                anywhere,
                anywhere,
                pl.BlockSpec((per_core, 8, 128), lambda n, c: (0, piece // 8, 0)),
                pl.BlockSpec((8, 128), lambda n, c: (0, 0)),
            ],
            out_specs=[anywhere, pl.BlockSpec((cells_local, piece), lambda n, c: (0, 0))],
            scratch_shapes=[pltpu.SemaphoreType.DMA((2,))],
        ),
        out_shape=[
            jax.ShapeDtypeStruct((cells_local, piece, width), jnp.float32),
            jax.ShapeDtypeStruct((cells_local, piece), jnp.float32),
        ],
        compiler_params=_params(),
        cost_estimate=busy,
    )(code, out, swapped, swapped, lines_mine)
    return new_centroids, child_mass, frame_score


def solution(mesh):
    return jax.shard_map(
        on_device,
        mesh=mesh,
        in_specs=(
            P(("groups", "cell", "frame"), None),
            P(("groups", "cell", "frame"), None),
            P("cell", None, None),
            P("cell"),
        ),
        out_specs=(
            P(("groups", "cell"), "frame", None),
            P(("groups", "cell"), "frame"),
            P(("groups", "cell", "frame")),
        ),
        check_vma=False,
    )
```

```python
import functools

import jax
import jax.numpy as jnp
from jax import lax
from jax.experimental import pallas as pl
from jax.experimental.pallas import tpu as pltpu
from jax.sharding import PartitionSpec as P

prior_mass = 1.0
cores = 2
wire = jnp.bfloat16
vmem_limit = 16 * 1024 * 1024
anywhere = pl.BlockSpec(memory_space=pl.ANY)
cheap = pl.CostEstimate(flops=1, bytes_accessed=1, transcendentals=0)
busy = pl.CostEstimate(flops=20_000_000_000, bytes_accessed=1, transcendentals=0)
dear = pl.CostEstimate(flops=20_000_000_000, bytes_accessed=1_000_000_000, transcendentals=0)
meta_extra = 16


def _hot(flat_row, segment, own_slots):
    rows = flat_row.shape[1]
    slot = lax.broadcasted_iota(jnp.int32, (own_slots, rows), 0) + segment * own_slots
    return jnp.where(slot == flat_row, 1.0, 0.0).astype(jnp.bfloat16)


def _pick(flat_row, meta, frames_ref, segment, out_ref):
    own_slots = out_ref.shape[0] - meta_extra
    hot = _hot(flat_row, segment, own_slots)
    out_ref[pl.ds(0, own_slots)] = jnp.dot(
        hot, frames_ref[...], preferred_element_type=jnp.float32
    ).astype(jnp.bfloat16)
    out_ref[pl.ds(own_slots, meta_extra)] = jnp.zeros((meta_extra, out_ref.shape[1]), jnp.bfloat16)
    out_ref[pl.ds(own_slots, meta_extra), pl.ds(0, 128)] = meta[
        segment * meta_extra : (segment + 1) * meta_extra
    ].astype(jnp.bfloat16)


def _place_kernel(
    per_core, reach, window, own_slots, segments, rel_ref, frames_ref, flat_ref, off_ref, meta_ref, *outs
):
    rows = rel_ref.shape[1]
    lines = meta_ref.shape[0]
    rel = rel_ref[...]
    line = lax.broadcasted_iota(jnp.int32, (lines, rows), 0)
    base = (line // meta_extra) * meta_extra
    segment = rel // meta_extra
    hits = jnp.where(rel == line, 1, 0)
    lane = lax.broadcasted_iota(jnp.int32, (lines, rows), 1)
    running = hits
    step = 1
    while step < rows:
        running += jnp.where(lane >= step, pltpu.roll(running, step, 1), 0)
        step *= 2
    count = jnp.sum(hits, axis=1, keepdims=True)
    ahead = jnp.sum(jnp.where((rel < line) & (rel >= base), 1, 0), axis=1, keepdims=True)
    behind = jnp.sum(
        jnp.where((rel <= line) & (rel >= base + per_core), 1, 0), axis=1, keepdims=True
    )
    back = (line - base)[:, :1] >= per_core
    start = jnp.where(back, own_slots - behind, ahead)
    floor = jnp.where(back, own_slots - reach, 0)
    first = jnp.minimum(((start - floor) >> 4) << 4, reach - window) + floor
    position = jnp.sum(hits * (running + (start - 1)), axis=0, keepdims=True)
    flat = segment * own_slots + position
    flat_ref[...] = flat
    off_ref[...] = jnp.sum(hits * (running + (start - first - 1)), axis=0, keepdims=True)
    column = lax.broadcasted_iota(jnp.int32, meta_ref.shape, 1)
    meta = jnp.where(
        column == 0,
        (first - floor) >> 4,
        jnp.where(column == 1, start - first, jnp.where(column == 2, count, 0)),
    ).astype(jnp.float32)
    meta_ref[...] = meta
    for g, out_ref in zip(segments, outs, strict=True):
        _pick(flat, meta, frames_ref, g, out_ref)


def _pick_kernel(segments, flat_ref, meta_ref, frames_ref, *outs):
    flat, meta = flat_ref[...], meta_ref[...]
    for g, out_ref in zip(segments, outs, strict=True):
        _pick(flat, meta, frames_ref, g, out_ref)


def _split(lines, rows):
    high = lines.astype(jnp.bfloat16).astype(jnp.float32)
    middle = (lines - high).astype(jnp.bfloat16).astype(jnp.float32)
    rest = jnp.zeros((rows - 3 * lines.shape[0], lines.shape[1]), jnp.float32)
    return jnp.concatenate([high, middle, lines - high - middle, rest], axis=0)


def _round(value):
    return lax.reduce_precision(value, 8, 7)


def _note_kernel(score_ref, out_ref):
    out_ref[...] = score_ref[:, 0]


def _copy_kernel(in_ref, out_ref):
    out_ref[...] = in_ref[...]


def _split(lines, rows):
    high = lines.astype(jnp.bfloat16).astype(jnp.float32)
    middle = (lines - high).astype(jnp.bfloat16).astype(jnp.float32)
    rest = jnp.zeros((rows - 3 * lines.shape[0], lines.shape[1]), jnp.float32)
    return jnp.concatenate([high, middle, lines - high - middle, rest], axis=0)


def _note_kernel(score_ref, out_ref):
    out_ref[...] = score_ref[:, 0]


def _copy_kernel(in_ref, out_ref):
    out_ref[...] = in_ref[...]


def _prior_kernel(group_count, code_ref, *refs):
    for g in range(group_count):
        size = refs[g].shape[1]
        refs[-1][:, g * size : (g + 1) * size] = refs[g][...].astype(jnp.float32)


def _cell_kernel(sources, window, reach, pieces, places, near, share, steps, per_core, begin, span, earlier, tail, *refs):
    code_ref, sharp_ref = refs[:2]
    refs = refs[2:]
    centre_refs, refs = refs[: len(places)], refs[len(places) :]
    piece = share // 2
    row_refs, refs = refs[:sources], refs[sources:]
    earlier_refs, refs = refs[:earlier], refs[earlier:]
    keep_ref, mass_ref, score_ref = refs[:3]
    send_refs, (held, centres, sems, meta_low, meta_sems) = refs[3:-5], refs[-5:]
    step = pl.program_id(0)
    loads = []
    first_only = begin + steps == 1
    reach = window if first_only else reach
    for n in range(sources):
        low = 0 if n % cores == 0 else span - meta_extra - reach
        loads.append(
            pltpu.make_async_copy(
                row_refs[n].at[pl.ds(low, reach)],
                held.at[n, pl.ds(0, reach)],
                sems.at[n],
            )
        )
    if not near:
        for n, low in enumerate(places):
            loads.append(
                pltpu.make_async_copy(
                    centre_refs[n].at[pl.ds(begin, steps)],
                    centres.at[:, pl.ds(low, centre_refs[n].shape[1])],
                    sems.at[sources + n],
                )
            )

    @pl.when(step == 0)
    def _():
        lines = [
            pltpu.make_async_copy(
                row_refs[n].at[pl.ds(span - meta_extra, meta_extra), pl.ds(0, 128)],
                meta_low.at[pl.ds(n * meta_extra, meta_extra)],
                meta_sems.at[n],
            )
            for n in range(sources)
        ]
        for copy in lines + loads:
            copy.start()
        for copy in lines:
            copy.wait()
        for copy in loads:
            copy.wait()

    if near:
        found = []
        for n in range(pieces):
            chip = lax.rem(code_ref[0] + n // 2, pieces // 2)
            kid = (chip * 2 + lax.rem(code_ref[1] + n % 2, 2)) * piece
            found.append(centre_refs[0][0, pl.ds(pl.multiple_of(kid, piece), piece)])
        centre = jnp.concatenate(found, axis=0)
    else:
        centre = centres[step]
    wide = centre.astype(jnp.float32)
    half_norm = 0.5 * jnp.sum(wide * wide, axis=1, keepdims=True)
    slot = lax.broadcasted_iota(jnp.int32, (1, sources * window), 1)
    valid = slot < 0
    lines = meta_low[...].astype(jnp.float32).astype(jnp.int32)
    line = lax.broadcasted_iota(jnp.int32, lines.shape, 0)
    firsts = []
    for n in range(sources):
        at_line = n * meta_extra + (n % cores) * per_core + begin
        found = lines[at_line : at_line + 1]
        if steps > 1:
            found = jnp.sum(jnp.where(line == at_line + step, lines, 0), axis=0, keepdims=True)
        firsts.append(None if first_only else found[0, 0] * 16)
        low = found[:, 1:2] + n * window
        valid = valid | ((slot >= low) & (slot < low + found[:, 2:3]))
    if first_only:
        chosen = held[...].reshape(sources * window, held.shape[2])
    else:
        chosen = jnp.concatenate(
            [held[n, pl.ds(pl.multiple_of(firsts[n], 16), window)] for n in range(sources)]
        )
    products = lax.dot_general(
        centre, chosen, (((1,), (1,)), ((), ())), preferred_element_type=jnp.float32
    )
    scores = sharp_ref[code_ref[2] * per_core + begin + step] * (products - half_norm)
    top = jnp.max(scores, axis=0, keepdims=True)
    exponent = jnp.exp(scores - top)
    total = jnp.sum(exponent, axis=0, keepdims=True)
    score_ref[0] = jnp.broadcast_to(
        jnp.where(valid, top + jnp.log(total), 0.0), score_ref.shape[1:]
    )
    resp = exponent * jnp.where(valid, 1.0 / total, 0.0)
    mass = jnp.sum(resp, axis=1, keepdims=True)
    mass_ref[step] = jnp.broadcast_to(mass, (mass.shape[0], 128)).T[: mass_ref.shape[1]]
    low = resp.astype(jnp.bfloat16)
    numer = jnp.dot(low, chosen, preferred_element_type=jnp.float32)
    keep_ref[0] = numer[:share] + prior_mass * centre[:share].astype(jnp.float32) if near else numer[:share]
    for n, ref in enumerate(send_refs):
        at_row = pl.multiple_of(step * share, share)
        ref[pl.ds(at_row, share)] = numer[(n + 1) * share : (n + 2) * share].astype(ref.dtype)

    if tail:

        @pl.when(step == steps - 1)
        def _():
            lines = [r[i, :1] for r in (*earlier_refs, mass_ref) for i in range(r.shape[0])]
            for n, ref in enumerate(send_refs):
                part = [v[:, (n + 1) * share : (n + 2) * share] for v in lines]
                rows = _split(jnp.concatenate(part, axis=0), tail)
                ref[pl.ds(steps * share, tail)] = jnp.zeros((tail, ref.shape[1]), ref.dtype)
                ref[pl.ds(steps * share, tail), pl.ds(0, share)] = rows.astype(ref.dtype)


def _pack_kernel(sources, window, *refs):
    line = 0
    for score_ref in refs[:-sources]:
        size = score_ref.shape[0]
        for n, out_ref in enumerate(refs[-sources:]):
            out_ref[line : line + size] = score_ref[:, n * window : (n + 1) * window]
        line += size


def _score_kernel(cells, window, rel_ref, off_ref, values_ref, out_ref):
    rows = rel_ref.shape[1]
    hot = jnp.where(
        lax.broadcasted_iota(jnp.int32, (window, rows), 0) == off_ref[...], 1.0, 0.0
    ).astype(jnp.bfloat16)
    rest = values_ref[...]
    mine = lax.broadcasted_iota(jnp.int32, (cells, rows), 0) == rel_ref[...]
    total = jnp.zeros((cells, rows), jnp.float32)
    for _ in range(3):
        term = rest.astype(jnp.bfloat16)
        rest = rest - term.astype(jnp.float32)
        total += jnp.dot(term, hot, preferred_element_type=jnp.float32)
    out_ref[...] = jnp.sum(jnp.where(mine, total, 0.0), axis=0, keepdims=True)


def _after(value, *others):
    return lax.optimization_barrier((value, *others))[0]


def _update_kernel(per_core, chips, piece, mine, code_ref, keep_ref, mass_ref, *refs):
    got_refs, refs = refs[: 2 * (chips - 1)], refs[2 * (chips - 1) :]
    (first_ref, others_ref, tail_ref), out_ref, weight = refs[:3], refs[3], refs[-1]
    step = pl.program_id(0)
    lines = mass_ref[:, 0, :128]
    for ref in [*got_refs[1::2], tail_ref]:
        rows = ref[...].astype(jnp.float32)
        for n in range(3):
            lines = lines + rows[n * per_core : (n + 1) * per_core]
    line = lax.broadcasted_iota(jnp.int32, lines.shape, 0)
    mass = jnp.sum(jnp.where(line == step, lines, 0.0), axis=0, keepdims=True)
    weight[...] = jnp.broadcast_to(1.0 / (mass + prior_mass), (128, 128)).T
    numer = keep_ref[0]
    for ref in got_refs[0::2]:
        numer = numer + ref[...].astype(jnp.float32)
    far = jnp.where(step == 0, first_ref[...], others_ref[...])
    low = lax.rem((code_ref[2] if mine else 1 - code_ref[2]) + code_ref[1], 2) * piece
    numer = numer + far.astype(jnp.float32)
    out_ref[0, :piece] = numer * weight[pl.ds(pl.multiple_of(low, piece), piece), :1]
    if not mine:
        out_ref[0, piece:] = jnp.zeros((8, out_ref.shape[2]), jnp.float32)
        out_ref[0, piece:, :128] = jnp.broadcast_to(mass, (8, 128))
        lines_ref = refs[4]

        @pl.when(step == 0)
        def _():
            lines_ref[...] = jnp.concatenate(
                [lines, jnp.zeros((lines_ref.shape[0] - per_core, 128), jnp.float32)], axis=0
            )


def _finish_kernel(per_core, piece, code_ref, _, swap_ref, line_ref, lines_ref, out_ref, mass_ref, sem):
    other = 1 - code_ref[2]
    copy = pltpu.make_async_copy(
        swap_ref.at[:, pl.ds(0, piece)], out_ref.at[pl.ds(other * per_core, per_core)], sem
    )
    copy.start()
    mine = lines_ref[:per_core]
    theirs = line_ref[:, 0]
    lines = jnp.where(
        other == 1, jnp.concatenate([mine, theirs], axis=0), jnp.concatenate([theirs, mine], axis=0)
    )
    here = lax.rem(code_ref[2] + code_ref[1], 2)
    mass_ref[...] = jnp.where(here == 0, lines[:, :piece], lines[:, piece : 2 * piece])
    copy.wait()


def _params():
    return pltpu.CompilerParams(vmem_limit_bytes=vmem_limit)


def _cell_call(code, sharp, arrays, near, row_blocks, window, reach, per_core, begin, steps, kids, share, sends, earlier, tail):
    sources = len(row_blocks)
    span, width = row_blocks[0].shape
    pieces = kids // (share // 2)
    arrays, places = zip(*arrays, strict=True)
    rows = sources * window
    out_shape = [
        jax.ShapeDtypeStruct((steps, share, width), jnp.float32),
        jax.ShapeDtypeStruct((steps, 8, kids), jnp.float32),
        jax.ShapeDtypeStruct((steps, 8, rows), jnp.float32),
    ] + [jax.ShapeDtypeStruct((steps * share + tail, width), wire)] * sends
    fixed = lambda shape: pl.BlockSpec(shape, lambda n, *_: (0,) * len(shape))
    moving = lambda shape: pl.BlockSpec((1, *shape[1:]), lambda n, *_: (n, 0, 0))
    return pl.pallas_call(
        functools.partial(
            _cell_kernel, sources, window, reach, pieces, places, near, share, steps, per_core, begin, span, len(earlier), tail
        ),
        grid_spec=pltpu.PrefetchScalarGridSpec(
            num_scalar_prefetch=2,
            grid=(steps,),
            in_specs=(
                [pl.BlockSpec((1, kids, width), lambda n, c, _: (c[2] * per_core + begin + n, 0, 0))]
                if near
                else [anywhere] * len(arrays)
            )
            + [anywhere] * sources
            + [fixed(v.shape) for v in earlier],
            out_specs=[
                (moving if n in (0, 2) else fixed)(o.shape) for n, o in enumerate(out_shape)
            ],
            scratch_shapes=[
                pltpu.VMEM((sources, window if begin + steps == 1 else reach, width), jnp.bfloat16),
                pltpu.VMEM((1 if near else steps, kids, width), jnp.bfloat16),
                pltpu.SemaphoreType.DMA((sources + len(places),)),
                pltpu.VMEM((sources * meta_extra, 128), jnp.bfloat16),
                pltpu.SemaphoreType.DMA((sources,)),
            ],
        ),
        out_shape=out_shape,
        compiler_params=pltpu.CompilerParams(vmem_limit_bytes=28 * 1024 * 1024),
        cost_estimate=busy,
    )(code, sharp, *arrays, *row_blocks, *earlier)


def on_device(frames, labels, centroids, sharpness):
    cell_count = lax.axis_size("cell")
    frame_count = lax.axis_size("frame")
    group_count = 2
    cells_local, kids, width = centroids.shape
    rows = frames.shape[0]
    cells_total = cells_local * cell_count
    half = cell_count // 2
    chips = frame_count // cores
    per_core = cells_local // cores
    cell_cap = 3 * rows // cells_total
    own_slots = 2 * rows // cell_count
    sources = half * cores
    window = -(-(cell_cap + 16) // 16) * 16
    while sources * window % 128:
        window += 16
    reach = min(own_slots, -(-per_core * cell_cap // 16) * 16)
    window = min(window, reach)
    share = kids // chips
    piece = share // group_count

    z = lax.axis_index("cell")
    j = lax.axis_index("frame")
    y = lax.axis_index("groups")
    x, k = j // cores, j % cores
    p, h = z % half, z // half

    def at(zz, xx, kk):
        return zz * frame_count + xx * cores + kk

    def hop_core(v):
        return lax.ppermute(v, "frame", [(i, i ^ 1) for i in range(frame_count)])

    def hop_chip(v, s):
        return lax.ppermute(
            v,
            "frame",
            [(a * cores + c, (a + s) % chips * cores + c) for a in range(chips) for c in range(cores)],
        )

    def hop_member(v, s):
        return lax.ppermute(
            v, "cell", [(b * half + i, b * half + (i + s) % half) for b in range(2) for i in range(half)]
        )

    def hop_partner(v):
        return lax.ppermute(v, "cell", [(i, (i + half) % cell_count) for i in range(cell_count)])

    def hop_group(v):
        return lax.ppermute(v, "groups", [(i, 1 - i) for i in range(2)])

    def hop_any(v, s, kk):
        pairs = [
            (at(b * half + i, a, c), at(b * half + (i + s) % half, a, c ^ kk))
            for b in range(2)
            for i in range(half)
            for a in range(chips)
            for c in range(cores)
        ]
        return lax.ppermute(v, ("cell", "frame"), pairs)

    parts = [(0, 1), (1, per_core - 1)]
    foreign_sharp = hop_partner(sharpness)
    first = hop_partner(
        lax.dynamic_slice(
            centroids,
            (k * per_core, (x * group_count + y) * piece, 0),
            (per_core, piece, width),
        )
    )
    by_chip = [first] + [hop_chip(first, -s) for s in range(1, chips)]
    by_group = hop_group(first)
    around = [*by_chip[1:], by_group]
    part = piece // 2
    foreign_pieces = [(first, 0), (by_group, piece)]
    for s in range(1, chips):
        foreign_pieces += [
            (by_chip[s], s * share),
            (hop_group(by_chip[s][:, :part]), s * share + piece),
            (hop_chip(by_group[:, part:], -s), s * share + piece + part),
        ]

    label = labels.reshape(1, rows)
    owner, local = label // cells_local, label % cells_local
    member = (owner % half - p + half) % half
    foreign = (owner // half != h).astype(jnp.int32)
    other = (local // per_core) ^ k
    rel = (member * 2 + foreign) * meta_extra + other * per_core + local % per_core

    seg = lambda s, t: s * 2 + t
    first_segs = [seg(s, 1) for s in range(1, half)]
    next_segs = [seg(s, 0) for s in range(1, half)]
    span = own_slots + meta_extra
    block = jax.ShapeDtypeStruct((span, width), jnp.bfloat16)
    lines = cell_count * meta_extra
    flat, off, meta, *blocks = pl.pallas_call(
        functools.partial(_place_kernel, per_core, reach, window, own_slots, first_segs),
        out_shape=[
            jax.ShapeDtypeStruct((1, rows), jnp.int32),
            jax.ShapeDtypeStruct((1, rows), jnp.int32),
            jax.ShapeDtypeStruct((lines, 128), jnp.float32),
        ]
        + [block] * len(first_segs),
        compiler_params=_params(),
        cost_estimate=dear,
    )(rel, frames)
    segments = dict(zip(first_segs, blocks, strict=True))

    blocks = pl.pallas_call(
        functools.partial(_pick_kernel, next_segs),
        out_shape=[block] * len(next_segs),
        compiler_params=_params(),
        cost_estimate=dear,
    )(_after(flat, first), meta, frames)
    segments.update(zip(next_segs, blocks, strict=True))
    received = {1: [hop_member(segments[seg(s, 1)], s) for s in range(1, half)]}
    here = {}
    for t, gate in ((1, (*blocks, foreign_sharp, *around)), (0, received[1])):
        here[t] = pl.pallas_call(
            functools.partial(_pick_kernel, [seg(0, t)]),
            out_shape=[block],
            compiler_params=_params(),
            cost_estimate=dear,
        )(_after(flat, *gate), meta, frames)[0]

    received[0] = [hop_member(segments[seg(s, 0)], s) for s in range(1, half)]

    def held_of(t, *gate):
        held = [here[t], hop_core(here[t])]
        for v in received[t]:
            v = _after(v, *gate)
            held += [v, hop_core(v)]
        return held

    held = {1: held_of(1, *around)}

    code = jnp.stack([x, y, k]).astype(jnp.int32)
    tail = -(-3 * per_core // 16) * 16

    def masses_in(rows):
        rows = rows[:, :share].astype(jnp.float32)
        return sum(rows[n * per_core : (n + 1) * per_core] for n in range(3))

    def over_chips(result, steps, earlier, extra):
        keep, mass, _, *sends = result
        mass = jnp.concatenate([*earlier, mass])[:, 0, :share]
        for s in range(1, chips):
            got = hop_chip(sends[s - 1], s)
            keep = keep + got[: steps * share].reshape(keep.shape).astype(jnp.float32)
            if extra:
                mass = mass + masses_in(got[steps * share :])
        return keep, mass

    results, totals, theirs, notes = [], [], [], []
    for t, begin, size in [(1, *part) for part in parts] + [(0, 0, per_core)]:
        if not t:
            held[0] = held_of(0, totals[0])
            notes.append(
                pl.pallas_call(
                    _copy_kernel,
                    out_shape=jax.ShapeDtypeStruct(notes[-1].shape, jnp.float32),
                    compiler_params=_params(),
                    cost_estimate=dear,
                )(_after(notes.pop(), totals[1]))
            )
        code_here = _after(code, notes[-1]) if results else code
        earlier = [r[1] for r in results] if t else []
        extra = 0 if t and begin + size < per_core else tail
        results.append(
            _cell_call(
                code_here, foreign_sharp if t else sharpness, foreign_pieces if t else [(centroids, 0)],
                not t, held[t], window, reach, per_core,
                begin, size, kids, share, chips - 1, earlier if extra else [], extra,
            )
        )
        if t:
            scores = results[-1][2]
            if totals:
                scores = _after(scores, totals[0])
            notes.append(
                pl.pallas_call(
                    _note_kernel,
                    out_shape=jax.ShapeDtypeStruct((size, sources * window), jnp.float32),
                    compiler_params=_params(),
                    cost_estimate=dear,
                )(scores)
            )
        if not t:
            arrived = [hop_chip(results[-1][3 + n], n + 1) for n in range(chips - 1)]
            break
        total, mass = over_chips(results[-1], size, earlier, extra)
        if t and extra:
            total = _after(total, notes[-1])
        total = total.astype(wire).reshape(size * share, width)
        if extra:
            high = _round(mass)
            middle = _round(mass - high)
            terms = jnp.concatenate([high, middle, mass - high - middle])
            behind = jnp.pad(terms.astype(wire), ((0, tail - terms.shape[0]), (0, width - share)))
            total = jnp.concatenate([total, behind])
        theirs.append(hop_partner(total))
        totals.append(total)
    score_parts = pl.pallas_call(
        functools.partial(_pack_kernel, sources, window),
        out_shape=[jax.ShapeDtypeStruct((2 * per_core, window), jnp.float32)] * sources,
        compiler_params=_params(),
        cost_estimate=dear,
    )(*notes, results[-1][2][:, 0])

    back = {}
    for s in range(half):
        for kk in range(cores):
            n = s * cores + kk
            back[s, kk] = score_parts[n] if n == 0 else hop_any(score_parts[n], -s, kk)
    values = []
    for s in range(half):
        for t in range(2):
            at_row = 0 if t else per_core
            for kk in range(cores):
                values.append(back[s, kk][at_row : at_row + per_core])
            values.append(jnp.zeros((meta_extra - cells_local, window), jnp.float32))
    frame_score = pl.pallas_call(
        functools.partial(_score_kernel, lines, window),
        out_shape=jax.ShapeDtypeStruct((1, rows), jnp.float32),
        compiler_params=_params(),
        cost_estimate=dear,
    )(rel, off, jnp.concatenate(values, axis=0)).reshape(rows)

    theirs = [_after(v, *arrived) for v in theirs]
    one_cell = lambda block, where: pl.BlockSpec(block, where)
    whole = lambda v: pl.BlockSpec(v.shape, lambda n, c: (0,) * v.ndim)
    behind = lambda steps: pl.BlockSpec((tail, 128), lambda n, c: (steps * share // tail, 0))
    keep, mass = results[-1][:2]

    def update(mine):
        def part(c):
            return lax.rem((c[2] if mine else 1 - c[2]) + c[1], 2)

        got, got_specs = [], []
        for v in arrived:
            got += [v, v]
            got_specs += [
                one_cell((piece, width), lambda n, c: (2 * n + part(c), 0)),
                behind(per_core),
            ]
        if mine:
            out_specs = [one_cell((1, piece, width), lambda n, c: (c[2] * per_core + n, 0, 0))]
            out_shape = [jax.ShapeDtypeStruct((cells_local, piece, width), jnp.float32)]
        else:
            out_specs = [
                one_cell((1, piece + 8, width), lambda n, c: (n, 0, 0)),
                pl.BlockSpec((8, 128), lambda n, c: (0, 0)),
            ]
            out_shape = [
                jax.ShapeDtypeStruct((per_core, piece + 8, width), jnp.float32),
                jax.ShapeDtypeStruct((8, 128), jnp.float32),
            ]
        return pl.pallas_call(
            functools.partial(_update_kernel, per_core, chips, piece, mine),
            grid_spec=pltpu.PrefetchScalarGridSpec(
                num_scalar_prefetch=1,
                grid=(per_core,),
                in_specs=[
                    one_cell((1, piece, width), lambda n, c: (n, part(c), 0)),
                    whole(mass),
                    *got_specs,
                    one_cell((piece, width), lambda n, c: (part(c), 0)),
                    one_cell((piece, width), lambda n, c: (2 * jnp.maximum(n - 1, 0) + part(c), 0)),
                    behind(per_core - 1),
                ],
                out_specs=out_specs,
                scratch_shapes=[pltpu.VMEM((128, 128), jnp.float32)],
            ),
            out_shape=out_shape,
            compiler_params=_params(),
            cost_estimate=busy,
        )(code, keep, mass, *got, theirs[0], theirs[1], theirs[1])

    swap, lines_mine = update(False)
    (out,) = update(True)
    swapped = hop_core(swap)
    new_centroids, child_mass = pl.pallas_call(
        functools.partial(_finish_kernel, per_core, piece),
        grid_spec=pltpu.PrefetchScalarGridSpec(
            num_scalar_prefetch=1,
            grid=(1,),
            in_specs=[
                anywhere,
                anywhere,
                pl.BlockSpec((per_core, 8, 128), lambda n, c: (0, piece // 8, 0)),
                pl.BlockSpec((8, 128), lambda n, c: (0, 0)),
            ],
            out_specs=[anywhere, pl.BlockSpec((cells_local, piece), lambda n, c: (0, 0))],
            scratch_shapes=[pltpu.SemaphoreType.DMA(())],
        ),
        out_shape=[
            jax.ShapeDtypeStruct(out.shape, jnp.float32),
            jax.ShapeDtypeStruct((cells_local, piece), jnp.float32),
        ],
        input_output_aliases={1: 0},
        compiler_params=_params(),
        cost_estimate=busy,
    )(code, out, swapped, swapped, lines_mine)
    return new_centroids, child_mass, frame_score


def solution(mesh):
    return jax.shard_map(
        on_device,
        mesh=mesh,
        in_specs=(
            P(("groups", "cell", "frame"), None),
            P(("groups", "cell", "frame"), None),
            P("cell", None, None),
            P("cell"),
        ),
        out_specs=(
            P(("groups", "cell"), "frame", None),
            P(("groups", "cell"), "frame"),
            P(("groups", "cell", "frame")),
        ),
        check_vma=False,
    )
```
